32 devices in a mesh: dp: 4 (over y, core), fsdp: 8 (over z, x).
Axes of the slice: x: 2, y: 2, z: 4, core: 2. Of those that a mesh axis runs over, the one named last changes fastest.
Arguments:
- x_source: bfloat16 [2, 16384, 1024], P(None, ('dp', 'fsdp')), may hold values from -8 to 8
- skip_source: bfloat16 [2, 16384, 1024], P(None, ('dp', 'fsdp')), may hold values from -8 to 8
- out_cotangent: bfloat16 [2, 8192, 1024], P(None, ('dp', 'fsdp')), may hold values from -6 to 6
- item_length: int32 [8, 2, 4, 4], P('fsdp'), may hold values from 1 to 128, as said below
- item_pack: int32 [8, 2, 4, 4], P('fsdp'), may hold values from 0 to 3, as said below
- item_offset: int32 [8, 2, 4, 4], P('fsdp'), may hold values from 0 to 255, as said below
- item_count: int32 [8, 2, 4, 4], P('fsdp'), may hold values from 1 to 128, as said below
- gains: float32 [2, 1024], P(None, 'fsdp'), may hold values from 0.3 to 2.4
- w_skip: float32 [2048, 1024], P('fsdp'), may hold values from -0.125 to 0.125
- w_qkv: float32 [1024, 3072], P('fsdp'), may hold values from -0.1875 to 0.1875
- w_out: float32 [1024, 1024], P('fsdp'), may hold values from -0.75 to 0.75
- w_up: float32 [1024, 4096], P('fsdp'), may hold values from -0.1875 to 0.1875
- w_down: float32 [4096, 1024], P('fsdp'), may hold values from -0.09375 to 0.09375
- gains_first: float32 [2, 1024], P(None, 'fsdp'), may hold values from -0.12 to 0.12
- first_skip: float32 [2048, 1024], P('fsdp'), may hold values from -0.12 to 0.12
- first_qkv: float32 [1024, 3072], P('fsdp'), may hold values from -0.12 to 0.12
- first_out: float32 [1024, 1024], P('fsdp'), may hold values from -0.12 to 0.12
- first_up: float32 [1024, 4096], P('fsdp'), may hold values from -0.12 to 0.12
- first_down: float32 [4096, 1024], P('fsdp'), may hold values from -0.12 to 0.12
- gains_second: float32 [2, 1024], P(None, 'fsdp'), may hold values from 0.0004 to 0.0016
- second_skip: float32 [2048, 1024], P('fsdp'), may hold values from 0.0004 to 0.0016
- second_qkv: float32 [1024, 3072], P('fsdp'), may hold values from 0.0004 to 0.0016
- second_out: float32 [1024, 1024], P('fsdp'), may hold values from 3e-05 to 0.00012
- second_up: float32 [1024, 4096], P('fsdp'), may hold values from 3e-05 to 0.00012
- second_down: float32 [4096, 1024], P('fsdp'), may hold values from 0.0004 to 0.0016
Outputs:
- out_frames: bfloat16 [2, 8192, 1024], P(None, ('dp', 'fsdp'))
- input_gradient: bfloat16 [2, 16384, 1024], P(None, ('dp', 'fsdp'))
- skip_gradient: bfloat16 [2, 16384, 1024], P(None, ('dp', 'fsdp'))
- gradient_norm: float32 [1], replicated
- gains_new: float32 [2, 1024], P(None, 'fsdp')
- gains_first_new: float32 [2, 1024], P(None, 'fsdp')
- gains_second_new: float32 [2, 1024], P(None, 'fsdp')
- skip_new: float32 [2048, 1024], P('fsdp')
- skip_first_new: float32 [2048, 1024], P('fsdp')
- skip_second_new: float32 [2048, 1024], P('fsdp')
- skip_copy: bfloat16 [2048, 1024], P('fsdp')
- qkv_new: float32 [1024, 3072], P('fsdp')
- qkv_first_new: float32 [1024, 3072], P('fsdp')
- qkv_second_new: float32 [1024, 3072], P('fsdp')
- qkv_copy: bfloat16 [1024, 3072], P('fsdp')
- out_new: float32 [1024, 1024], P('fsdp')
- out_first_new: float32 [1024, 1024], P('fsdp')
- out_second_new: float32 [1024, 1024], P('fsdp')
- out_copy: bfloat16 [1024, 1024], P('fsdp')
- up_new: float32 [1024, 4096], P('fsdp')
- up_first_new: float32 [1024, 4096], P('fsdp')
- up_second_new: float32 [1024, 4096], P('fsdp')
- up_copy: bfloat16 [1024, 4096], P('fsdp')
- down_new: float32 [4096, 1024], P('fsdp')
- down_first_new: float32 [4096, 1024], P('fsdp')
- down_second_new: float32 [4096, 1024], P('fsdp')
- down_copy: bfloat16 [4096, 1024], P('fsdp')
The draws below stay inside these ranges and needn't reach their ends.
Inputs may be any that keep to these rules, and one draw needn't show every extreme that they name: `item_length`: each source shard holds its utterances in slot order from its first row; in every group and micro-batch one source shard holds exactly 512 frames, every pack receives exactly 256 frames, and the longest utterance has exactly 128 frames. `item_pack`: each source shard sends exactly one utterance to each pack of its group. `item_offset`: the utterances of a pack tile its 256 rows without gaps. `item_count`: at most the utterance's length; in group 0 and micro-batch 0 every utterance of 128 frames has all 128 frames counted.
All inputs are finite; a program needn't handle non-finite values.
Results may differ from the reference program's by a relative error of at most 0.025.
Values may be sent and summed in bfloat16 or wider, within the bound.
A program may use at most 320 MiB of HBM per device.

```python
import math
import jax
import jax.numpy as jnp
from jax import lax

D = 1024
HEADS = 16
HD = 64
FF = 4096
ROWS = 256
MB = 2
STEP = 5
SRC = 512
FRAMES = 8192
SRC_ALL = 16384
N_DP = 4
N_FSDP = 8


def plan_group(key):
    dp_count = N_DP
    capacity = 2 * ROWS // N_DP
    remainder = ROWS - capacity
    base_share = remainder // (dp_count - 1)
    extra_rows = remainder - base_share * (dp_count - 1)
    key_heavy, key_jitter, key_slots, key_order = jax.random.split(key, 4)
    heavy = jax.random.randint(key_heavy, (), 0, dp_count)
    jitter = jax.random.randint(key_jitter, (dp_count, dp_count - 1), 0, base_share)
    shares = base_share + jitter - jnp.roll(jitter, -1, axis=1) + (jnp.arange(dp_count - 1) < extra_rows).astype(jnp.int32)
    others = (heavy + 1 + jnp.arange(dp_count - 1)) % dp_count
    placed = (others[:, None] == jnp.arange(dp_count)[None, :]).astype(jnp.int32)
    cell_rows = jnp.sum(shares[:, :, None] * placed[None], axis=1) + capacity * (jnp.arange(dp_count) == heavy).astype(jnp.int32)[None, :]
    slot_packs = jax.vmap(lambda sub_key: jax.random.permutation(sub_key, dp_count))(jax.random.split(key_slots, dp_count))
    pack_order = jax.vmap(lambda sub_key: jax.random.permutation(sub_key, dp_count))(jax.random.split(key_order, dp_count))
    pack_rank = jnp.argsort(pack_order, axis=1)
    earlier = (pack_rank[:, None, :] < pack_rank[:, :, None]).astype(jnp.int32)
    cell_offsets = jnp.sum(earlier * cell_rows[:, None, :], axis=2)
    sources = jnp.arange(dp_count)[:, None]
    lengths = cell_rows[slot_packs, sources].astype(jnp.int32)
    offsets = cell_offsets[slot_packs, sources].astype(jnp.int32)
    return (lengths, slot_packs.astype(jnp.int32), offsets)


def plan_all_drawn(key):
    keys_all = jax.random.split(key, N_FSDP * MB)
    lengths, packs, offsets = jax.vmap(plan_group)(keys_all)
    new_shape = (N_FSDP, MB, N_DP, N_DP)
    return (lengths.reshape(new_shape), packs.reshape(new_shape), offsets.reshape(new_shape))


def draw_item_length(key, part):
    return plan_all_drawn(key)[0]


def draw_item_pack(key, part):
    return plan_all_drawn(key)[1]


def draw_item_offset(key, part):
    return plan_all_drawn(key)[2]


def draw_item_count(key, part):
    lengths = plan_all_drawn(key)[0]
    key = jax.random.fold_in(key, 7)
    counts = jax.random.randint(key, lengths.shape, 1, lengths + 1).astype(jnp.int32)
    capacity = 2 * ROWS // N_DP
    first_group = (jnp.arange(N_FSDP)[:, None, None, None] == 0) & (jnp.arange(MB)[None, :, None, None] == 0)
    full = first_group & (lengths == capacity)
    return jnp.where(full, lengths, counts).astype(jnp.int32)


def column_ramp(start_value, end_value):
    fraction = jnp.arange(D, dtype=jnp.float32) / (D - 1)
    return start_value + (end_value - start_value) * fraction


def frame_draw(key, ramp_low, ramp_high):
    frame_shape = (MB, SRC_ALL, D)
    noise = jax.random.truncated_normal(key, -4.0, 4.0, frame_shape, jnp.float32)
    return noise * column_ramp(ramp_low, ramp_high)


def draw_x_source(key, part):
    key = jax.random.fold_in(key, 11)
    values = frame_draw(key, 0.6, 1.2)
    return values.astype(jnp.bfloat16)


def draw_skip_source(key, part):
    key = jax.random.fold_in(key, 13)
    values = frame_draw(key, 1.2, 1.8)
    return values.astype(jnp.bfloat16)


def draw_gains(key, part):
    key = jax.random.fold_in(key, 17)
    factor = jax.random.uniform(key, (2, D), jnp.float32, 0.85, 1.15)
    return factor * column_ramp(0.6, 1.8)[None, :]


def block_scale(key, extent, shards, low, high):
    def one(dim, blocks):
        heights = jax.random.uniform(jax.random.fold_in(jax.random.fold_in(key, 6), dim), (blocks,), jnp.float32, low / len(shards), high / len(shards))
        return jnp.repeat(jnp.exp(heights), extent[dim] // blocks).reshape((-1,) + (1,) * (len(extent) - dim - 1))

    loudness = one(*shards[0])
    for cut in shards[1:]:
        loudness = loudness * one(*cut)
    return loudness


def bell_draw(rng, shape, scale, most, cuts=(), kind=jnp.bfloat16):
    entries = scale * jax.random.normal(rng, shape, jnp.float32)
    if cuts:
        entries = entries * block_scale(rng, shape, cuts, -0.22, 0.18)
    return jnp.clip(entries, -most, most).astype(kind)


def setup_inputs(seed: int = 0) -> dict:
    seeds = jax.random.split(jax.random.key(seed), 26)
    x_source = draw_x_source(jax.random.fold_in(seeds[25], 71), 0)
    skip_source = draw_skip_source(jax.random.fold_in(seeds[25], 71), 0)
    out_cotangent = bell_draw(seeds[2], (MB, FRAMES, D), 1.0, 6.0, ((1, 32),))
    item_length = draw_item_length(jax.random.fold_in(seeds[25], 71), 0)
    item_pack = draw_item_pack(jax.random.fold_in(seeds[25], 71), 0)
    item_offset = draw_item_offset(jax.random.fold_in(seeds[25], 71), 0)
    item_count = draw_item_count(jax.random.fold_in(seeds[25], 71), 0)
    gains = draw_gains(jax.random.fold_in(seeds[25], 71), 0)
    w_skip = bell_draw(seeds[8], (2 * D, D), (2 * D) ** -0.5, 0.125, ((0, 8),), jnp.float32)
    w_qkv = bell_draw(seeds[9], (D, 3 * D), D ** -0.5, 0.1875, ((0, 8),), jnp.float32)
    w_out = bell_draw(seeds[10], (D, D), (D // 16) ** -0.5, 0.75, ((0, 8),), jnp.float32)
    w_up = bell_draw(seeds[11], (D, FF), D ** -0.5, 0.1875, ((0, 8),), jnp.float32)
    w_down = bell_draw(seeds[12], (FF, D), FF ** -0.5, 0.09375, ((0, 8),), jnp.float32)
    gains_first = bell_draw(seeds[13], (2, D), 0.02, 0.12, ((1, 8),), jnp.float32)
    first_skip = bell_draw(seeds[14], (2 * D, D), 0.02, 0.12, ((0, 8),), jnp.float32)
    first_qkv = bell_draw(seeds[15], (D, 3 * D), 0.02, 0.12, ((0, 8),), jnp.float32)
    first_out = bell_draw(seeds[16], (D, D), 0.02, 0.12, ((0, 8),), jnp.float32)
    first_up = bell_draw(seeds[17], (D, FF), 0.02, 0.12, ((0, 8),), jnp.float32)
    first_down = bell_draw(seeds[18], (FF, D), 0.02, 0.12, ((0, 8),), jnp.float32)
    gains_second = jnp.clip(jnp.exp(math.log(0.0016) - 1.3862944 * jax.random.uniform(seeds[19], (2, D), jnp.float32) ** block_scale(seeds[19], (2, D), ((1, 8),), -0.2, 0.2)), 0.0004, 0.0016)
    second_skip = jnp.clip(jnp.exp(math.log(0.0016) - 1.3862944 * jax.random.uniform(seeds[20], (2 * D, D), jnp.float32) ** block_scale(seeds[20], (2 * D, D), ((0, 8),), -0.2, 0.2)), 0.0004, 0.0016)
    second_qkv = jnp.clip(jnp.exp(math.log(0.0016) - 1.3862944 * jax.random.uniform(seeds[21], (D, 3 * D), jnp.float32) ** block_scale(seeds[21], (D, 3 * D), ((0, 8),), -0.2, 0.2)), 0.0004, 0.0016)
    second_out = jnp.clip(jnp.exp(math.log(0.00012) - 1.3862944 * jax.random.uniform(seeds[22], (D, D), jnp.float32) ** block_scale(seeds[22], (D, D), ((0, 8),), -0.2, 0.2)), 2.9999999242136255e-05, 0.00012)
    second_up = jnp.clip(jnp.exp(math.log(0.00012) - 1.3862944 * jax.random.uniform(seeds[23], (D, FF), jnp.float32) ** block_scale(seeds[23], (D, FF), ((0, 8),), -0.2, 0.2)), 2.9999999242136255e-05, 0.00012)
    second_down = jnp.clip(jnp.exp(math.log(0.0016) - 1.3862944 * jax.random.uniform(seeds[24], (FF, D), jnp.float32) ** block_scale(seeds[24], (FF, D), ((0, 8),), -0.2, 0.2)), 0.0004, 0.0016)
    return dict(x_source=x_source, skip_source=skip_source, out_cotangent=out_cotangent, item_length=item_length, item_pack=item_pack, item_offset=item_offset, item_count=item_count, gains=gains, w_skip=w_skip, w_qkv=w_qkv, w_out=w_out, w_up=w_up, w_down=w_down, gains_first=gains_first, first_skip=first_skip, first_qkv=first_qkv, first_out=first_out, first_up=first_up, first_down=first_down, gains_second=gains_second, second_skip=second_skip, second_qkv=second_qkv, second_out=second_out, second_up=second_up, second_down=second_down)


@jax.custom_vjp
def low(v):
    return lax.optimization_barrier(v.astype(jnp.bfloat16)).astype(jnp.float32)

@jax.custom_vjp
def low_back(v):
    return v

def low_keep(v):
    return (low(v), None)

def low_pass(kept, grad):
    return (grad,)

def back_keep(v):
    return (v, None)

def back_low(kept, grad):
    return (low(grad),)
low.defvjp(low_keep, low_pass)
low_back.defvjp(back_keep, back_low)
HIGH = lax.Precision.HIGHEST
BETA_FIRST = 0.5
BETA_SECOND = 0.5
ADAM_EPSILON = 1e-08
WEIGHT_DECAY = 0.01

def norm_rows(hidden, gain_row):
    centre = hidden - lax.optimization_barrier(jnp.mean(hidden, axis=-1, keepdims=True))
    spread = lax.optimization_barrier(jnp.mean(centre * centre, axis=-1, keepdims=True))
    return centre * lax.rsqrt(spread + 1e-05) * gain_row

def alibi_bias(length):
    position = jnp.arange(length, dtype=jnp.float32)
    distance = jnp.abs(position[:, None] - position[None, :])
    slopes = jnp.exp2(-8.0 * (jnp.arange(HEADS, dtype=jnp.float32) + 1.0) / HEADS)
    return -slopes[:, None, None] * distance[None]

def matmul(left, right):
    return jnp.dot(left, right, precision=HIGH)

def layer(params, inputs, source):
    used_skip, used_qkv, used_out, used_up, used_down, used_gains = [low(item) for item in params]
    inputs = low_back(inputs)
    row_count = inputs.shape[0]
    pack_count = row_count // ROWS
    base_rows = low_back(matmul(inputs, used_skip))
    normed_one = low(norm_rows(base_rows, used_gains[0]))
    qkv_rows = low(low_back(matmul(normed_one, used_qkv)))
    heads_shape = (pack_count, ROWS, HEADS, HD)
    queries = qkv_rows[:, :D].reshape(heads_shape)
    keys_all = qkv_rows[:, D:2 * D].reshape(heads_shape)
    values_all = qkv_rows[:, 2 * D:].reshape(heads_shape)
    scores = jnp.einsum('nqhe,nkhe->nhqk', queries, keys_all, precision=HIGH) * HD ** (-0.5) + alibi_bias(ROWS)[None]
    scores = low_back(scores)
    same_item = source[:, :, None] == source[:, None, :]
    scores = jnp.where(same_item[:, None], scores, -1e+30)
    probs_low = low(jax.nn.softmax(scores, axis=-1))
    mixed_heads = jnp.einsum('nhqk,nkhe->nqhe', probs_low, values_all, precision=HIGH).reshape(row_count, D)
    mixed_heads = low(low_back(mixed_heads))
    after_attn = base_rows + low_back(matmul(mixed_heads, used_out))
    normed_two = low(norm_rows(after_attn, used_gains[1]))
    up_rows = low_back(matmul(normed_two, used_up))
    activated = low(jax.nn.gelu(up_rows, approximate=True))
    return after_attn + low_back(matmul(activated, used_down))

def plan_all(lengths, packs, offsets, counts):
    starts = jnp.cumsum(lengths, axis=1) - lengths
    destinations = jnp.arange(N_DP, dtype=jnp.int32)
    matches = packs[None] == destinations[:, None, None]

    def chosen(values):
        return lax.optimization_barrier(jnp.sum(jnp.where(matches, values[None], 0), axis=2))
    length_in, offset_in, start_in, count_in = (chosen(lengths), chosen(offsets), chosen(starts), chosen(counts))
    position = jnp.arange(ROWS, dtype=jnp.int32)
    inside = (position[None, :, None] >= offset_in[:, None, :]) & (position[None, :, None] < (offset_in + length_in)[:, None, :])

    def select(values):
        return lax.optimization_barrier(jnp.sum(jnp.where(inside, values[:, None, :], 0), axis=2))
    source = lax.optimization_barrier(jnp.sum(jnp.where(inside, destinations[None, None, :], 0), axis=2))
    row_in_source = select(start_in) + position[None, :] - select(offset_in)
    weight = select(count_in).astype(jnp.float32) / select(length_in).astype(jnp.float32)
    return (source, row_in_source, weight)

def adam_update(master, first, second, gradient, rate, decay):
    first_new = BETA_FIRST * first + (1.0 - BETA_FIRST) * gradient
    second_new = BETA_SECOND * second + (1.0 - BETA_SECOND) * gradient * gradient
    first_hat = first_new / (1.0 - BETA_FIRST ** STEP)
    second_hat = second_new / (1.0 - BETA_SECOND ** STEP)
    master_new = master - rate * (first_hat / (jnp.sqrt(second_hat) + ADAM_EPSILON) + decay * master)
    return (master_new, first_new, second_new)

def reference(x_source, skip_source, out_cotangent, item_length, item_pack, item_offset, item_count, gains, w_skip, w_qkv, w_out, w_up, w_down, gains_first, first_skip, first_qkv, first_out, first_up, first_down, gains_second, second_skip, second_qkv, second_out, second_up, second_down):
    source, row_in_source, weight = jax.vmap(jax.vmap(plan_all))(item_length, item_pack, item_offset, item_count)
    group_index = jnp.arange(N_FSDP, dtype=jnp.int32)[:, None, None, None]
    global_row = (source * N_FSDP + group_index) * SRC + row_in_source
    x_flat = x_source.reshape(MB * SRC_ALL, D)
    skip_flat = skip_source.reshape(MB * SRC_ALL, D)
    cot_blocks = out_cotangent.reshape(MB, N_DP, N_FSDP, ROWS, D)
    params = (w_skip, w_qkv, w_out, w_up, w_down, gains)

    def step(totals, counter):
        group_now = counter // MB
        batch_now = counter % MB
        picked = global_row[group_now, batch_now].reshape(-1) + batch_now * SRC_ALL
        inputs = jnp.concatenate([x_flat[picked], skip_flat[picked]], axis=1).astype(jnp.float32)
        segment = source[group_now, batch_now]
        target = cot_blocks[batch_now, :, group_now].reshape(N_DP * ROWS, D).astype(jnp.float32)
        scaling = weight[group_now, batch_now].reshape(-1, 1)
        outputs, back = jax.vjp(lambda values, rows_in: layer(values, rows_in, segment), params, inputs)
        gradients, d_inputs = back(scaling * target)
        totals = jax.tree.map(jnp.add, totals, gradients)
        return (totals, (outputs.astype(jnp.bfloat16), d_inputs.astype(jnp.bfloat16), picked))
    start_totals = jax.tree.map(jnp.zeros_like, params)
    totals, stacked = lax.scan(step, start_totals, jnp.arange(N_FSDP * MB, dtype=jnp.int32))
    outputs, d_inputs, picked_all = stacked
    out_frames = outputs.reshape(N_FSDP, MB, N_DP, ROWS, D).transpose(1, 2, 0, 3, 4).reshape(MB, FRAMES, D)
    d_all = jnp.zeros((MB * SRC_ALL, 2 * D), jnp.bfloat16).at[picked_all.reshape(-1)].set(d_inputs.reshape(-1, 2 * D))
    input_gradient = d_all[:, :D].reshape(MB, SRC_ALL, D)
    skip_gradient = d_all[:, D:].reshape(MB, SRC_ALL, D)
    squares = jnp.float32(0.0)
    for gradient in totals:
        squares = squares + jnp.sum(gradient * gradient)
    gradient_norm = jnp.sqrt(squares)
    param_count = 6 * D * D + 2 * D * FF + 2 * D
    clip = jnp.minimum(1.0, 0.02 * math.sqrt(param_count) / gradient_norm)
    grad_skip, grad_qkv, grad_out, grad_up, grad_down, grad_gains = [clip * gradient for gradient in totals]
    gains_new, gains_first_new, gains_second_new = adam_update(gains, gains_first, gains_second, grad_gains, 0.3, 0.0)
    skip_new, skip_first_new, skip_second_new = adam_update(w_skip, first_skip, second_skip, grad_skip, 0.5 / math.sqrt(2 * D), WEIGHT_DECAY)
    qkv_new, qkv_first_new, qkv_second_new = adam_update(w_qkv, first_qkv, second_qkv, grad_qkv, 0.5 / math.sqrt(D), WEIGHT_DECAY)
    out_new, out_first_new, out_second_new = adam_update(w_out, first_out, second_out, grad_out, 0.5 / math.sqrt(D // 16), WEIGHT_DECAY)
    up_new, up_first_new, up_second_new = adam_update(w_up, first_up, second_up, grad_up, 0.5 / math.sqrt(D), WEIGHT_DECAY)
    down_new, down_first_new, down_second_new = adam_update(w_down, first_down, second_down, grad_down, 0.5 / math.sqrt(FF), WEIGHT_DECAY)
    return (out_frames, input_gradient, skip_gradient, gradient_norm.reshape(1), gains_new, gains_first_new, gains_second_new, skip_new, skip_first_new, skip_second_new, skip_new.astype(jnp.bfloat16), qkv_new, qkv_first_new, qkv_second_new, qkv_new.astype(jnp.bfloat16), out_new, out_first_new, out_second_new, out_new.astype(jnp.bfloat16), up_new, up_first_new, up_second_new, up_new.astype(jnp.bfloat16), down_new, down_first_new, down_second_new, down_new.astype(jnp.bfloat16))
```

```python
from functools import partial
import math

import jax
import jax.numpy as jnp
from jax import lax
from jax.experimental import pallas as pl
from jax.experimental.pallas import tpu as pltpu
from jax.sharding import PartitionSpec as P

D = 1024
HEADS = 16
HD = 64
FF = 4096
STEP = 5
CORES = 2
OUTER = 4

BETA_FIRST = 0.5
BETA_SECOND = 0.5
ADAM_EPSILON = 1e-08
WEIGHT_DECAY = 0.01
NORM_EPSILON = 1e-05

BF16 = jnp.bfloat16
F32 = jnp.float32
MESH = pl.DeviceIdType.MESH

GATHER_UNITS = ((0, 0, 1, False), (1, 0, 1, True), (2, 0, 1, False), (3, 0, 1, True), (4, 0, 2, False), (4, 1, 2, False))


def sizes():
    n_dp, n_fsdp = lax.axis_size("dp"), lax.axis_size("fsdp")
    return n_dp // CORES, CORES, OUTER, n_fsdp // OUTER


def place():
    rows, cores, outer, inner = sizes()
    dp, fsdp = lax.axis_index("dp"), lax.axis_index("fsdp")
    return dp // cores, lax.rem(dp, cores), fsdp // inner, lax.rem(fsdp, inner)


def gather_kernel(dims, *refs):
    n_y, n_c, n_a, n_b = dims
    count = 5
    shards, payload, gains = refs[:count], refs[count], refs[count + 1]
    outs = refs[count + 2 : 2 * count + 4]
    fulls, arrived, gains_full = outs[:count], outs[count], outs[count + 1]
    send_sem, recv_sem, local_sem = refs[2 * count + 4 :]
    dp, fsdp = lax.axis_index("dp"), lax.axis_index("fsdp")
    y, c, a, b = dp // n_c, lax.rem(dp, n_c), fsdp // n_b, lax.rem(fsdp, n_b)
    n_dp, n_fsdp = n_y * n_c, n_a * n_b
    used = [0, 0]
    sent = []

    def remote(src, dst, landing, device):
        index = used[0]
        used[0] += 1
        copy = pltpu.make_async_remote_copy(
            src_ref=src, dst_ref=dst, send_sem=send_sem.at[index], recv_sem=recv_sem.at[index],
            device_id=device, device_id_type=MESH,
        )
        copy.start()
        sent.append(copy)
        return pltpu.make_async_remote_copy(
            src_ref=src, dst_ref=landing, send_sem=send_sem.at[index], recv_sem=recv_sem.at[index],
            device_id=device, device_id_type=MESH,
        )

    def local(src, dst):
        index = used[1]
        used[1] += 1
        copy = pltpu.make_async_copy(src, dst, local_sem.at[index])
        copy.start()
        return copy

    def turn(value, step, size):
        return lax.rem(value + (step + size) % size, size)

    frames = []
    for k in range(1, n_dp):
        to, back = turn(dp, k, n_dp), turn(dp, -k, n_dp)
        frames.append(remote(payload.at[:, to], arrived.at[:, dp], arrived.at[:, back], (to, fsdp)))
    own_frames = local(payload.at[:, dp], arrived.at[:, dp])
    gain_copies = []
    for k in range(1, n_fsdp):
        to, back = turn(fsdp, k, n_fsdp), turn(fsdp, -k, n_fsdp)
        gain_copies.append(remote(gains, gains_full.at[fsdp], gains_full.at[back], (dp, to)))
    own_gains = local(gains, gains_full.at[fsdp])

    units = []
    for matrix, part, parts, shared in GATHER_UNITS:
        width = shards[matrix].shape[1] // parts
        units.append((matrix, part * width, width, shared))
    state = [{} for _ in units]

    def columns(unit, of_y):
        matrix, first, width, shared = unit
        if shared:
            step = width // (n_c * n_y)
            return pl.ds(pl.multiple_of(first + (c * n_y + of_y) * step, 128), step)
        step = width // n_c
        return pl.ds(pl.multiple_of(first + c * step, 128), step)

    def stage_outer(index):
        matrix, first, width, shared = units[index]
        cols, full, shard = columns(units[index], y), fulls[matrix], shards[matrix]
        state[index]["outer"] = [
            remote(
                shard.at[:, cols], full.at[a, b, :, cols], full.at[turn(a, -k, n_a), b, :, cols],
                (dp, turn(a, k, n_a) * n_b + b),
            )
            for k in range(1, n_a)
        ]
        whole = pl.ds(first, width)
        state[index]["own"] = local(shard.at[:, whole], full.at[a, b, :, whole])

    def spread(index, block, of_y, kinds):
        matrix, first, width, shared = units[index]
        full, cols = fulls[matrix], columns(units[index], of_y)
        view = full.at[block[0], block[1], :, cols]
        if "y" in kinds and shared:
            for k in range(1, n_y):
                source = turn(y, -k, n_y)
                landing = full.at[block[0], block[1], :, columns(units[index], source)]
                copy = remote(view, view, landing, (turn(y, k, n_y) * n_c + c, fsdp))
                state[index].setdefault("y", []).append((copy, block, source))
        if "c" in kinds:
            step = width // (n_c * n_y) if shared else width // n_c
            other = (
                first + ((1 - c) * n_y + of_y) * step if shared else first + (1 - c) * step
            )
            landing = full.at[block[0], block[1], :, pl.ds(pl.multiple_of(other, 128), step)]
            copy = remote(view, view, landing, (y * n_c + 1 - c, fsdp))
            state[index].setdefault("c", []).append(copy)

    def stage_inner(index):
        matrix, first, width, shared = units[index]
        cols, full = columns(units[index], y), fulls[matrix]
        state[index]["own"].wait()
        for copy in state[index]["outer"]:
            copy.wait_recv()
        state[index]["inner"] = [
            remote(
                full.at[:, b, :, cols], full.at[:, b, :, cols], full.at[:, turn(b, -k, n_b), :, cols],
                (dp, a * n_b + turn(b, k, n_b)),
            )
            for k in range(1, n_b)
        ]
        for k in range(1, n_a):
            spread(index, (turn(a, -k, n_a), b), y, "yc")

    def stage_y(index):
        for k, copy in zip(range(1, n_b), state[index]["inner"]):
            copy.wait_recv()
            spread(index, (slice(None), turn(b, -k, n_b)), y, "yc")

    def stage_c(index):
        for copy, block, source in state[index].get("y", []):
            copy.wait_recv()
            spread(index, block, source, "c")

    count_units = len(units)
    for step in range(count_units + 3):
        if step < count_units:
            stage_outer(step)
        if 0 <= step - 1 < count_units:
            stage_inner(step - 1)
        if 0 <= step - 2 < count_units:
            stage_y(step - 2)
        if 0 <= step - 3 < count_units:
            stage_c(step - 3)
    for copy in frames + gain_copies:
        copy.wait_recv()
    for index in range(count_units):
        for copy in state[index].get("c", []):
            copy.wait_recv()
    for copy in sent:
        copy.wait_send()
    own_frames.wait()
    own_gains.wait()


def gather_all(shards, payload, gains):
    dims = sizes()
    n_y, n_c, n_a, n_b = dims
    total = n_y * n_c - 1 + n_a * n_b - 1
    for _, _, _, shared in GATHER_UNITS:
        groups = n_a - 1 + n_b - 1
        total += groups + ((n_y - 1) * groups + n_y * groups if shared else groups)
    anywhere = pl.BlockSpec(memory_space=pl.ANY)
    out_shape = [
        jax.ShapeDtypeStruct((n_a, n_b) + shard.shape, shard.dtype) for shard in shards
    ] + [
        jax.ShapeDtypeStruct(payload.shape, payload.dtype),
        jax.ShapeDtypeStruct((n_a * n_b,) + gains.shape, gains.dtype),
    ]
    results = pl.pallas_call(
        partial(gather_kernel, dims),
        out_shape=out_shape,
        in_specs=[anywhere] * (len(shards) + 2),
        out_specs=[anywhere] * len(out_shape),
        scratch_shapes=[
            pltpu.SemaphoreType.DMA((total,)),
            pltpu.SemaphoreType.DMA((total,)),
            pltpu.SemaphoreType.DMA((len(GATHER_UNITS) + 2,)),
        ],
        compiler_params=pltpu.CompilerParams(has_side_effects=True),
        name="gather_weights",
    )(*shards, payload, gains)
    fulls = [
        full.reshape(n_a * n_b * shard.shape[0], shard.shape[1])
        for full, shard in zip(results, shards)
    ]
    return fulls, results[-2], results[-1]


def move(value, axis, shift):
    n_y, n_c, n_a, n_b = sizes()
    dims = {"y": n_y, "c": n_c, "a": n_a, "b": n_b}
    pairs = []
    for source in range(n_y * n_c * n_a * n_b):
        at = {
            "y": source // (n_c * n_a * n_b),
            "c": source // (n_a * n_b) % n_c,
            "a": source // n_b % n_a,
            "b": source % n_b,
        }
        at[axis] = (at[axis] + shift) % dims[axis]
        target = ((at["y"] * n_c + at["c"]) * n_a + at["a"]) * n_b + at["b"]
        pairs.append((source, target))
    return lax.ppermute(value, ("dp", "fsdp"), pairs)


def swap(value, axis, mask):
    n_y, n_c, n_a, n_b = sizes()
    pairs = []
    for source in range(n_y * n_c * n_a * n_b):
        at = {
            "y": source // (n_c * n_a * n_b),
            "c": source // (n_a * n_b) % n_c,
            "a": source // n_b % n_a,
            "b": source % n_b,
        }
        at[axis] = at[axis] ^ mask
        target = ((at["y"] * n_c + at["c"]) * n_a + at["a"]) * n_b + at["b"]
        pairs.append((source, target))
    return lax.ppermute(value, ("dp", "fsdp"), pairs)


def pick(value, index, axis):
    return lax.dynamic_index_in_dim(value, index, axis, keepdims=False)


def add_all(values):
    total = values[0].astype(F32)
    for value in values[1:]:
        total = total + value.astype(F32)
    return total.astype(BF16)


def both_cores(value):
    return jnp.concatenate([value, move(value, "c", 1)], axis=0)


def weight_gradient(left, right, shared):
    n_y, n_c, n_a, n_b = sizes()
    y, c, a, b = place()
    width = right.shape[1] // n_c
    halves = right.reshape(right.shape[0], n_c, width)
    mine, other = pick(halves, c, 1), pick(halves, 1 - c, 1)
    left_all = both_cores(left)
    right_all = jnp.concatenate([mine, move(other, "c", 1)], axis=0)
    partial_sum = lax.dot_general(
        left_all, right_all, (((0,), (0,)), ((), ())), preferred_element_type=F32
    ).astype(BF16)
    rows = left.shape[1] // (n_a * n_b)
    blocks = partial_sum.reshape(n_a, n_b, rows, width)
    if shared:
        step = width // n_y
        pieces = blocks.reshape(n_a, n_b, rows, n_y, step)
        got = [
            move(pick(pieces, (y + k) % n_y, 3), "y", k) for k in range(1, n_y)
        ]
        blocks = add_all([pick(pieces, y, 3)] + got)
    got = [move(pick(blocks, (b + k) % n_b, 1), "b", k) for k in range(1, n_b)]
    blocks = add_all([pick(blocks, b, 1)] + got)
    got = [move(pick(blocks, (a + k) % n_a, 0), "a", k) for k in range(1, n_a)]
    own = add_all([pick(blocks, a, 0)] + got)
    if shared:
        full = jnp.zeros((n_y, rows, step), BF16)
        full = lax.dynamic_update_index_in_dim(full, own, y, 0)
        for k in range(1, n_y):
            full = lax.dynamic_update_index_in_dim(full, move(own, "y", k), (y - k) % n_y, 0)
        own = jnp.moveaxis(full, 0, 1).reshape(rows, width)
    else:
        mask = 1
        while mask < n_y:
            own = add_all([own, swap(own, "y", mask)])
            mask *= 2
    other = move(own, "c", 1)
    return jnp.where(
        c == 0, jnp.concatenate([own, other], axis=1), jnp.concatenate([other, own], axis=1)
    ).astype(F32)


def sum_over(value, axis, count):
    mask = 1
    while mask < count:
        value = value + swap(value, axis, mask)
        mask *= 2
    return value


def dot_rows(left, right):
    return jnp.dot(left, right, preferred_element_type=F32)


def dot_right(left, right):
    return lax.dot_general(left, right, (((1,), (1,)), ((), ())), preferred_element_type=F32)


def norm_parts(hidden):
    centre = hidden - jnp.mean(hidden, axis=-1, keepdims=True)
    spread = jnp.mean(centre * centre, axis=-1, keepdims=True)
    scale = lax.rsqrt(spread + NORM_EPSILON)
    return centre * scale, scale


def norm_back(normal, scale, gain_row, gradient):
    scaled = gradient * gain_row
    grad_gain = jnp.sum(gradient * normal, axis=0)
    back = scale * (
        scaled
        - jnp.mean(scaled, axis=-1, keepdims=True)
        - normal * jnp.mean(scaled * normal, axis=-1, keepdims=True)
    )
    return back, grad_gain


def alibi_bias(length):
    position = jnp.arange(length, dtype=F32)
    distance = jnp.abs(position[:, None] - position[None, :])
    slopes = jnp.exp2(-8.0 * (jnp.arange(HEADS, dtype=F32) + 1.0) / HEADS)
    return -slopes[:, None, None] * distance[None]


def attention_scores(queries, keys_all, alibi_terms, same_item):
    scores = (
        jnp.einsum("nqhe,nkhe->nhqk", queries, keys_all, preferred_element_type=F32) * HD ** (-0.5)
        + alibi_terms[None]
    )
    return jnp.where(same_item[:, None], scores, -1e30)


def adam_update(master, first, second, gradient, rate, decay):
    first_new = BETA_FIRST * first + (1.0 - BETA_FIRST) * gradient
    second_new = BETA_SECOND * second + (1.0 - BETA_SECOND) * gradient * gradient
    first_hat = first_new / (1.0 - BETA_FIRST**STEP)
    second_hat = second_new / (1.0 - BETA_SECOND**STEP)
    master_new = master - rate * (
        first_hat / (jnp.sqrt(second_hat) + ADAM_EPSILON) + decay * master
    )
    return (master_new, first_new, second_new)


def one_hot(indices, filled, size):
    hit = indices[..., None] == jnp.arange(size, dtype=jnp.int32)
    return (hit & filled[..., None]).astype(BF16)


def frame_plans(lengths, packs, offsets, counts, source_rows, row_count, capacity):
    n_dp = lax.axis_size("dp")
    own = lax.axis_index("dp")
    slot = jnp.arange(capacity, dtype=jnp.int32)
    ids = jnp.arange(n_dp, dtype=jnp.int32)
    own_lengths, own_packs = pick(lengths, own, 1), pick(packs, own, 1)
    starts = jnp.cumsum(own_lengths, axis=1) - own_lengths
    matches = own_packs[:, None, :] == ids[None, :, None]
    length_to = jnp.sum(jnp.where(matches, own_lengths[:, None, :], 0), axis=2)
    start_to = jnp.sum(jnp.where(matches, starts[:, None, :], 0), axis=2)
    filled = slot < length_to[..., None]
    send = one_hot(start_to[..., None] + slot, filled, source_rows)
    here = packs == own

    def chosen(values):
        return jnp.sum(jnp.where(here, values, 0), axis=2)

    length_from, offset_from, count_from = chosen(lengths), chosen(offsets), chosen(counts)
    filled = slot < length_from[..., None]
    back = one_hot(offset_from[..., None] + slot, filled, row_count)
    position = jnp.arange(row_count, dtype=jnp.int32)
    inside = (position[None, :, None] >= offset_from[:, None, :]) & (
        position[None, :, None] < (offset_from + length_from)[:, None, :]
    )

    def select(values):
        return jnp.sum(jnp.where(inside, values[:, None, :], 0), axis=2)

    source = select(jnp.broadcast_to(ids, offset_from.shape))
    weight = select(count_from).astype(F32) / select(length_from).astype(F32)
    return send, back, source, weight


def on_device(
    x_source, skip_source, out_cotangent, item_length, item_pack, item_offset, item_count,
    gains, w_skip, w_qkv, w_out, w_up, w_down,
    gains_first, first_skip, first_qkv, first_out, first_up, first_down,
    gains_second, second_skip, second_qkv, second_out, second_up, second_down,
):
    n_y, n_c, n_a, n_b = sizes()
    n_dp, n_fsdp = n_y * n_c, n_a * n_b
    y, c, a, b = place()
    dp, fsdp = lax.axis_index("dp"), lax.axis_index("fsdp")
    micro, source_rows, width = x_source.shape
    row_count = out_cotangent.shape[1]
    capacity = source_rows // n_dp
    rows = micro * row_count

    send, back, source, weight = frame_plans(
        item_length[0], item_pack[0], item_offset[0], item_count[0], source_rows, row_count, capacity
    )

    def to_packs(values):
        return jnp.einsum("bpsr,brw->bpsw", send, values, preferred_element_type=F32).astype(BF16)

    payload = jnp.concatenate([to_packs(x_source), to_packs(skip_source)], axis=-1)
    shards = [w.astype(BF16) for w in (w_skip, w_qkv, w_out, w_up, w_down)]
    own_gains = gains.shape[1]
    low_gains = jnp.zeros((8, 128), F32).at[:2, :own_gains].set(gains.astype(BF16).astype(F32))
    (used_skip, used_qkv, used_out, used_up, used_down), arrived, gains_all = gather_all(
        shards, payload, low_gains
    )
    used_gains = jnp.moveaxis(gains_all[:, :2, :own_gains], 0, 1).reshape(2, width)

    packed = jnp.einsum("bpst,bpsw->btw", back, arrived, preferred_element_type=F32)
    packed = packed.astype(BF16).reshape(rows, 2 * width)
    base_rows = dot_rows(packed, used_skip)
    normal_one, scale_one = norm_parts(base_rows)
    normed_one = (normal_one * used_gains[0]).astype(BF16)
    qkv_rows = dot_rows(normed_one, used_qkv).astype(BF16)
    heads_shape = (micro, row_count, HEADS, HD)
    queries = qkv_rows[:, :width].reshape(heads_shape)
    keys_all = qkv_rows[:, width : 2 * width].reshape(heads_shape)
    values_all = qkv_rows[:, 2 * width :].reshape(heads_shape)
    alibi_terms = alibi_bias(row_count)
    same_item = source[:, :, None] == source[:, None, :]
    scores = attention_scores(queries, keys_all, alibi_terms, same_item)
    row_peak = jnp.max(scores, axis=-1, keepdims=True)
    log_total = row_peak + jnp.log(jnp.sum(jnp.exp(scores - row_peak), axis=-1, keepdims=True))
    probs_low = jnp.exp(scores - log_total).astype(BF16)
    mixed = jnp.einsum("nhqk,nkhe->nqhe", probs_low, values_all, preferred_element_type=F32)
    mixed = mixed.reshape(rows, width).astype(BF16)
    after_attn = base_rows + dot_rows(mixed, used_out)
    normal_two, scale_two = norm_parts(after_attn)
    normed_two = (normal_two * used_gains[1]).astype(BF16)
    up_rows = dot_rows(normed_two, used_up)
    activated, gelu_back = jax.vjp(partial(jax.nn.gelu, approximate=True), up_rows)
    activated = activated.astype(BF16)
    out_frames = (after_attn + dot_rows(activated, used_down)).astype(BF16)

    d_out = weight.reshape(rows, 1) * out_cotangent.reshape(rows, width).astype(F32)
    d_out_low = d_out.astype(BF16)
    grad_down = weight_gradient(activated, d_out_low, False)
    d_up = gelu_back(dot_right(d_out_low, used_down))[0].astype(BF16)
    grad_up = weight_gradient(normed_two, d_up, True)
    d_after_norm, grad_gain_two = norm_back(
        normal_two, scale_two, used_gains[1], dot_right(d_up, used_up)
    )
    d_after = d_out + d_after_norm
    d_after_low = d_after.astype(BF16)
    grad_out = weight_gradient(mixed, d_after_low, False)
    d_mixed = dot_right(d_after_low, used_out).astype(BF16).reshape(heads_shape)
    scores = attention_scores(queries, keys_all, alibi_terms, same_item)
    probs = jnp.exp(scores - log_total)
    probs_low = probs.astype(BF16)
    d_probs = jnp.einsum("nqhe,nkhe->nhqk", d_mixed, values_all, preferred_element_type=F32)
    d_values = jnp.einsum("nhqk,nqhe->nkhe", probs_low, d_mixed, preferred_element_type=F32)
    d_scores = (probs * (d_probs - jnp.sum(probs * d_probs, axis=-1, keepdims=True))).astype(BF16)
    d_queries = jnp.einsum("nhqk,nkhe->nqhe", d_scores, keys_all, preferred_element_type=F32)
    d_keys = jnp.einsum("nhqk,nqhe->nkhe", d_scores, queries, preferred_element_type=F32)
    d_qkv = jnp.concatenate(
        [
            (d_queries * HD ** (-0.5)).reshape(rows, width),
            (d_keys * HD ** (-0.5)).reshape(rows, width),
            d_values.reshape(rows, width),
        ],
        axis=1,
    ).astype(BF16)
    grad_qkv = weight_gradient(normed_one, d_qkv, True)
    d_base_norm, grad_gain_one = norm_back(
        normal_one, scale_one, used_gains[0], dot_right(d_qkv, used_qkv)
    )
    d_base_low = (d_after + d_base_norm).astype(BF16)
    d_packed = dot_right(d_base_low, used_skip).astype(BF16).reshape(micro, row_count, 2 * width)
    returning = jnp.einsum("bpst,btw->bpsw", back, d_packed, preferred_element_type=F32).astype(BF16)
    returned = jnp.zeros_like(returning)
    returned = lax.dynamic_update_index_in_dim(returned, pick(returning, dp, 1), dp, 1)
    for k in range(1, n_dp):
        pairs = [
            (s * n_fsdp + f, (s + k) % n_dp * n_fsdp + f) for s in range(n_dp) for f in range(n_fsdp)
        ]
        got = lax.ppermute(pick(returning, (dp + k) % n_dp, 1), ("dp", "fsdp"), pairs)
        returned = lax.dynamic_update_index_in_dim(returned, got, (dp - k) % n_dp, 1)
    grad_skip = weight_gradient(packed, d_base_low, False)
    in_gradient = jnp.einsum("bpsr,bpsw->brw", send, returned, preferred_element_type=F32)
    in_gradient = in_gradient.astype(BF16)
    input_gradient, skip_gradient = in_gradient[..., :width], in_gradient[..., width:]

    grad_gains = lax.psum(jnp.stack([grad_gain_one, grad_gain_two]), ("dp", "fsdp"))
    grad_gains = pick(grad_gains.reshape(2, n_fsdp, own_gains), fsdp, 1)

    gradients = (grad_skip, grad_qkv, grad_out, grad_up, grad_down, grad_gains)
    squares = jnp.float32(0.0)
    for gradient in gradients:
        squares = squares + jnp.sum(gradient * gradient)
    squares = sum_over(sum_over(jnp.full((8, 128), squares), "b", n_b), "a", n_a)
    gradient_norm = jnp.sqrt(squares[0, 0])
    param_count = 6 * D * D + 2 * D * FF + 2 * D
    clip = jnp.minimum(1.0, 0.02 * math.sqrt(param_count) / gradient_norm)
    grad_skip, grad_qkv, grad_out, grad_up, grad_down, grad_gains = [clip * g for g in gradients]
    results = [out_frames.reshape(micro, row_count, width), input_gradient, skip_gradient]
    results.append(gradient_norm.reshape(1))
    results.extend(adam_update(gains, gains_first, gains_second, grad_gains, 0.3, 0.0))
    for master, first, second, gradient, fan_in in (
        (w_skip, first_skip, second_skip, grad_skip, 2 * D),
        (w_qkv, first_qkv, second_qkv, grad_qkv, D),
        (w_out, first_out, second_out, grad_out, D // 16),
        (w_up, first_up, second_up, grad_up, D),
        (w_down, first_down, second_down, grad_down, FF),
    ):
        new = adam_update(master, first, second, gradient, 0.5 / math.sqrt(fan_in), WEIGHT_DECAY)
        results.extend(new)
        results.append(new[0].astype(BF16))
    return tuple(results)


def solution(mesh):
    frames = P(None, ("dp", "fsdp"), None)
    plan = P("fsdp", None, None, None)
    gain, weight = P(None, "fsdp"), P("fsdp", None)
    return jax.shard_map(
        on_device,
        mesh=mesh,
        in_specs=(frames,) * 3 + (plan,) * 4 + ((gain,) + (weight,) * 5) * 3,
        out_specs=(frames,) * 3 + (P(),) + (gain,) * 3 + (weight,) * 20,
        check_vma=False,
    )
```

```python
from functools import partial
import math

import jax
import jax.numpy as jnp
from jax import lax
from jax.experimental import pallas as pl
from jax.experimental.pallas import tpu as pltpu
from jax.sharding import PartitionSpec as P

D = 1024
HEADS = 16
HD = 64
FF = 4096
STEP = 5
CORES = 2
OUTER = 4

BETA_FIRST = 0.5
BETA_SECOND = 0.5
ADAM_EPSILON = 1e-08
WEIGHT_DECAY = 0.01
NORM_EPSILON = 1e-05

BF16 = jnp.bfloat16
F32 = jnp.float32
MESH = pl.DeviceIdType.MESH

GATHER_UNITS = (
    (0, 0, 2, False), (0, 1, 2, False), (1, 0, 2, True), (1, 1, 2, True), (2, 0, 1, False),
    (3, 0, 2, True), (3, 1, 2, True),
    (4, 0, 4, False), (4, 1, 4, False), (4, 2, 4, False), (4, 3, 4, False),
)
VMEM_LIMIT = 63 * 2**20
REDUCE_UNITS = (
    (4, 0, 2, False), (4, 1, 2, False), (3, 0, 2, True), (3, 1, 2, True), (2, 0, 1, False),
    (1, 0, 2, False), (1, 1, 2, False), (0, 0, 2, False), (0, 1, 2, False),
)


def sizes():
    n_dp, n_fsdp = lax.axis_size("dp"), lax.axis_size("fsdp")
    return n_dp // CORES, CORES, OUTER, n_fsdp // OUTER


def place():
    rows, cores, outer, inner = sizes()
    dp, fsdp = lax.axis_index("dp"), lax.axis_index("fsdp")
    return dp // cores, lax.rem(dp, cores), fsdp // inner, lax.rem(fsdp, inner)


def turn(value, step, size):
    return lax.rem(value + (step + size) % size, size)


class Copies:
    def __init__(self, send_sem, recv_sem, local_sem):
        self.send_sem, self.recv_sem, self.local_sem = send_sem, recv_sem, local_sem
        self.remotes, self.locals, self.sent = 0, 0, []

    def remote(self, src, dst, land, device):
        index = self.remotes
        self.remotes += 1
        sems = dict(send_sem=self.send_sem.at[index], recv_sem=self.recv_sem.at[index])
        copy = pltpu.make_async_remote_copy(
            src_ref=src, dst_ref=dst, device_id=device, device_id_type=MESH, **sems
        )
        copy.start()
        self.sent.append(copy)
        return pltpu.make_async_remote_copy(
            src_ref=src, dst_ref=land, device_id=device, device_id_type=MESH, **sems
        )

    def local(self, src, dst):
        index = self.locals
        self.locals += 1
        copy = pltpu.make_async_copy(src, dst, self.local_sem.at[index])
        copy.start()
        return copy


def whole(ref, first=0, width=None):
    n_a, n_b, rows, columns = ref.shape
    width = columns if width is None else width
    return ref[:, :, :, pl.ds(first, width)].reshape(n_a * n_b * rows, width)


def row_loop(rows, chunk, body):
    @pl.loop(0, rows // chunk)
    def _(i):
        body(pl.ds(pl.multiple_of(i * chunk, chunk), chunk))


def norm_into(hidden, gain_row, target):
    def body(at):
        centre = hidden[at, :]
        centre = centre - jnp.mean(centre, axis=-1, keepdims=True)
        spread = jnp.mean(centre * centre, axis=-1, keepdims=True)
        target[at, :] = (centre * lax.rsqrt(spread + NORM_EPSILON) * gain_row).astype(BF16)

    row_loop(hidden.shape[0], 64, body)


GELU_SCALE = math.sqrt(2.0 / math.pi)


def gelu(u):
    return 0.5 * u * (1.0 + jnp.tanh(GELU_SCALE * (u + 0.044715 * (u * u * u))))


def head_probs(queries, keys_all, distance, same, slope):
    scores = lax.dot_general(
        queries, keys_all, (((1,), (1,)), ((), ())), preferred_element_type=F32
    )
    scores = jnp.where(same, scores * HD ** (-0.5) - slope * distance, -1e30)
    weights = jnp.exp(scores - jnp.max(scores, axis=-1, keepdims=True))
    return weights / jnp.sum(weights, axis=-1, keepdims=True)


def pair_mask(rows):
    lane = lax.broadcasted_iota(jnp.int32, (rows, 2 * HD), 1)
    return lane < HD


def forward_kernel(dims, *refs):
    n_y, n_c, n_a, n_b = dims
    masters, payload, gains, pack_hot, ids_down, ids_across, slopes = (
        refs[:5], refs[5], refs[6], refs[7], refs[8], refs[9], refs[10]
    )
    refs = refs[11:]
    fulls_out, refs = refs[:5], refs[5:]
    packed_out, base_out, qkv_out, mixed_out, after_out, up_out, act_out = refs[:7]
    one_out, two_out, frames_out, gains_out = refs[7:11]
    refs = refs[11:]
    fulls, refs = refs[:5], refs[5:]
    stage, arrived, hot, gains_all, packed, base, one, qkv, mixed, after, two, up, out = refs[:13]
    send_sem, recv_sem, local_sem = refs[13:]
    dp, fsdp = lax.axis_index("dp"), lax.axis_index("fsdp")
    y, c, a, b = dp // n_c, lax.rem(dp, n_c), fsdp // n_b, lax.rem(fsdp, n_b)
    n_dp, n_fsdp = n_y * n_c, n_a * n_b
    copies = Copies(send_sem, recv_sem, local_sem)
    remote, local = copies.remote, copies.local
    micro = payload.shape[0]
    slots = payload.shape[2]

    staged = {}

    def load(m):
        rows, columns = masters[m].shape
        view = stage.at[m % 2, pl.ds(0, rows * columns // 1024)]
        if columns == 1024:
            staged[m] = [local(masters[m], view)]
        else:
            parts = columns // 1024
            staged[m] = [
                local(
                    masters[m].at[:, pl.ds(p * 1024, 1024)],
                    stage.at[m % 2, pl.ds(p * rows, rows)],
                )
                for p in range(parts)
            ]

    load(0)
    load(1)
    frames = []
    slab = n_dp * slots

    def slot(group):
        return pl.ds(pl.multiple_of(group * slots, 16), slots)

    gain_copies = []
    own_gains = local(gains, gains_all.at[fsdp])
    hot_copy = local(pack_hot, hot)
    for k in range(1, n_dp):
        to, back = turn(dp, k, n_dp), turn(dp, -k, n_dp)
        for i in range(micro):
            frames.append(
                remote(
                    payload.at[i, to], arrived.at[i, slot(dp)], arrived.at[i, slot(back)], (to, fsdp)
                )
            )
    own_frames = [local(payload.at[i, dp], arrived.at[i, slot(dp)]) for i in range(micro)]

    units = []
    for m, part, parts, shared in GATHER_UNITS:
        width = masters[m].shape[1] // parts
        units.append((m, part * width, width, shared and width // (n_c * n_y) % 128 == 0))
    state = [{"x": [], "y": [], "c": []} for _ in units]

    def columns(u, of_c, of_y):
        m, first, width, shared = units[u]
        if shared:
            step = width // (n_c * n_y)
            return pl.ds(pl.multiple_of(first + (of_c * n_y + of_y) * step, 128), step)
        step = width // n_c
        return pl.ds(pl.multiple_of(first + of_c * step, 128), step)

    def convert(m):
        for copy in staged[m]:
            copy.wait()
        rows, width = masters[m].shape

        def body(at):
            for p in range(width // 1024):
                low = stage[m % 2, pl.ds(at.start + p * rows, at.size), :].astype(BF16)
                fulls[m][a, b, at, pl.ds(p * 1024, 1024)] = low

        row_loop(rows, 32, body)

    def stage_z(u):
        m = units[u][0]
        cols = columns(u, c, y)
        view = fulls[m].at[a, b, :, cols]
        state[u]["z"] = [
            remote(
                view, view, fulls[m].at[turn(a, -k, n_a), b, :, cols],
                (dp, turn(a, k, n_a) * n_b + b),
            )
            for k in range(1, n_a)
        ]

    def spread(u, block_a, block_b, of_y, to_y):
        m, first, width, shared = units[u]
        full = fulls[m]
        view = full.at[block_a, block_b, :, columns(u, c, of_y)]
        if to_y and shared:
            for k in range(1, n_y):
                source = turn(y, -k, n_y)
                landing = full.at[block_a, block_b, :, columns(u, c, source)]
                copy = remote(view, view, landing, (turn(y, k, n_y) * n_c + c, fsdp))
                state[u]["y"].append((copy, block_a, block_b, source))
        landing = full.at[block_a, block_b, :, columns(u, 1 - c, of_y)]
        state[u]["c"].append(remote(view, view, landing, (y * n_c + 1 - c, fsdp)))

    def send_x(u, step):
        m = units[u][0]
        cols, block_a = columns(u, c, y), turn(a, -step, n_a)
        view = fulls[m].at[block_a, b, :, cols]
        for k in range(1, n_b):
            landing = fulls[m].at[block_a, turn(b, -k, n_b), :, cols]
            state[u]["x"].append(remote(view, view, landing, (dp, a * n_b + turn(b, k, n_b))))

    def stage_own(u):
        send_x(u, 0)

    def stage_x(u):
        for k in range(1, n_a):
            state[u]["z"][k - 1].wait_recv()
            send_x(u, k)
            spread(u, turn(a, -k, n_a), b, y, True)

    def stage_s(u):
        for copy in state[u]["x"]:
            copy.wait_recv()
        for k in range(1, n_b):
            spread(u, slice(None), turn(b, -k, n_b), y, True)

    def stage_c(u):
        for copy, block_a, block_b, source in state[u]["y"]:
            copy.wait_recv()
            spread(u, block_a, block_b, source, False)

    outgoing = []

    def finish(u):
        m, first, width, shared = units[u]
        for copy in state[u]["c"]:
            copy.wait_recv()
        cols = pl.ds(first, width)
        outgoing.append(local(fulls[m].at[:, :, :, cols], fulls_out[m].at[:, :, :, cols]))

    for m in range(5):
        convert(m)
        if m + 2 < 5:
            load(m + 2)
        for u in range(len(units)):
            if units[u][0] == m:
                stage_z(u)
        if m == 0:
            stage_own(0)
            stage_own(1)
            for k in range(1, n_fsdp):
                to, back = turn(fsdp, k, n_fsdp), turn(fsdp, -k, n_fsdp)
                gain_copies.append(
                    remote(gains, gains_all.at[fsdp], gains_all.at[back], (dp, to))
                )

    count = len(units)

    def comm(u):
        if u + 2 < count:
            stage_own(u + 2)
        if u < count:
            stage_x(u)
        if u >= 1:
            stage_s(u - 1)

    tokens, width = base.shape
    per_pack = tokens // micro

    def make_packed():
        for copy in frames:
            copy.wait_recv()
        for copy in own_frames:
            copy.wait()
        hot_copy.wait()
        for i in range(micro):
            for half in range(2):
                cols = pl.ds(half * 1024, 1024)
                packed[pl.ds(i * per_pack, per_pack), cols] = jnp.dot(
                    hot[i], arrived[i, :, cols], preferred_element_type=F32
                ).astype(BF16)
        outgoing.append(local(packed, packed_out))

    gain_rows = []

    def make_gains():
        for copy in gain_copies:
            copy.wait_recv()
        own_gains.wait()
        outgoing.append(local(gains_all, gains_out))
        own = D // n_fsdp
        for row in range(2):
            gain_rows.append(
                jnp.concatenate([gains_all[f, pl.ds(row, 1), pl.ds(0, own)] for f in range(n_fsdp)], axis=1)
            )

    def make_base():
        for first in (0, 512):
            base[:, pl.ds(first, 512)] = jnp.dot(
                packed[...], whole(fulls[0], first, 512), preferred_element_type=F32
            )
        norm_into(base, gain_rows[0], one)
        outgoing.append(local(base, base_out))
        outgoing.append(local(one, one_out))

    def make_qkv():
        for first in range(0, 3 * D, 512):
            qkv[:, pl.ds(first, 512)] = jnp.dot(
                one[...], whole(fulls[1], first, 512), preferred_element_type=F32
            ).astype(BF16)
        outgoing.append(local(qkv, qkv_out))

    def attend(i):
        rows = pl.ds(i * per_pack, per_pack)
        position = lax.broadcasted_iota(jnp.int32, (per_pack, per_pack), 0)
        distance = jnp.abs(
            position - lax.broadcasted_iota(jnp.int32, (per_pack, per_pack), 1)
        ).astype(F32)
        first_head = pair_mask(per_pack)

        @pl.loop(0, HEADS // 2)
        def _(pair):
            def cols(part):
                return pl.ds(pl.multiple_of(part * D + pair * 2 * HD, 128), 2 * HD)

            same = ids_down[i] == ids_across[i]
            queries, keys_all, values_all = (qkv[rows, cols(part)] for part in range(3))
            results = []
            for head in range(2):
                mine = first_head if head == 0 else jnp.logical_not(first_head)
                slope = slopes[pl.ds(2 * pair + head, 1), :]
                probs = head_probs(
                    jnp.where(mine, queries, jnp.zeros_like(queries)), keys_all, distance, same, slope
                )
                results.append(
                    jnp.dot(probs.astype(BF16), values_all, preferred_element_type=F32)
                )
            mixed[rows, cols(0)] = jnp.where(first_head, results[0], results[1]).astype(BF16)

    def make_after():
        outgoing.append(local(mixed, mixed_out))
        for first in (0, 512):
            cols = pl.ds(first, 512)
            after[:, cols] = base[:, cols] + jnp.dot(
                mixed[...], whole(fulls[2], first, 512), preferred_element_type=F32
            )
        norm_into(after, gain_rows[1], two)
        outgoing.append(local(after, after_out))
        outgoing.append(local(two, two_out))

    up_copies = [None, None]
    half_ff = FF // 2

    def make_up(j):
        slot_now = j % 2
        if up_copies[slot_now] is not None:
            up_copies[slot_now].wait()
        cols = pl.ds(j * 512, 512)
        up[slot_now] = jnp.dot(
            two[...], whole(fulls[3], j * 512, 512), preferred_element_type=F32
        )
        up_copies[slot_now] = local(up.at[slot_now], up_out.at[:, cols])
        half, within = j * 512 // half_ff, j * 512 % half_ff

        def body(at):
            act = gelu(up[slot_now, at, :]).astype(BF16)
            arrived[half, at, pl.ds(within, 512)] = act

        row_loop(tokens, 64, body)

    def send_act(half):
        outgoing.append(
            local(arrived.at[half], act_out.at[:, pl.ds(half * half_ff, half_ff)])
        )

    def make_out(first, step):
        cols = pl.ds(first, step)
        weight = whole(fulls[4], first, step)
        total = after[:, cols] + jnp.dot(
            arrived[0], weight[:half_ff], preferred_element_type=F32
        )
        total += jnp.dot(arrived[1], weight[half_ff:], preferred_element_type=F32)
        out[:, cols] = total.astype(BF16)

    comm(0)
    comm(1)
    comm(2)
    make_gains()
    comm(3)
    make_packed()
    finish(0)
    finish(1)
    make_base()
    comm(4)
    stage_c(2)
    stage_c(3)
    comm(5)
    finish(2)
    finish(3)
    make_qkv()
    comm(6)
    attend(0)
    comm(7)
    finish(4)
    attend(1)
    make_after()
    stage_c(5)
    comm(8)
    finish(5)
    for j in range(4):
        make_up(j)
    send_act(0)
    stage_c(6)
    comm(9)
    finish(6)
    for j in range(4, 8):
        make_up(j)
    send_act(1)
    comm(10)
    finish(7)
    make_out(0, 256)
    comm(11)
    finish(8)
    make_out(256, 256)
    finish(9)
    make_out(512, 256)
    finish(10)
    make_out(768, 256)
    outgoing.append(local(out, frames_out))
    for copy in outgoing + [c for c in up_copies if c is not None]:
        copy.wait()
    for copy in copies.sent:
        copy.wait_send()


def forward_all(masters, payload, gains, pack_hot, source):
    dims = sizes()
    n_y, n_c, n_a, n_b = dims
    n_fsdp = n_a * n_b
    micro, n_dp, slots, _ = payload.shape
    per_pack = source.shape[1]
    tokens = micro * per_pack
    total = micro * (n_y * n_c - 1) + n_fsdp - 1
    for _, _, _, shared in GATHER_UNITS:
        groups = n_a - 1 + n_b - 1
        total += (n_a - 1) + n_a * (n_b - 1)
        total += (n_y - 1) * groups + n_y * groups if shared else groups
    shape = jax.ShapeDtypeStruct
    full_shapes = [(n_a, n_b) + master.shape for master in masters]
    out_shape = [shape(s, BF16) for s in full_shapes]
    out_shape += [
        shape((tokens, 2 * D), BF16), shape((tokens, D), F32), shape((tokens, 3 * D), BF16),
        shape((tokens, D), BF16), shape((tokens, D), F32), shape((tokens, FF), F32),
        shape((tokens, FF), BF16), shape((tokens, D), BF16), shape((tokens, D), BF16),
        shape((tokens, D), BF16), shape((n_fsdp,) + gains.shape, F32),
    ]
    anywhere = pl.BlockSpec(memory_space=pl.ANY)
    inside = pl.BlockSpec(memory_space=pltpu.VMEM)
    slopes = jnp.exp2(-8.0 * (jnp.arange(HEADS, dtype=F32) + 1.0) / HEADS)
    slopes = jnp.broadcast_to(slopes[:, None], (HEADS, per_pack))
    stage_rows = max(m.shape[0] * m.shape[1] // 1024 for m in masters)
    results = pl.pallas_call(
        partial(forward_kernel, dims),
        out_shape=out_shape,
        in_specs=[anywhere] * 8 + [inside] * 3,
        out_specs=[anywhere] * len(out_shape),
        scratch_shapes=[pltpu.VMEM(s, BF16) for s in full_shapes]
        + [
            pltpu.VMEM((2, stage_rows, 1024), F32),
            pltpu.VMEM((micro, n_dp * slots, 2 * D), BF16),
            pltpu.VMEM((micro, per_pack, n_dp * slots), BF16),
            pltpu.VMEM((n_fsdp,) + gains.shape, F32),
            pltpu.VMEM((tokens, 2 * D), BF16),
            pltpu.VMEM((tokens, D), F32),
            pltpu.VMEM((tokens, D), BF16),
            pltpu.VMEM((tokens, 3 * D), BF16),
            pltpu.VMEM((tokens, D), BF16),
            pltpu.VMEM((tokens, D), F32),
            pltpu.VMEM((tokens, D), BF16),
            pltpu.VMEM((2, tokens, 512), F32),
            pltpu.VMEM((tokens, D), BF16),
            pltpu.SemaphoreType.DMA((total,)),
            pltpu.SemaphoreType.DMA((total,)),
            pltpu.SemaphoreType.DMA((64,)),
        ],
        compiler_params=pltpu.CompilerParams(
            has_side_effects=True, vmem_limit_bytes=VMEM_LIMIT
        ),
        name="gather_and_forward",
    )(
        *masters, payload, gains, pack_hot,
        source[:, :, None], source[:, None, :], slopes,
    )
    return results


def move(value, axis, shift):
    n_y, n_c, n_a, n_b = sizes()
    dims = {"y": n_y, "c": n_c, "a": n_a, "b": n_b}
    pairs = []
    for source in range(n_y * n_c * n_a * n_b):
        at = {
            "y": source // (n_c * n_a * n_b),
            "c": source // (n_a * n_b) % n_c,
            "a": source // n_b % n_a,
            "b": source % n_b,
        }
        at[axis] = (at[axis] + shift) % dims[axis]
        target = ((at["y"] * n_c + at["c"]) * n_a + at["a"]) * n_b + at["b"]
        pairs.append((source, target))
    return lax.ppermute(value, ("dp", "fsdp"), pairs)


def swap(value, axis, mask):
    n_y, n_c, n_a, n_b = sizes()
    pairs = []
    for source in range(n_y * n_c * n_a * n_b):
        at = {
            "y": source // (n_c * n_a * n_b),
            "c": source // (n_a * n_b) % n_c,
            "a": source // n_b % n_a,
            "b": source % n_b,
        }
        at[axis] = at[axis] ^ mask
        target = ((at["y"] * n_c + at["c"]) * n_a + at["a"]) * n_b + at["b"]
        pairs.append((source, target))
    return lax.ppermute(value, ("dp", "fsdp"), pairs)


def pick(value, index, axis):
    return lax.dynamic_index_in_dim(value, index, axis, keepdims=False)


def add_all(values):
    total = values[0].astype(F32)
    for value in values[1:]:
        total = total + value.astype(F32)
    return total.astype(BF16)


def reduce_kernel(dims, shapes, *refs):
    n_y, n_c, n_a, n_b = dims
    count = 5
    lefts, rights, returning = refs[:count], refs[count : 2 * count], refs[2 * count]
    outs = refs[2 * count + 1 : 3 * count + 1]
    returned = refs[3 * count + 1]
    scratch = refs[3 * count + 2 :]
    sums, finals = scratch[:count], scratch[count : 2 * count]
    left_bufs, right_bufs = scratch[2 * count : 2 * count + 3], scratch[2 * count + 3 : 2 * count + 6]
    rest = scratch[2 * count + 6 :]
    landing = rest[: 3 * len(REDUCE_UNITS)]
    send_sem, recv_sem, local_sem, credit = rest[3 * len(REDUCE_UNITS) :]
    dp, fsdp = lax.axis_index("dp"), lax.axis_index("fsdp")
    y, c, a, b = dp // n_c, lax.rem(dp, n_c), fsdp // n_b, lax.rem(fsdp, n_b)
    n_dp = n_y * n_c
    used = [0, 0]
    sent = []
    other_core = (y * n_c + 1 - c, fsdp)
    slot_of = {4: 0, 0: 0, 3: 1, 1: 1, 2: 2}

    def remote(src, dst, land, device):
        index = used[0]
        used[0] += 1
        sems = dict(send_sem=send_sem.at[index], recv_sem=recv_sem.at[index])
        copy = pltpu.make_async_remote_copy(
            src_ref=src, dst_ref=dst, device_id=device, device_id_type=MESH, **sems
        )
        copy.start()
        sent.append(copy)
        return pltpu.make_async_remote_copy(
            src_ref=src, dst_ref=land, device_id=device, device_id_type=MESH, **sems
        )

    def local(src, dst):
        index = used[1]
        used[1] += 1
        copy = pltpu.make_async_copy(src, dst, local_sem.at[index])
        copy.start()
        return copy

    def turn(value, step, size):
        return lax.rem(value + (step + size) % size, size)

    tokens = lefts[0].shape[0]
    acts = {}

    def send_acts(m):
        depth, width = lefts[m].shape[1], rights[m].shape[1] // n_c
        left, right = left_bufs[slot_of[m]], right_bufs[slot_of[m]]
        mine = pl.ds(pl.multiple_of(c * width, 128), width)
        others = pl.ds(pl.multiple_of((1 - c) * width, 128), width)
        low, high = pl.ds(0, tokens), pl.ds(tokens, tokens)
        here = [
            local(rights[m].at[:, mine], right.at[low, pl.ds(0, width)]),
            local(lefts[m], left.at[low, pl.ds(0, depth)]),
        ]
        there = right.at[high, pl.ds(0, width)]
        away = [remote(rights[m].at[:, others], there, there, other_core)]
        there = left.at[high, pl.ds(0, depth)]
        away.append(remote(lefts[m], there, there, other_core))
        acts[m] = (here, away)

    def wait_acts(m):
        here, away = acts[m]
        for copy in here:
            copy.wait()
        for copy in away:
            copy.wait_recv()

    units = []
    for m, part, parts, shared in REDUCE_UNITS:
        width = shapes[m][1] // n_c // parts
        units.append((m, part * width, width, shared))
    state = [{} for _ in units]

    def piece(unit, of_y):
        m, first, width, shared = unit
        if shared:
            step = width // n_y
            return pl.ds(pl.multiple_of(first + of_y * step, 128), step), step
        return pl.ds(first, width), width

    def product(u):
        m, first, width, shared = units[u]
        rows = sums[m].shape[2]
        left, right, total = left_bufs[slot_of[m]], right_bufs[slot_of[m]], sums[m]
        group = max(1, 512 // (n_b * rows))
        tile = group * n_b * rows

        @pl.loop(0, n_a // group)
        def _(i):
            at = pl.ds(pl.multiple_of(i * tile, 128), tile)
            value = lax.dot_general(
                left[:, at], right[:, pl.ds(first, width)], (((0,), (0,)), ((), ())),
                preferred_element_type=F32,
            ).astype(BF16)
            total[pl.ds(i * group, group), :, :, pl.ds(first, width)] = value.reshape(
                group, n_b, rows, width
            )

    def chunks(outer, rows, body):
        chunk = min(64, rows)
        per = rows // chunk

        @pl.loop(0, outer * per)
        def _(i):
            body(i // per, pl.ds(pl.multiple_of(lax.rem(i, per) * chunk, 16), chunk))

    def y_send(u):
        m, first, width, shared = units[u]
        for k in range(1, n_y):
            cols, step = piece(units[u], turn(y, k, n_y))
            there = landing[3 * u].at[k - 1]
            state[u].setdefault("y", []).append(
                remote(sums[m].at[:, :, :, cols], there, there, (turn(y, k, n_y) * n_c + c, fsdp))
            )

    def y_add(u):
        m = units[u][0]
        for copy in state[u]["y"]:
            copy.wait_recv()
        cols, step = piece(units[u], y)

        def body(outer, rows):
            at = (outer // n_b, lax.rem(outer, n_b), rows, cols)
            value = sums[m][at].astype(F32)
            for k in range(1, n_y):
                value += landing[3 * u][k - 1, outer // n_b, lax.rem(outer, n_b), rows, :].astype(F32)
            sums[m][at] = value.astype(BF16)

        chunks(n_a * n_b, sums[m].shape[2], body)

    def x_land(u):
        return landing[3 * u + 1] if units[u][3] else landing[3 * u]

    def z_land(u):
        return landing[3 * u + 2] if units[u][3] else landing[3 * u + 1]

    def x_send(u):
        m = units[u][0]
        cols, step = piece(units[u], y)
        state[u]["x"] = []
        for k in range(1, n_b):
            there = x_land(u).at[k - 1]
            to = turn(b, k, n_b)
            state[u]["x"].append(
                remote(sums[m].at[:, to, :, cols], there, there, (dp, a * n_b + to))
            )

    def x_add(u):
        m = units[u][0]
        for copy in state[u]["x"]:
            copy.wait_recv()
        cols, step = piece(units[u], y)

        def body(outer, rows):
            value = sums[m][outer, b, rows, cols].astype(F32)
            for k in range(1, n_b):
                value += x_land(u)[k - 1, outer, rows, :].astype(F32)
            sums[m][outer, b, rows, cols] = value.astype(BF16)

        chunks(n_a, sums[m].shape[2], body)

    def z_send(u):
        m = units[u][0]
        cols, step = piece(units[u], y)
        state[u]["z"] = []
        for k in range(1, n_a):
            there = z_land(u).at[k - 1]
            to = turn(a, k, n_a)
            state[u]["z"].append(
                remote(sums[m].at[to, b, :, cols], there, there, (dp, to * n_b + b))
            )

    def z_add(u):
        m, first, width, shared = units[u]
        for copy in state[u]["z"]:
            copy.wait_recv()
        cols, step = piece(units[u], y)
        half = shapes[m][1] // n_c

        def body(outer, rows):
            value = sums[m][a, b, rows, cols].astype(F32)
            for k in range(1, n_a):
                value += z_land(u)[k - 1, rows, :].astype(F32)
            if shared:
                at = pl.ds(pl.multiple_of(c * half + first + y * step, 128), step)
                finals[m][rows, at] = value.astype(BF16)
            else:
                landing[3 * u + 2][y, rows, :] = value.astype(BF16)

        chunks(1, sums[m].shape[2], body)

    def last_send(u):
        m, first, width, shared = units[u]
        half = shapes[m][1] // n_c
        state[u]["last"] = []
        for k in range(1, n_y):
            device = (turn(y, k, n_y) * n_c + c, fsdp)
            from_y = turn(y, -k, n_y)
            if shared:
                step = width // n_y
                mine = pl.ds(pl.multiple_of(c * half + first + y * step, 128), step)
                theirs = pl.ds(pl.multiple_of(c * half + first + from_y * step, 128), step)
                view = finals[m].at[:, mine]
                state[u]["last"].append(remote(view, view, finals[m].at[:, theirs], device))
            else:
                view = landing[3 * u + 2].at[y]
                state[u]["last"].append(remote(view, view, landing[3 * u + 2].at[from_y], device))

    def last_add(u):
        m, first, width, shared = units[u]
        half = shapes[m][1] // n_c
        for copy in state[u]["last"]:
            copy.wait_recv()
        at = pl.ds(pl.multiple_of(c * half + first, 128), width)
        if not shared:

            def body(outer, rows):
                value = landing[3 * u + 2][0, rows, :].astype(F32)
                for k in range(1, n_y):
                    value += landing[3 * u + 2][k, rows, :].astype(F32)
                finals[m][rows, at] = value.astype(BF16)

            chunks(1, sums[m].shape[2], body)
        view = finals[m].at[:, at]
        theirs = pl.ds(pl.multiple_of((1 - c) * half + first, 128), width)
        state[u]["core"] = remote(view, view, finals[m].at[:, theirs], other_core)

    def give_credit(index):
        pl.semaphore_signal(credit.at[index], inc=1, device_id=other_core, device_id_type=MESH)

    for m in (4, 3, 2):
        send_acts(m)
    wait_acts(4)
    for u in (0, 1):
        product(u)
        x_send(u)
    give_credit(0)
    wait_acts(3)
    for u in (2, 3):
        product(u)
        y_send(u)
    give_credit(1)
    frames = []
    for k in range(1, n_dp):
        to, back = turn(dp, k, n_dp), turn(dp, -k, n_dp)
        frames.append(
            remote(returning.at[:, to], returned.at[:, dp], returned.at[:, back], (to, fsdp))
        )
    own_frames = local(returning.at[:, dp], returned.at[:, dp])
    wait_acts(2)
    product(4)
    x_send(4)
    pl.semaphore_wait(credit.at[1], 1)
    send_acts(1)
    pl.semaphore_wait(credit.at[0], 1)
    send_acts(0)
    wait_acts(1)
    for u in (5, 6):
        product(u)
        x_send(u)
    x_add(0)
    z_send(0)
    wait_acts(0)
    for u in (7, 8):
        product(u)
        x_send(u)

    def xz(u):
        x_add(u)
        z_send(u)

    def yx(u):
        y_add(u)
        x_send(u)

    def zl(u):
        z_add(u)
        last_send(u)

    for do, u in (
        (yx, 2), (xz, 1), (yx, 3), (zl, 0), (xz, 4), (zl, 1), (xz, 5), (zl, 4), (xz, 6), (zl, 5),
        (xz, 7), (zl, 6), (xz, 8), (zl, 7), (xz, 2), (zl, 8), (xz, 3), (zl, 2), (last_add, 0),
        (last_add, 1), (last_add, 4), (last_add, 5), (last_add, 6), (last_add, 7), (last_add, 8),
        (zl, 3), (last_add, 2), (last_add, 3),
    ):
        do(u)
    for u in range(len(units)):
        state[u]["core"].wait_recv()
    final_copies = [local(finals[m], outs[m]) for m in range(count)]
    for copy in frames:
        copy.wait_recv()
    own_frames.wait()
    for copy in sent:
        copy.wait_send()
    for copy in final_copies:
        copy.wait()


def reduce_all(lefts, rights, returning):
    dims = sizes()
    n_y, n_c, n_a, n_b = dims
    n_fsdp = n_a * n_b
    tokens = lefts[0].shape[0]
    shapes = [(left.shape[1], right.shape[1]) for left, right in zip(lefts, rights)]
    anywhere = pl.BlockSpec(memory_space=pl.ANY)
    scratch = [pltpu.VMEM((n_a, n_b, r // n_fsdp, w // n_c), BF16) for r, w in shapes]
    scratch += [pltpu.VMEM((r // n_fsdp, w), BF16) for r, w in shapes]
    scratch += [
        pltpu.VMEM((2 * tokens, max(shapes[m][0] for m in group)), BF16)
        for group in ((4, 0), (3, 1), (2,))
    ]
    scratch += [
        pltpu.VMEM((2 * tokens, max(shapes[m][1] // n_c for m in group)), BF16)
        for group in ((4, 0), (3, 1), (2,))
    ]
    for m, part, parts, shared in REDUCE_UNITS:
        rows, width = shapes[m][0] // n_fsdp, shapes[m][1] // n_c // parts
        if shared:
            step = width // n_y
            scratch += [
                pltpu.VMEM((n_y - 1, n_a, n_b, rows, step), BF16),
                pltpu.VMEM((n_b - 1, n_a, rows, step), BF16),
                pltpu.VMEM((n_a - 1, rows, step), BF16),
            ]
        else:
            scratch += [
                pltpu.VMEM((n_b - 1, n_a, rows, width), BF16),
                pltpu.VMEM((n_a - 1, rows, width), BF16),
                pltpu.VMEM((n_y, rows, width), BF16),
            ]
    total = 10 + n_y * n_c - 1
    for _, _, _, shared in REDUCE_UNITS:
        total += (n_b - 1) + (n_a - 1) + (n_y - 1) + 1 + (n_y - 1 if shared else 0)
    scratch += [
        pltpu.SemaphoreType.DMA((total,)),
        pltpu.SemaphoreType.DMA((total,)),
        pltpu.SemaphoreType.DMA((16,)),
        pltpu.SemaphoreType.REGULAR((2,)),
    ]
    out_shape = [jax.ShapeDtypeStruct((r // n_fsdp, w), BF16) for r, w in shapes]
    out_shape.append(jax.ShapeDtypeStruct(returning.shape, returning.dtype))
    results = pl.pallas_call(
        partial(reduce_kernel, dims, shapes),
        out_shape=out_shape,
        in_specs=[anywhere] * 11,
        out_specs=[anywhere] * 6,
        scratch_shapes=scratch,
        compiler_params=pltpu.CompilerParams(
            has_side_effects=True, vmem_limit_bytes=60 * 2**20
        ),
        name="reduce_gradients",
    )(*lefts, *rights, returning)
    return results[:5], results[5]


def sum_over(value, axis, count):
    mask = 1
    while mask < count:
        value = value + swap(value, axis, mask)
        mask *= 2
    return value


def dot_rows(left, right):
    return jnp.dot(left, right, preferred_element_type=F32)


def dot_right(left, right):
    return lax.dot_general(left, right, (((1,), (1,)), ((), ())), preferred_element_type=F32)


def norm_parts(hidden):
    centre = hidden - jnp.mean(hidden, axis=-1, keepdims=True)
    spread = jnp.mean(centre * centre, axis=-1, keepdims=True)
    scale = lax.rsqrt(spread + NORM_EPSILON)
    return centre * scale, scale


def norm_back(normal, scale, gain_row, gradient):
    scaled = gradient * gain_row
    grad_gain = jnp.sum(gradient * normal, axis=0)
    back = scale * (
        scaled
        - jnp.mean(scaled, axis=-1, keepdims=True)
        - normal * jnp.mean(scaled * normal, axis=-1, keepdims=True)
    )
    return back, grad_gain


def alibi_bias(length):
    position = jnp.arange(length, dtype=F32)
    distance = jnp.abs(position[:, None] - position[None, :])
    slopes = jnp.exp2(-8.0 * (jnp.arange(HEADS, dtype=F32) + 1.0) / HEADS)
    return -slopes[:, None, None] * distance[None]


def attention_scores(queries, keys_all, alibi_terms, same_item):
    scores = (
        jnp.einsum("nqhe,nkhe->nhqk", queries, keys_all, preferred_element_type=F32) * HD ** (-0.5)
        + alibi_terms[None]
    )
    return jnp.where(same_item[:, None], scores, -1e30)


def adam_update(master, first, second, gradient, rate, decay):
    first_new = BETA_FIRST * first + (1.0 - BETA_FIRST) * gradient
    second_new = BETA_SECOND * second + (1.0 - BETA_SECOND) * gradient * gradient
    first_hat = first_new / (1.0 - BETA_FIRST**STEP)
    second_hat = second_new / (1.0 - BETA_SECOND**STEP)
    master_new = master - rate * (
        first_hat / (jnp.sqrt(second_hat) + ADAM_EPSILON) + decay * master
    )
    return (master_new, first_new, second_new)


def one_hot(indices, filled, size):
    hit = indices[..., None] == jnp.arange(size, dtype=jnp.int32)
    return (hit & filled[..., None]).astype(BF16)


def frame_plans(lengths, packs, offsets, counts, source_rows, row_count, capacity):
    n_dp = lax.axis_size("dp")
    own = lax.axis_index("dp")
    slot = jnp.arange(capacity, dtype=jnp.int32)
    ids = jnp.arange(n_dp, dtype=jnp.int32)
    own_lengths, own_packs = pick(lengths, own, 1), pick(packs, own, 1)
    starts = jnp.cumsum(own_lengths, axis=1) - own_lengths
    matches = own_packs[:, None, :] == ids[None, :, None]
    length_to = jnp.sum(jnp.where(matches, own_lengths[:, None, :], 0), axis=2)
    start_to = jnp.sum(jnp.where(matches, starts[:, None, :], 0), axis=2)
    filled = slot < length_to[..., None]
    send = one_hot(start_to[..., None] + slot, filled, source_rows)
    here = packs == own

    def chosen(values):
        return jnp.sum(jnp.where(here, values, 0), axis=2)

    length_from, offset_from, count_from = chosen(lengths), chosen(offsets), chosen(counts)
    filled = slot < length_from[..., None]
    back = one_hot(offset_from[..., None] + slot, filled, row_count)
    position = jnp.arange(row_count, dtype=jnp.int32)
    inside = (position[None, :, None] >= offset_from[:, None, :]) & (
        position[None, :, None] < (offset_from + length_from)[:, None, :]
    )

    def select(values):
        return jnp.sum(jnp.where(inside, values[:, None, :], 0), axis=2)

    source = select(jnp.broadcast_to(ids, offset_from.shape))
    weight = select(count_from).astype(F32) / select(length_from).astype(F32)
    return send, back, source, weight


def on_device(
    x_source, skip_source, out_cotangent, item_length, item_pack, item_offset, item_count,
    gains, w_skip, w_qkv, w_out, w_up, w_down,
    gains_first, first_skip, first_qkv, first_out, first_up, first_down,
    gains_second, second_skip, second_qkv, second_out, second_up, second_down,
):
    n_y, n_c, n_a, n_b = sizes()
    n_dp, n_fsdp = n_y * n_c, n_a * n_b
    y, c, a, b = place()
    dp, fsdp = lax.axis_index("dp"), lax.axis_index("fsdp")
    micro, source_rows, width = x_source.shape
    row_count = out_cotangent.shape[1]
    capacity = source_rows // n_dp
    rows = micro * row_count

    send, back, source, weight = frame_plans(
        item_length[0], item_pack[0], item_offset[0], item_count[0], source_rows, row_count, capacity
    )

    def to_packs(values):
        return jnp.einsum("bpsr,brw->bpsw", send, values, preferred_element_type=F32).astype(BF16)

    payload = jnp.concatenate([to_packs(x_source), to_packs(skip_source)], axis=-1)
    own_gains = gains.shape[1]
    low_gains = jnp.zeros((8, 128), F32).at[:2, :own_gains].set(gains.astype(BF16).astype(F32))
    results = forward_all(
        (w_skip, w_qkv, w_out, w_up, w_down), payload, low_gains,
        jnp.moveaxis(back.reshape(micro, n_dp * capacity, row_count), 1, 2), source,
    )
    fulls, results = results[:5], results[5:]
    used_skip, used_qkv, used_out, used_up, used_down = (
        full.reshape(-1, full.shape[-1]) for full in fulls
    )
    packed, base_rows, qkv_rows, mixed, after_attn, up_rows, activated = results[:7]
    normed_one, normed_two, out_frames, gains_all = results[7:]
    used_gains = jnp.moveaxis(gains_all[:, :2, :own_gains], 0, 1).reshape(2, width)
    normal_one, scale_one = norm_parts(base_rows)
    normal_two, scale_two = norm_parts(after_attn)
    heads_shape = (micro, row_count, HEADS, HD)
    queries = qkv_rows[:, :width].reshape(heads_shape)
    keys_all = qkv_rows[:, width : 2 * width].reshape(heads_shape)
    values_all = qkv_rows[:, 2 * width :].reshape(heads_shape)
    alibi_terms = alibi_bias(row_count)
    same_item = source[:, :, None] == source[:, None, :]
    gelu_back = jax.vjp(partial(jax.nn.gelu, approximate=True), up_rows)[1]

    d_out = weight.reshape(rows, 1) * out_cotangent.reshape(rows, width).astype(F32)
    d_out_low = d_out.astype(BF16)
    d_up = gelu_back(dot_right(d_out_low, used_down))[0].astype(BF16)
    d_after_norm, grad_gain_two = norm_back(
        normal_two, scale_two, used_gains[1], dot_right(d_up, used_up)
    )
    d_after = d_out + d_after_norm
    d_after_low = d_after.astype(BF16)
    d_mixed = dot_right(d_after_low, used_out).astype(BF16).reshape(heads_shape)
    scores = attention_scores(queries, keys_all, alibi_terms, same_item)
    probs = jax.nn.softmax(scores, axis=-1)
    probs_low = probs.astype(BF16)
    d_probs = jnp.einsum("nqhe,nkhe->nhqk", d_mixed, values_all, preferred_element_type=F32)
    d_values = jnp.einsum("nhqk,nqhe->nkhe", probs_low, d_mixed, preferred_element_type=F32)
    d_scores = (probs * (d_probs - jnp.sum(probs * d_probs, axis=-1, keepdims=True))).astype(BF16)
    d_queries = jnp.einsum("nhqk,nkhe->nqhe", d_scores, keys_all, preferred_element_type=F32)
    d_keys = jnp.einsum("nhqk,nqhe->nkhe", d_scores, queries, preferred_element_type=F32)
    d_qkv = jnp.concatenate(
        [
            (d_queries * HD ** (-0.5)).reshape(rows, width),
            (d_keys * HD ** (-0.5)).reshape(rows, width),
            d_values.reshape(rows, width),
        ],
        axis=1,
    ).astype(BF16)
    d_base_norm, grad_gain_one = norm_back(
        normal_one, scale_one, used_gains[0], dot_right(d_qkv, used_qkv)
    )
    d_base_low = (d_after + d_base_norm).astype(BF16)
    d_packed = dot_right(d_base_low, used_skip).astype(BF16).reshape(micro, row_count, 2 * width)
    returning = jnp.einsum("bpst,btw->bpsw", back, d_packed, preferred_element_type=F32).astype(BF16)
    (grad_skip, grad_qkv, grad_out, grad_up, grad_down), returned = reduce_all(
        (packed, normed_one, mixed, normed_two, activated),
        (d_base_low, d_qkv, d_after_low, d_up, d_out_low),
        returning,
    )
    in_gradient = jnp.einsum("bpsr,bpsw->brw", send, returned, preferred_element_type=F32)
    in_gradient = in_gradient.astype(BF16)
    input_gradient, skip_gradient = in_gradient[..., :width], in_gradient[..., width:]

    grad_gains = lax.psum(jnp.stack([grad_gain_one, grad_gain_two]), ("dp", "fsdp"))
    grad_gains = pick(grad_gains.reshape(2, n_fsdp, own_gains), fsdp, 1)

    gradients = [g.astype(F32) for g in (grad_skip, grad_qkv, grad_out, grad_up, grad_down)]
    gradients.append(grad_gains)
    squares = jnp.float32(0.0)
    for gradient in gradients:
        squares = squares + jnp.sum(gradient * gradient)
    squares = sum_over(sum_over(jnp.full((8, 128), squares), "b", n_b), "a", n_a)
    gradient_norm = jnp.sqrt(squares[0, 0])
    param_count = 6 * D * D + 2 * D * FF + 2 * D
    clip = jnp.minimum(1.0, 0.02 * math.sqrt(param_count) / gradient_norm)
    grad_skip, grad_qkv, grad_out, grad_up, grad_down, grad_gains = [clip * g for g in gradients]
    results = [out_frames.reshape(micro, row_count, width), input_gradient, skip_gradient]
    results.append(gradient_norm.reshape(1))
    results.extend(adam_update(gains, gains_first, gains_second, grad_gains, 0.3, 0.0))
    for master, first, second, gradient, fan_in in (
        (w_skip, first_skip, second_skip, grad_skip, 2 * D),
        (w_qkv, first_qkv, second_qkv, grad_qkv, D),
        (w_out, first_out, second_out, grad_out, D // 16),
        (w_up, first_up, second_up, grad_up, D),
        (w_down, first_down, second_down, grad_down, FF),
    ):
        new = adam_update(master, first, second, gradient, 0.5 / math.sqrt(fan_in), WEIGHT_DECAY)
        results.extend(new)
        results.append(new[0].astype(BF16))
    return tuple(results)


def solution(mesh):
    frames = P(None, ("dp", "fsdp"), None)
    plan = P("fsdp", None, None, None)
    gain, weight = P(None, "fsdp"), P("fsdp", None)
    return jax.shard_map(
        on_device,
        mesh=mesh,
        in_specs=(frames,) * 3 + (plan,) * 4 + ((gain,) + (weight,) * 5) * 3,
        out_specs=(frames,) * 3 + (P(),) + (gain,) * 3 + (weight,) * 20,
        check_vma=False,
    )
```

```python
from functools import partial
import math

import jax
import jax.numpy as jnp
from jax import lax
from jax.experimental import pallas as pl
from jax.experimental.pallas import tpu as pltpu
from jax.sharding import PartitionSpec as P

D = 1024
HEADS = 16
HD = 64
FF = 4096
STEP = 5
CORES = 2
OUTER = 4

BETA_FIRST = 0.5
BETA_SECOND = 0.5
ADAM_EPSILON = 1e-08
WEIGHT_DECAY = 0.01
NORM_EPSILON = 1e-05

BF16 = jnp.bfloat16
F32 = jnp.float32
MESH = pl.DeviceIdType.MESH

GATHER_UNITS = (
    (0, 0, 2, False), (0, 1, 2, False), (1, 0, 2, True), (1, 1, 2, True), (2, 0, 1, False),
    (3, 0, 2, True), (3, 1, 2, True),
    (4, 0, 4, False), (4, 1, 4, False), (4, 2, 4, False), (4, 3, 4, False),
)
VMEM_LIMIT = 63 * 2**20
REDUCE_UNITS = (
    (4, 0, 2, False), (4, 1, 2, False), (3, 0, 2, True), (3, 1, 2, True), (2, 0, 1, False),
    (1, 0, 2, False), (1, 1, 2, False), (0, 0, 2, False), (0, 1, 2, False),
)


def sizes():
    n_dp, n_fsdp = lax.axis_size("dp"), lax.axis_size("fsdp")
    return n_dp // CORES, CORES, OUTER, n_fsdp // OUTER


def place():
    rows, cores, outer, inner = sizes()
    dp, fsdp = lax.axis_index("dp"), lax.axis_index("fsdp")
    return dp // cores, lax.rem(dp, cores), fsdp // inner, lax.rem(fsdp, inner)


def turn(value, step, size):
    return lax.rem(value + (step + size) % size, size)


class Remote:
    def __init__(self, src, dst, land, device, **sems):
        self.given = pltpu.make_async_remote_copy(
            src_ref=src, dst_ref=dst, device_id=device, device_id_type=MESH, **sems
        )
        self.given.start()
        self.taken = (src, land, device, sems)
        self.left = False

    def wait_recv(self):
        src, land, device, sems = self.taken
        pltpu.make_async_remote_copy(
            src_ref=src, dst_ref=land, device_id=device, device_id_type=MESH, **sems
        ).wait_recv()

    def wait_send(self):
        if not self.left:
            self.given.wait_send()
        self.left = True


class Copies:
    def __init__(self, send_sem, recv_sem, local_sem):
        self.send_sem, self.recv_sem, self.local_sem = send_sem, recv_sem, local_sem
        self.locals, self.sent = 0, []

    def remote(self, src, dst, land, device):
        index = len(self.sent)
        sems = dict(send_sem=self.send_sem.at[index], recv_sem=self.recv_sem.at[index])
        self.sent.append(Remote(src, dst, land, device, **sems))
        return self.sent[-1]

    def local(self, src, dst):
        index = self.locals
        self.locals += 1
        copy = pltpu.make_async_copy(src, dst, self.local_sem.at[index])
        copy.start()
        return copy


def whole(ref, first=0, width=None):
    n_a, n_b, rows, columns = ref.shape
    width = columns if width is None else width
    return ref[:, :, :, pl.ds(first, width)].reshape(n_a * n_b * rows, width)


def row_loop(rows, chunk, body):
    @pl.loop(0, rows // chunk)
    def _(i):
        body(pl.ds(pl.multiple_of(i * chunk, chunk), chunk))


def norm_into(hidden, gain_row, target, hat, scales, first):
    def body(at):
        centre = hidden[at, :]
        centre = centre - jnp.mean(centre, axis=-1, keepdims=True)
        spread = jnp.mean(centre * centre, axis=-1, keepdims=True)
        scale = lax.rsqrt(spread + NORM_EPSILON)
        normal = centre * scale
        target[at, :] = (normal * gain_row).astype(BF16)
        hat[at, :] = normal.astype(BF16)
        scales[at, pl.ds(first, 64)] = jnp.broadcast_to(scale, (scale.shape[0], 64))

    row_loop(hidden.shape[0], 64, body)


GELU_SCALE = math.sqrt(2.0 / math.pi)


def gelu_and_slope(u):
    square = u * u
    bent = jnp.tanh(GELU_SCALE * (u + 0.044715 * (square * u)))
    half = 0.5 * (1.0 + bent)
    slope = half + (0.5 * GELU_SCALE) * u * (1.0 - bent * bent) * (1.0 + 0.134145 * square)
    return u * half, slope


def head_probs(queries, keys_all, distance, same, slope):
    scores = lax.dot_general(
        queries, keys_all, (((1,), (1,)), ((), ())), preferred_element_type=F32
    )
    scores = jnp.where(same, scores * HD ** (-0.5) - slope * distance, -1e30)
    weights = jnp.exp(scores - jnp.max(scores, axis=-1, keepdims=True))
    return weights / jnp.sum(weights, axis=-1, keepdims=True)


def pair_mask(rows):
    lane = lax.broadcasted_iota(jnp.int32, (rows, 2 * HD), 1)
    return lane < HD


def forward_kernel(dims, *refs):
    n_y, n_c, n_a, n_b = dims
    masters, payload, gains, pack_hot, ids_down, ids_across, slopes = (
        refs[:5], refs[5], refs[6], refs[7], refs[8], refs[9], refs[10]
    )
    refs = refs[11:]
    fulls_out, refs = refs[:5], refs[5:]
    packed_out, qkv_out, mixed_out, slope_out, act_out, one_out, two_out = refs[:7]
    hat_one_out, hat_two_out, scales_out, frames_out, gains_out = refs[7:12]
    refs = refs[12:]
    fulls, refs = refs[:5], refs[5:]
    stage, arrived, hot, gains_all, packed, base, one, qkv, mixed, after, two, up, out = refs[:13]
    hat_one, hat_two, scales, slope_buf = refs[13:17]
    send_sem, recv_sem, local_sem = refs[17:]
    dp, fsdp = lax.axis_index("dp"), lax.axis_index("fsdp")
    y, c, a, b = dp // n_c, lax.rem(dp, n_c), fsdp // n_b, lax.rem(fsdp, n_b)
    n_dp, n_fsdp = n_y * n_c, n_a * n_b
    copies = Copies(send_sem, recv_sem, local_sem)
    remote, local = copies.remote, copies.local
    micro = payload.shape[0]
    slots = payload.shape[2]

    staged = {}

    def load(m):
        rows, columns = masters[m].shape
        view = stage.at[m % 2, pl.ds(0, rows * columns // 1024)]
        if columns == 1024:
            staged[m] = [local(masters[m], view)]
        else:
            parts = columns // 1024
            staged[m] = [
                local(
                    masters[m].at[:, pl.ds(p * 1024, 1024)],
                    stage.at[m % 2, pl.ds(p * rows, rows)],
                )
                for p in range(parts)
            ]

    load(0)
    load(1)
    frames = []
    slab = n_dp * slots

    def slot(group):
        return pl.ds(pl.multiple_of(group * slots, 16), slots)

    gain_copies = []
    own_gains = local(gains, gains_all.at[fsdp])
    hot_copy = local(pack_hot, hot)
    for k in range(1, n_dp):
        to, back = turn(dp, k, n_dp), turn(dp, -k, n_dp)
        for i in range(micro):
            frames.append(
                remote(
                    payload.at[i, to], arrived.at[i, slot(dp)], arrived.at[i, slot(back)], (to, fsdp)
                )
            )
    own_frames = [local(payload.at[i, dp], arrived.at[i, slot(dp)]) for i in range(micro)]

    units = []
    for m, part, parts, shared in GATHER_UNITS:
        width = masters[m].shape[1] // parts
        units.append((m, part * width, width, shared and width // (n_c * n_y) % 128 == 0))
    state = [{"x": [], "y": [], "c": []} for _ in units]

    def columns(u, of_c, of_y):
        m, first, width, shared = units[u]
        if shared:
            step = width // (n_c * n_y)
            return pl.ds(pl.multiple_of(first + (of_c * n_y + of_y) * step, 128), step)
        step = width // n_c
        return pl.ds(pl.multiple_of(first + of_c * step, 128), step)

    def convert(m):
        for copy in staged[m]:
            copy.wait()
        rows, width = masters[m].shape

        def body(at):
            for p in range(width // 1024):
                low = stage[m % 2, pl.ds(at.start + p * rows, at.size), :].astype(BF16)
                fulls[m][a, b, at, pl.ds(p * 1024, 1024)] = low

        row_loop(rows, 32, body)

    def stage_z(u):
        m = units[u][0]
        cols = columns(u, c, y)
        view = fulls[m].at[a, b, :, cols]
        state[u]["z"] = [
            remote(
                view, view, fulls[m].at[turn(a, -k, n_a), b, :, cols],
                (dp, turn(a, k, n_a) * n_b + b),
            )
            for k in range(1, n_a)
        ]

    def spread(u, block_a, block_b, of_y, to_y):
        m, first, width, shared = units[u]
        full = fulls[m]
        view = full.at[block_a, block_b, :, columns(u, c, of_y)]
        if to_y and shared:
            for k in range(1, n_y):
                source = turn(y, -k, n_y)
                landing = full.at[block_a, block_b, :, columns(u, c, source)]
                copy = remote(view, view, landing, (turn(y, k, n_y) * n_c + c, fsdp))
                state[u]["y"].append((copy, block_a, block_b, source))
        landing = full.at[block_a, block_b, :, columns(u, 1 - c, of_y)]
        state[u]["c"].append(remote(view, view, landing, (y * n_c + 1 - c, fsdp)))

    def send_x(u, step):
        m = units[u][0]
        cols, block_a = columns(u, c, y), turn(a, -step, n_a)
        view = fulls[m].at[block_a, b, :, cols]
        for k in range(1, n_b):
            landing = fulls[m].at[block_a, turn(b, -k, n_b), :, cols]
            state[u]["x"].append(remote(view, view, landing, (dp, a * n_b + turn(b, k, n_b))))

    def stage_own(u):
        send_x(u, 0)

    def stage_x(u):
        for k in range(1, n_a):
            state[u]["z"][k - 1].wait_recv()
            send_x(u, k)
            spread(u, turn(a, -k, n_a), b, y, True)

    def stage_s(u):
        for copy in state[u]["x"]:
            copy.wait_recv()
        for k in range(1, n_b):
            spread(u, slice(None), turn(b, -k, n_b), y, True)

    def stage_c(u):
        for copy, block_a, block_b, source in state[u]["y"]:
            copy.wait_recv()
            spread(u, block_a, block_b, source, False)

    outgoing = []

    def finish(u):
        m, first, width, shared = units[u]
        for copy in state[u]["c"]:
            copy.wait_recv()
        cols = pl.ds(first, width)
        outgoing.append(local(fulls[m].at[:, :, :, cols], fulls_out[m].at[:, :, :, cols]))

    for m in range(5):
        convert(m)
        if m + 2 < 5:
            load(m + 2)
        for u in range(len(units)):
            if units[u][0] == m:
                stage_z(u)
        if m == 0:
            stage_own(0)
            stage_own(1)
            for k in range(1, n_fsdp):
                to, back = turn(fsdp, k, n_fsdp), turn(fsdp, -k, n_fsdp)
                gain_copies.append(
                    remote(gains, gains_all.at[fsdp], gains_all.at[back], (dp, to))
                )

    count = len(units)

    def comm(u):
        if u + 2 < count:
            stage_own(u + 2)
        if u < count:
            stage_x(u)
        if u >= 1:
            stage_s(u - 1)

    tokens, width = base.shape
    per_pack = tokens // micro

    def make_packed():
        for copy in frames:
            copy.wait_recv()
        for copy in own_frames:
            copy.wait()
        hot_copy.wait()
        for i in range(micro):
            for half in range(2):
                cols = pl.ds(half * 1024, 1024)
                packed[pl.ds(i * per_pack, per_pack), cols] = jnp.dot(
                    hot[i], arrived[i, :, cols], preferred_element_type=F32
                ).astype(BF16)
        outgoing.append(local(packed, packed_out))

    gain_rows = []

    def make_gains():
        for copy in gain_copies:
            copy.wait_recv()
        own_gains.wait()
        outgoing.append(local(gains_all, gains_out))
        own = D // n_fsdp
        for row in range(2):
            gain_rows.append(
                jnp.concatenate([gains_all[f, pl.ds(row, 1), pl.ds(0, own)] for f in range(n_fsdp)], axis=1)
            )

    def make_base():
        for first in (0, 512):
            base[:, pl.ds(first, 512)] = jnp.dot(
                packed[...], whole(fulls[0], first, 512), preferred_element_type=F32
            )
        norm_into(base, gain_rows[0], one, hat_one, scales, 0)
        outgoing.append(local(hat_one, hat_one_out))
        outgoing.append(local(one, one_out))

    def make_qkv():
        for first in range(0, 3 * D, 512):
            qkv[:, pl.ds(first, 512)] = jnp.dot(
                one[...], whole(fulls[1], first, 512), preferred_element_type=F32
            ).astype(BF16)
        outgoing.append(local(qkv, qkv_out))

    def attend(i):
        rows = pl.ds(i * per_pack, per_pack)
        position = lax.broadcasted_iota(jnp.int32, (per_pack, per_pack), 0)
        distance = jnp.abs(
            position - lax.broadcasted_iota(jnp.int32, (per_pack, per_pack), 1)
        ).astype(F32)
        first_head = pair_mask(per_pack)

        @pl.loop(0, HEADS // 2)
        def _(pair):
            def cols(part):
                return pl.ds(pl.multiple_of(part * D + pair * 2 * HD, 128), 2 * HD)

            same = ids_down[i] == ids_across[i]
            queries, keys_all, values_all = (qkv[rows, cols(part)] for part in range(3))
            results = []
            for head in range(2):
                mine = first_head if head == 0 else jnp.logical_not(first_head)
                slope = slopes[pl.ds(2 * pair + head, 1), :]
                probs = head_probs(
                    jnp.where(mine, queries, jnp.zeros_like(queries)), keys_all, distance, same, slope
                )
                results.append(
                    jnp.dot(probs.astype(BF16), values_all, preferred_element_type=F32)
                )
            mixed[rows, cols(0)] = jnp.where(first_head, results[0], results[1]).astype(BF16)

    def make_after():
        outgoing.append(local(mixed, mixed_out))
        for first in (0, 512):
            cols = pl.ds(first, 512)
            after[:, cols] = base[:, cols] + jnp.dot(
                mixed[...], whole(fulls[2], first, 512), preferred_element_type=F32
            )
        norm_into(after, gain_rows[1], two, hat_two, scales, 64)
        outgoing.append(local(hat_two, hat_two_out))
        outgoing.append(local(scales, scales_out))
        outgoing.append(local(two, two_out))

    slope_copies = [None, None]
    half_ff = FF // 2

    def make_up(j):
        slot_now = j % 2
        cols = pl.ds(j * 512, 512)
        up[...] = jnp.dot(two[...], whole(fulls[3], j * 512, 512), preferred_element_type=F32)
        if slope_copies[slot_now] is not None:
            slope_copies[slot_now].wait()
        half, within = j * 512 // half_ff, j * 512 % half_ff

        def body(at):
            value, slope = gelu_and_slope(up[at, :])
            arrived[half, at, pl.ds(within, 512)] = value.astype(BF16)
            slope_buf[slot_now, at, :] = slope.astype(BF16)

        row_loop(tokens, 64, body)
        slope_copies[slot_now] = local(slope_buf.at[slot_now], slope_out.at[:, cols])

    def send_act(half):
        outgoing.append(
            local(arrived.at[half], act_out.at[:, pl.ds(half * half_ff, half_ff)])
        )

    def make_out(first, step):
        cols = pl.ds(first, step)
        weight = whole(fulls[4], first, step)
        total = after[:, cols] + jnp.dot(
            arrived[0], weight[:half_ff], preferred_element_type=F32
        )
        total += jnp.dot(arrived[1], weight[half_ff:], preferred_element_type=F32)
        out[:, cols] = total.astype(BF16)

    comm(0)
    comm(1)
    comm(2)
    make_gains()
    comm(3)
    make_packed()
    finish(0)
    finish(1)
    make_base()
    comm(4)
    stage_c(2)
    stage_c(3)
    comm(5)
    finish(2)
    finish(3)
    make_qkv()
    comm(6)
    attend(0)
    comm(7)
    finish(4)
    attend(1)
    make_after()
    stage_c(5)
    comm(8)
    finish(5)
    for j in range(4):
        make_up(j)
    send_act(0)
    stage_c(6)
    comm(9)
    finish(6)
    for j in range(4, 8):
        make_up(j)
    send_act(1)
    comm(10)
    finish(7)
    make_out(0, 256)
    comm(11)
    finish(8)
    make_out(256, 256)
    finish(9)
    make_out(512, 256)
    finish(10)
    make_out(768, 256)
    outgoing.append(local(out, frames_out))
    for copy in outgoing + slope_copies:
        copy.wait()
    for copy in copies.sent:
        copy.wait_send()


def forward_all(masters, payload, gains, pack_hot, source):
    dims = sizes()
    n_y, n_c, n_a, n_b = dims
    n_fsdp = n_a * n_b
    micro, n_dp, slots, _ = payload.shape
    per_pack = source.shape[1]
    tokens = micro * per_pack
    total = micro * (n_y * n_c - 1) + n_fsdp - 1
    for _, _, _, shared in GATHER_UNITS:
        groups = n_a - 1 + n_b - 1
        total += (n_a - 1) + n_a * (n_b - 1)
        total += (n_y - 1) * groups + n_y * groups if shared else groups
    shape = jax.ShapeDtypeStruct
    full_shapes = [(n_a, n_b) + master.shape for master in masters]
    out_shape = [shape(s, BF16) for s in full_shapes]
    out_shape += [
        shape((tokens, 2 * D), BF16), shape((tokens, 3 * D), BF16), shape((tokens, D), BF16),
        shape((tokens, FF), BF16), shape((tokens, FF), BF16),
        shape((tokens, D), BF16), shape((tokens, D), BF16),
        shape((tokens, D), BF16), shape((tokens, D), BF16),
        shape((tokens, 128), F32),
        shape((tokens, D), BF16), shape((n_fsdp,) + gains.shape, F32),
    ]
    anywhere = pl.BlockSpec(memory_space=pl.ANY)
    inside = pl.BlockSpec(memory_space=pltpu.VMEM)
    slopes = jnp.exp2(-8.0 * (jnp.arange(HEADS, dtype=F32) + 1.0) / HEADS)
    slopes = jnp.broadcast_to(slopes[:, None], (HEADS, per_pack))
    stage_rows = max(m.shape[0] * m.shape[1] // 1024 for m in masters)
    results = pl.pallas_call(
        partial(forward_kernel, dims),
        out_shape=out_shape,
        in_specs=[anywhere] * 8 + [inside] * 3,
        out_specs=[anywhere] * len(out_shape),
        scratch_shapes=[pltpu.VMEM(s, BF16) for s in full_shapes]
        + [
            pltpu.VMEM((2, stage_rows, 1024), F32),
            pltpu.VMEM((micro, n_dp * slots, 2 * D), BF16),
            pltpu.VMEM((micro, per_pack, n_dp * slots), BF16),
            pltpu.VMEM((n_fsdp,) + gains.shape, F32),
            pltpu.VMEM((tokens, 2 * D), BF16),
            pltpu.VMEM((tokens, D), F32),
            pltpu.VMEM((tokens, D), BF16),
            pltpu.VMEM((tokens, 3 * D), BF16),
            pltpu.VMEM((tokens, D), BF16),
            pltpu.VMEM((tokens, D), F32),
            pltpu.VMEM((tokens, D), BF16),
            pltpu.VMEM((tokens, 512), F32),
            pltpu.VMEM((tokens, D), BF16),
            pltpu.VMEM((tokens, D), BF16),
            pltpu.VMEM((tokens, D), BF16),
            pltpu.VMEM((tokens, 128), F32),
            pltpu.VMEM((2, tokens, 512), BF16),
            pltpu.SemaphoreType.DMA((total,)),
            pltpu.SemaphoreType.DMA((total,)),
            pltpu.SemaphoreType.DMA((64,)),
        ],
        compiler_params=pltpu.CompilerParams(
            has_side_effects=True, vmem_limit_bytes=VMEM_LIMIT
        ),
        name="gather_and_forward",
    )(
        *masters, payload, gains, pack_hot,
        source[:, :, None], source[:, None, :], slopes,
    )
    return results


def norm_back(hat, scale, gain_row, gradient):
    scaled = gradient * gain_row
    back = scale * (
        scaled
        - jnp.mean(scaled, axis=-1, keepdims=True)
        - hat * jnp.mean(scaled * hat, axis=-1, keepdims=True)
    )
    return back, jnp.sum(gradient * hat, axis=0, keepdims=True)


RING = 4


def backward_kernel(dims, shapes, *refs):
    n_y, n_c, n_a, n_b = dims
    fulls, refs = refs[:5], refs[5:]
    (packed, qkv, mixed, slope, act, one, two, hat_one, hat_two, scales,
     cotangent, frame_weight, gains_all, back_hot, ids_down, ids_across, slopes) = refs[:17]
    refs = refs[17:]
    outs, returned, gains_out, squares_out = refs[:5], refs[5], refs[6], refs[7]
    refs = refs[8:]
    sums, finals, refs = refs[:5], refs[5:10], refs[10:]
    (pool, low_far, wide, wide_far, left_far, ring, slope_buf, acc, hidden,
     cot, low, hat, gain_buf, gain_land, square_buf, square_land) = refs[:16]
    refs = refs[16:]
    landing, refs = refs[: 3 * len(REDUCE_UNITS)], refs[3 * len(REDUCE_UNITS) :]
    send_sem, recv_sem, local_sem, credit = refs
    dp, fsdp = lax.axis_index("dp"), lax.axis_index("fsdp")
    y, c, a, b = dp // n_c, lax.rem(dp, n_c), fsdp // n_b, lax.rem(fsdp, n_b)
    n_dp, n_fsdp = n_y * n_c, n_a * n_b
    other_core = (y * n_c + 1 - c, fsdp)
    copies = Copies(send_sem, recv_sem, local_sem)
    remote, local = copies.remote, copies.local
    tokens = cot.shape[0]
    micro = ids_down.shape[0]
    per_pack = tokens // micro
    near, far = pl.ds(0, tokens), pl.ds(tokens, tokens)

    order = []
    for block in range(4):
        order += [(4, block * 1024, 0), (4, block * 1024, 512)]
        order += [(3, 0, block * 1024), (3, 0, block * 1024 + 512)]
    order += [(2, 0, 0), (2, 0, 512)]
    order += [(1, 0, first) for first in range(0, 3 * D, 512)]
    order += [(0, first, second) for first in (0, 1024) for second in (0, 512)]
    ring_copies = {}
    ring_state = [0, 0]

    def ring_load():
        index = ring_state[0]
        if index < len(order):
            m, first, second = order[index]
            ring_copies[index] = local(
                fulls[m].at[pl.ds(first, 1024), pl.ds(second, 512)], ring.at[index % RING]
            )
            ring_state[0] += 1

    def ring_next():
        index = ring_state[1]
        ring_state[1] += 1
        ring_copies.pop(index).wait()
        return ring.at[index % RING]

    def far_half(width):
        return pl.ds(pl.multiple_of((1 - c) * width, 128), width)

    cot_copy = local(cotangent, cot)
    for _ in range(RING):
        ring_load()
    half_ff = FF // 2
    slope_copies = {}

    def slope_load(j):
        slope_copies[j] = local(slope.at[:, pl.ds(j * 512, 512)], slope_buf.at[j % 2])

    slope_load(0)
    slope_load(1)
    act_here, act_away = [], []
    for half in range(2):
        view = act.at[:, pl.ds(half * half_ff, half_ff)]
        act_away.append(remote(view, pool.at[half, far], pool.at[half, far], other_core))
        act_here.append(local(view, pool.at[half, near]))
    hat_copy = local(hat_two, hat)
    two_away = remote(two, left_far, left_far, other_core)

    units = []
    for m, part, parts, shared in REDUCE_UNITS:
        width = shapes[m][1] // n_c // parts
        units.append((m, part * width, width, shared))
    state = [{} for _ in units]

    def piece(unit, of_y):
        m, first, width, shared = unit
        if shared:
            step = width // n_y
            return pl.ds(pl.multiple_of(first + of_y * step, 128), step), step
        return pl.ds(first, width), width

    def product(u, left_near, left_other, right_near, right_far):
        m, first, width, shared = units[u]
        rows = sums[m].shape[2]
        group = max(1, 512 // (n_b * rows))
        tile = group * n_b * rows
        half = shapes[m][1] // n_c
        mine = pl.ds(pl.multiple_of(c * half + first, 128), width)

        @pl.loop(0, n_a // group)
        def _(i):
            contract = (((0,), (0,)), ((), ()))
            value = lax.dot_general(
                left_near(i, tile), right_near[:, mine], contract, preferred_element_type=F32
            )
            value += lax.dot_general(
                left_other(i, tile), right_far[:, pl.ds(first, width)], contract,
                preferred_element_type=F32,
            )
            sums[m][pl.ds(i * group, group), :, :, pl.ds(first, width)] = value.astype(BF16).reshape(
                group, n_b, rows, width
            )

    def tiles(ref, rows, first):
        def pick_tile(i, tile):
            return ref[rows, pl.ds(pl.multiple_of(first + i * tile, 128), tile)]

        return pick_tile

    def pool_tiles(rows):
        def pick_tile(i, tile):
            per = half_ff // tile
            return pool[i // per, rows, pl.ds(pl.multiple_of(lax.rem(i, per) * tile, 128), tile)]

        return pick_tile

    def chunks(outer, rows, body):
        chunk = min(64, rows)
        per = rows // chunk

        @pl.loop(0, outer * per)
        def _(i):
            body(i // per, pl.ds(pl.multiple_of(lax.rem(i, per) * chunk, 16), chunk))


    def y_send(u):
        m, first, width, shared = units[u]
        for k in range(1, n_y):
            cols, step = piece(units[u], turn(y, k, n_y))
            there = landing[3 * u].at[k - 1]
            state[u].setdefault("y", []).append(
                remote(sums[m].at[:, :, :, cols], there, there, (turn(y, k, n_y) * n_c + c, fsdp))
            )

    def y_add(u):
        m = units[u][0]
        for copy in state[u]["y"]:
            copy.wait_recv()
        cols, step = piece(units[u], y)

        def body(outer, rows):
            at = (outer // n_b, lax.rem(outer, n_b), rows, cols)
            value = sums[m][at].astype(F32)
            for k in range(1, n_y):
                value += landing[3 * u][k - 1, outer // n_b, lax.rem(outer, n_b), rows, :].astype(F32)
            sums[m][at] = value.astype(BF16)

        chunks(n_a * n_b, sums[m].shape[2], body)

    def x_land(u):
        return landing[3 * u + 1] if units[u][3] else landing[3 * u]

    def z_land(u):
        return landing[3 * u + 2] if units[u][3] else landing[3 * u + 1]

    def x_send(u):
        m = units[u][0]
        cols, step = piece(units[u], y)
        state[u]["x"] = []
        for k in range(1, n_b):
            there = x_land(u).at[k - 1]
            to = turn(b, k, n_b)
            state[u]["x"].append(
                remote(sums[m].at[:, to, :, cols], there, there, (dp, a * n_b + to))
            )

    def x_add(u):
        m = units[u][0]
        for copy in state[u]["x"]:
            copy.wait_recv()
        cols, step = piece(units[u], y)

        def body(outer, rows):
            value = sums[m][outer, b, rows, cols].astype(F32)
            for k in range(1, n_b):
                value += x_land(u)[k - 1, outer, rows, :].astype(F32)
            sums[m][outer, b, rows, cols] = value.astype(BF16)

        chunks(n_a, sums[m].shape[2], body)

    def z_send(u):
        m = units[u][0]
        cols, step = piece(units[u], y)
        state[u]["z"] = []
        for k in range(1, n_a):
            there = z_land(u).at[k - 1]
            to = turn(a, k, n_a)
            state[u]["z"].append(
                remote(sums[m].at[to, b, :, cols], there, there, (dp, to * n_b + b))
            )

    def z_add(u):
        m, first, width, shared = units[u]
        for copy in state[u]["z"]:
            copy.wait_recv()
        cols, step = piece(units[u], y)
        half = shapes[m][1] // n_c

        def body(outer, rows):
            value = sums[m][a, b, rows, cols].astype(F32)
            for k in range(1, n_a):
                value += z_land(u)[k - 1, rows, :].astype(F32)
            if shared:
                at = pl.ds(pl.multiple_of(c * half + first + y * step, 128), step)
                finals[m][rows, at] = value.astype(BF16)
            elif n_y == 2:
                sums[m][a, b, rows, cols] = value.astype(BF16)
            else:
                landing[3 * u + 2][y, rows, :] = value.astype(BF16)

        chunks(1, sums[m].shape[2], body)

    def last_send(u):
        m, first, width, shared = units[u]
        half = shapes[m][1] // n_c
        state[u]["last"] = []
        for k in range(1, n_y):
            device = (turn(y, k, n_y) * n_c + c, fsdp)
            from_y = turn(y, -k, n_y)
            if shared:
                step = width // n_y
                mine = pl.ds(pl.multiple_of(c * half + first + y * step, 128), step)
                theirs = pl.ds(pl.multiple_of(c * half + first + from_y * step, 128), step)
                view = finals[m].at[:, mine]
                state[u]["last"].append(remote(view, view, finals[m].at[:, theirs], device))
            elif n_y == 2:
                view, there = sums[m].at[a, b, :, piece(units[u], y)[0]], landing[3 * u + 2].at[0]
                state[u]["last"].append(remote(view, there, there, device))
            else:
                view = landing[3 * u + 2].at[y]
                state[u]["last"].append(remote(view, view, landing[3 * u + 2].at[from_y], device))

    def last_add(u):
        m, first, width, shared = units[u]
        half = shapes[m][1] // n_c
        for copy in state[u]["last"]:
            copy.wait_recv()
        at = pl.ds(pl.multiple_of(c * half + first, 128), width)
        if not shared:

            def body(outer, rows):
                value = landing[3 * u + 2][0, rows, :].astype(F32)
                if n_y == 2:
                    value += sums[m][a, b, rows, pl.ds(first, width)].astype(F32)
                for k in range(1, n_y if n_y > 2 else 0):
                    value += landing[3 * u + 2][k, rows, :].astype(F32)
                finals[m][rows, at] = value.astype(BF16)

            chunks(1, sums[m].shape[2], body)
        view = finals[m].at[:, at]
        theirs = pl.ds(pl.multiple_of((1 - c) * half + first, 128), width)
        state[u]["core"] = remote(view, view, finals[m].at[:, theirs], other_core)

    def xz(u):
        x_add(u)
        z_send(u)

    def yx(u):
        y_add(u)
        x_send(u)

    def zl(u):
        z_add(u)
        last_send(u)


    def partners():
        result = []
        mask = 1
        while mask < n_b:
            result.append((dp, a * n_b + (b ^ mask)))
            mask *= 2
        mask = 1
        while mask < n_a:
            result.append((dp, (a ^ mask) * n_b + b))
            mask *= 2
        count = len(result)
        mask = 1
        while mask < n_y:
            result.append(((y ^ mask) * n_c + c, fsdp))
            mask *= 2
        result.append(other_core)
        return result, count

    every_partner, fsdp_count = partners()
    small = {}

    def exchange(name, step, buf, land, device):
        small[name, step] = remote(buf.at[step], land.at[step], land.at[step], device)

    def absorb(name, step, buf, land):
        small[name, step].wait_recv()
        buf[step + 1] = buf[step] + land[step]

    def gain_step(step):
        if step > 0:
            absorb("gains", step - 1, gain_buf, gain_land)
        if step < len(every_partner):
            exchange("gains", step, gain_buf, gain_land, every_partner[step])

    def give_credit(index):
        pl.semaphore_signal(credit.at[index], inc=1, device_id=other_core, device_id_type=MESH)


    own = D // n_fsdp

    def gain_row(row):
        return jnp.concatenate(
            [gains_all[f, pl.ds(row, 1), pl.ds(0, own)] for f in range(n_fsdp)], axis=1
        )

    cot_copy.wait()

    def low_body(at):
        low[at, :] = (frame_weight[at, :] * cot[at, :].astype(F32)).astype(BF16)

    row_loop(tokens, 64, low_body)
    low_away = remote(low.at[:, far_half(D // n_c)], low_far, low_far, other_core)

    def dot_right(left, right):
        return lax.dot_general(left, right, (((1,), (1,)), ((), ())), preferred_element_type=F32)

    def add_product(left, weight, first):
        for start in (0, 512):
            cols = pl.ds(start, 512)
            value = dot_right(left, weight[cols, :])
            acc[:, cols] = value if first else acc[:, cols] + value

    def feed_forward(block):
        down = (ring_next(), ring_next())
        for part in range(2):
            j = 2 * block + part
            slope_copies[j].wait()
            rows = pl.ds(part * 512, 512)
            d_act = dot_right(low[:, :512], down[0][rows, :])
            d_act += dot_right(low[:, 512:], down[1][rows, :])
            wide[:, pl.ds(j * 512, 512)] = (d_act * slope_buf[j % 2].astype(F32)).astype(BF16)
            if j + 2 < 8:
                slope_load(j + 2)
        ring_load()
        ring_load()
        for part in range(2):
            j = 2 * block + part
            add_product(wide[:, pl.ds(j * 512, 512)], ring_next(), j == 0)
            ring_load()

    feed_forward(0)
    feed_forward(1)
    for copy in act_here:
        copy.wait()
    for copy in act_away:
        copy.wait_recv()
    low_away.wait_recv()
    for u in (0, 1):
        product(u, pool_tiles(near), pool_tiles(far), low, low_far)
        x_send(u)
    give_credit(0)
    left_here = [
        local(two, pool.at[0, near, pl.ds(0, D)]),
        local(one, pool.at[0, near, pl.ds(D, D)]),
    ]
    qkv_here = [
        local(qkv.at[:, pl.ds(0, D)], pool.at[1, near, pl.ds(0, D)]),
        local(qkv.at[:, pl.ds(D, D)], pool.at[1, near, pl.ds(D, D)]),
        local(qkv.at[:, pl.ds(2 * D, D)], pool.at[1, far, pl.ds(0, D)]),
        local(mixed, pool.at[1, far, pl.ds(D, D)]),
    ]
    feed_forward(2)
    feed_forward(3)
    pl.semaphore_wait(credit.at[0], 1)
    there = pool.at[0, far, pl.ds(0, D)]
    mixed_away = remote(mixed, there, there, other_core)
    wide_away = remote(wide.at[:, far_half(half_ff)], wide_far, wide_far, other_core)
    hat_copy.wait()
    low_away.wait_send()
    gain_buf[0] = jnp.zeros_like(gain_buf[0])
    gain_two = gain_row(1)

    def after_body(at):
        back, grad_gain = norm_back(
            hat[at, :].astype(F32), scales[at, pl.ds(64, 1)], gain_two, acc[at, :]
        )
        d_after = frame_weight[at, :] * cot[at, :].astype(F32) + back
        hidden[at, :] = d_after
        low[at, :] = d_after.astype(BF16)
        gain_buf[0, pl.ds(1, 1), :] += grad_gain

    row_loop(tokens, 64, after_body)
    after_away = remote(low.at[:, far_half(D // n_c)], low_far, low_far, other_core)
    hat_copy = local(hat_one, hat)
    pair = (ring_next(), ring_next())
    for start in (0, 512):
        cols = pl.ds(start, 512)
        value = dot_right(low[:, :512], pair[0][cols, :]) + dot_right(low[:, 512:], pair[1][cols, :])
        cot[:, cols] = value.astype(BF16)
    ring_load()
    ring_load()
    for copy in left_here + qkv_here:
        copy.wait()
    two_away.wait_recv()
    wide_away.wait_recv()
    for u in (2, 3):
        product(u, tiles(pool.at[0], near, 0), tiles(left_far, near, 0), wide, wide_far)
        y_send(u)
    mixed_away.wait_recv()
    after_away.wait_recv()
    product(4, tiles(pool.at[1], far, D), tiles(pool.at[0], far, 0), low, low_far)
    give_credit(1)
    x_send(4)
    wide_away.wait_send()
    pl.semaphore_wait(credit.at[1], 1)
    packed_away = remote(packed, pool.at[0, far], pool.at[0, far], other_core)
    one_away = remote(one, left_far, left_far, other_core)

    def attend_back(i):
        rows = pl.ds(i * per_pack, per_pack)
        rows_far = pl.ds(tokens + i * per_pack, per_pack)
        position = lax.broadcasted_iota(jnp.int32, (per_pack, per_pack), 0)
        distance = jnp.abs(
            position - lax.broadcasted_iota(jnp.int32, (per_pack, per_pack), 1)
        ).astype(F32)
        first_head = pair_mask(per_pack)

        @pl.loop(0, HEADS // 2)
        def _(pair):
            def cols(first):
                return pl.ds(pl.multiple_of(first + pair * 2 * HD, 128), 2 * HD)

            same = ids_down[i] == ids_across[i]
            queries, keys_all = pool[1, rows, cols(0)], pool[1, rows, cols(D)]
            values_all = pool[1, rows_far, cols(0)]
            d_mixed = cot[rows, cols(0)]
            zero = jnp.zeros_like(queries)
            total = [None, None, None]
            for head in range(2):
                mine = first_head if head == 0 else jnp.logical_not(first_head)
                query, key, d_head = (
                    jnp.where(mine, value, zero) for value in (queries, keys_all, d_mixed)
                )
                probs = head_probs(
                    query, keys_all, distance, same, slopes[pl.ds(2 * pair + head, 1), :]
                )
                d_probs = dot_right(d_head, values_all)
                carried = jnp.sum(probs * d_probs, axis=-1, keepdims=True)
                d_scores = (probs * (d_probs - carried)).astype(BF16)
                contract = (((0,), (0,)), ((), ()))
                parts = (
                    jnp.dot(d_scores, key, preferred_element_type=F32),
                    lax.dot_general(d_scores, query, contract, preferred_element_type=F32),
                    lax.dot_general(
                        probs.astype(BF16), d_head, contract, preferred_element_type=F32
                    ),
                )
                total = [p if t is None else t + p for t, p in zip(total, parts)]
            wide[rows, cols(0)] = (total[0] * HD ** (-0.5)).astype(BF16)
            wide[rows, cols(D)] = (total[1] * HD ** (-0.5)).astype(BF16)
            wide[rows, cols(2 * D)] = total[2].astype(BF16)

    attend_back(0)
    xz(0)
    attend_back(1)
    qkv_half = 3 * D // n_c
    qkv_view = wide_far.at[:, pl.ds(0, qkv_half)]
    qkv_away = remote(wide.at[:, far_half(qkv_half)], qkv_view, qkv_view, other_core)
    for part in range(6):
        add_product(wide[:, pl.ds(part * 512, 512)], ring_next(), part == 0)
        ring_load()
    one_away.wait_recv()
    qkv_away.wait_recv()
    for u in (5, 6):
        product(u, tiles(pool.at[0], near, D), tiles(left_far, near, 0), wide, wide_far)
        x_send(u)
    packed_here = local(packed, pool.at[0, near])
    hat_copy.wait()
    after_away.wait_send()
    gain_one = gain_row(0)

    def base_body(at):
        back, grad_gain = norm_back(
            hat[at, :].astype(F32), scales[at, pl.ds(0, 1)], gain_one, acc[at, :]
        )
        low[at, :] = (hidden[at, :] + back).astype(BF16)
        gain_buf[0, pl.ds(0, 1), :] += grad_gain

    row_loop(tokens, 64, base_body)
    base_away = remote(low.at[:, far_half(D // n_c)], low_far, low_far, other_core)
    gain_step(0)
    qkv_away.wait_send()
    for half in range(2):
        pair = (ring_next(), ring_next())
        for start in (0, 512):
            cols = pl.ds(start, 512)
            value = dot_right(low[:, :512], pair[0][cols, :])
            value += dot_right(low[:, 512:], pair[1][cols, :])
            wide[:, pl.ds(half * 1024 + start, 512)] = value.astype(BF16)
        ring_load()
        ring_load()
    packed_here.wait()
    packed_away.wait_recv()
    base_away.wait_recv()
    for u in (7, 8):
        product(u, tiles(pool.at[0], near, 0), tiles(pool.at[0], far, 0), low, low_far)
    xz(1)
    slots = back_hot.shape[1] // n_dp
    slab = n_dp * slots
    for i in range(micro):
        for half in range(2):
            cols = pl.ds(half * 1024, 1024)
            pool[1, pl.ds(i * slab, slab), cols] = jnp.dot(
                back_hot[i], wide[pl.ds(i * per_pack, per_pack), cols], preferred_element_type=F32
            ).astype(BF16)
    frames = []

    def slot(group, base=0):
        return pl.ds(pl.multiple_of(base + group * slots, 16), slots)

    for k in range(1, n_dp):
        to, back = turn(dp, k, n_dp), turn(dp, -k, n_dp)
        for i in range(micro):
            frames.append(
                remote(
                    pool.at[1, slot(to, i * slab)], returned.at[i, slot(dp)],
                    returned.at[i, slot(back)], (to, fsdp),
                )
            )
    own_frames = [local(pool.at[1, slot(dp, i * slab)], returned.at[i, slot(dp)]) for i in range(micro)]
    gain_step(1)
    yx(2)
    xz(4)
    yx(3)
    x_send(7)
    x_send(8)
    steps = [
        (zl, 0), (zl, 1), (zl, 4), (xz, 5), (last_add, 0), (last_add, 1), (xz, 6), (zl, 5),
        (last_add, 4), (xz, 2), (zl, 6), (last_add, 5), (xz, 3), (zl, 2), (xz, 7), (zl, 3),
        (last_add, 6), (last_add, 2), (xz, 8), (zl, 7), (last_add, 3), (last_add, 7), (zl, 8),
        (last_add, 8),
    ]
    step_gain = 2
    for index, (do, u) in enumerate(steps):
        do(u)
        if index % 2 == 0 and step_gain <= len(every_partner):
            gain_step(step_gain)
            step_gain += 1
    while step_gain <= len(every_partner):
        gain_step(step_gain)
        step_gain += 1
    outgoing = []
    square_buf[0] = jnp.zeros_like(square_buf[0])

    def add_squares(m):
        rows, columns = finals[m].shape
        chunk = min(32, rows)

        @pl.loop(0, rows // chunk)
        def _(i):
            at = pl.ds(pl.multiple_of(i * chunk, chunk), chunk)
            for first in range(0, columns, 1024):
                value = finals[m][at, pl.ds(first, 1024)].astype(F32)
                value = (value * value).reshape(chunk // 8, 8, 8, 128)
                square_buf[0] += jnp.sum(value, axis=(0, 2))

    for m in (4, 3, 2, 1, 0):
        for u in range(len(units)):
            if units[u][0] == m:
                state[u]["core"].wait_recv()
        outgoing.append(local(finals[m], outs[m]))
        add_squares(m)
    for step in range(fsdp_count):
        exchange("squares", step, square_buf, square_land, every_partner[step])
        absorb("squares", step, square_buf, square_land)
    last = len(every_partner)
    outgoing.append(local(gain_buf.at[last], gains_out))
    outgoing.append(local(square_buf.at[fsdp_count], squares_out))
    for copy in frames:
        copy.wait_recv()
    for copy in own_frames + outgoing:
        copy.wait()
    for copy in copies.sent:
        copy.wait_send()


def backward_all(fulls, saved, cotangent, frame_weight, gains_all, back_hot, source):
    dims = sizes()
    n_y, n_c, n_a, n_b = dims
    n_fsdp = n_a * n_b
    tokens = cotangent.shape[0]
    micro, slab, per_pack = back_hot.shape
    shapes = [full.shape for full in fulls]
    shape = jax.ShapeDtypeStruct
    anywhere = pl.BlockSpec(memory_space=pl.ANY)
    inside = pl.BlockSpec(memory_space=pltpu.VMEM)
    steps = (n_y * n_c * n_a * n_b).bit_length() - 1
    scratch = [pltpu.VMEM((n_a, n_b, r // n_fsdp, w // n_c), BF16) for r, w in shapes]
    scratch += [pltpu.VMEM((r // n_fsdp, w), BF16) for r, w in shapes]
    scratch += [
        pltpu.VMEM((2, 2 * tokens, FF // 2), BF16),
        pltpu.VMEM((tokens, D // n_c), BF16),
        pltpu.VMEM((tokens, FF), BF16),
        pltpu.VMEM((tokens, FF // n_c), BF16),
        pltpu.VMEM((tokens, D), BF16),
        pltpu.VMEM((RING, 1024, 512), BF16),
        pltpu.VMEM((2, tokens, 512), BF16),
        pltpu.VMEM((tokens, D), F32),
        pltpu.VMEM((tokens, D), F32),
        pltpu.VMEM((tokens, D), BF16),
        pltpu.VMEM((tokens, D), BF16),
        pltpu.VMEM((tokens, D), BF16),
        pltpu.VMEM((steps + 1, 8, D), F32),
        pltpu.VMEM((steps, 8, D), F32),
        pltpu.VMEM((steps + 1, 8, 128), F32),
        pltpu.VMEM((steps, 8, 128), F32),
    ]
    for m, part, parts, shared in REDUCE_UNITS:
        rows, width = shapes[m][0] // n_fsdp, shapes[m][1] // n_c // parts
        if shared:
            step = width // n_y
            scratch += [
                pltpu.VMEM((n_y - 1, n_a, n_b, rows, step), BF16),
                pltpu.VMEM((n_b - 1, n_a, rows, step), BF16),
                pltpu.VMEM((n_a - 1, rows, step), BF16),
            ]
        else:
            scratch += [
                pltpu.VMEM((n_b - 1, n_a, rows, width), BF16),
                pltpu.VMEM((n_a - 1, rows, width), BF16),
                pltpu.VMEM((1 if n_y == 2 else n_y, rows, width), BF16),
            ]
    total = 10 + micro * (n_y * n_c - 1) + 2 * steps
    for _, _, _, shared in REDUCE_UNITS:
        total += (n_b - 1) + (n_a - 1) + (n_y - 1) + 1 + (n_y - 1 if shared else 0)
    scratch += [
        pltpu.SemaphoreType.DMA((total,)),
        pltpu.SemaphoreType.DMA((total,)),
        pltpu.SemaphoreType.DMA((72,)),
        pltpu.SemaphoreType.REGULAR((2,)),
    ]
    out_shape = [shape((r // n_fsdp, w), BF16) for r, w in shapes]
    out_shape += [
        shape((micro, slab, 2 * D), BF16), shape((8, D), F32), shape((8, 128), F32),
    ]
    slopes = jnp.exp2(-8.0 * (jnp.arange(HEADS, dtype=F32) + 1.0) / HEADS)
    slopes = jnp.broadcast_to(slopes[:, None], (HEADS, per_pack))
    results = pl.pallas_call(
        partial(backward_kernel, dims, shapes),
        out_shape=out_shape,
        in_specs=[anywhere] * 14 + [inside] + [anywhere] + [inside] * 6,
        out_specs=[anywhere] * len(out_shape),
        scratch_shapes=scratch,
        compiler_params=pltpu.CompilerParams(
            has_side_effects=True, vmem_limit_bytes=VMEM_LIMIT
        ),
        name="backward_and_reduce",
    )(
        *fulls, *saved, cotangent, frame_weight, gains_all, back_hot,
        source[:, :, None], source[:, None, :], slopes,
    )
    return results


def pick(value, index, axis):
    return lax.dynamic_index_in_dim(value, index, axis, keepdims=False)


def adam_update(master, first, second, gradient, rate, decay):
    first_new = BETA_FIRST * first + (1.0 - BETA_FIRST) * gradient
    second_new = BETA_SECOND * second + (1.0 - BETA_SECOND) * gradient * gradient
    first_hat = first_new / (1.0 - BETA_FIRST**STEP)
    second_hat = second_new / (1.0 - BETA_SECOND**STEP)
    master_new = master - rate * (
        first_hat / (jnp.sqrt(second_hat) + ADAM_EPSILON) + decay * master
    )
    return (master_new, first_new, second_new)


def one_hot(indices, filled, size):
    hit = indices[..., None] == jnp.arange(size, dtype=jnp.int32)
    return (hit & filled[..., None]).astype(BF16)


def frame_plans(lengths, packs, offsets, counts, source_rows, row_count, capacity):
    n_dp = lax.axis_size("dp")
    own = lax.axis_index("dp")
    slot = jnp.arange(capacity, dtype=jnp.int32)
    ids = jnp.arange(n_dp, dtype=jnp.int32)
    own_lengths, own_packs = pick(lengths, own, 1), pick(packs, own, 1)
    starts = jnp.cumsum(own_lengths, axis=1) - own_lengths
    matches = own_packs[:, None, :] == ids[None, :, None]
    length_to = jnp.sum(jnp.where(matches, own_lengths[:, None, :], 0), axis=2)
    start_to = jnp.sum(jnp.where(matches, starts[:, None, :], 0), axis=2)
    filled = slot < length_to[..., None]
    send = one_hot(start_to[..., None] + slot, filled, source_rows)
    here = packs == own

    def chosen(values):
        return jnp.sum(jnp.where(here, values, 0), axis=2)

    length_from, offset_from, count_from = chosen(lengths), chosen(offsets), chosen(counts)
    filled = slot < length_from[..., None]
    back = one_hot(offset_from[..., None] + slot, filled, row_count)
    position = jnp.arange(row_count, dtype=jnp.int32)
    inside = (position[None, :, None] >= offset_from[:, None, :]) & (
        position[None, :, None] < (offset_from + length_from)[:, None, :]
    )

    def select(values):
        return jnp.sum(jnp.where(inside, values[:, None, :], 0), axis=2)

    source = select(jnp.broadcast_to(ids, offset_from.shape))
    weight = select(count_from).astype(F32) / select(length_from).astype(F32)
    return send, back, source, weight


def on_device(
    x_source, skip_source, out_cotangent, item_length, item_pack, item_offset, item_count,
    gains, w_skip, w_qkv, w_out, w_up, w_down,
    gains_first, first_skip, first_qkv, first_out, first_up, first_down,
    gains_second, second_skip, second_qkv, second_out, second_up, second_down,
):
    n_y, n_c, n_a, n_b = sizes()
    n_dp, n_fsdp = n_y * n_c, n_a * n_b
    y, c, a, b = place()
    dp, fsdp = lax.axis_index("dp"), lax.axis_index("fsdp")
    micro, source_rows, width = x_source.shape
    row_count = out_cotangent.shape[1]
    capacity = source_rows // n_dp
    rows = micro * row_count

    send, back, source, weight = frame_plans(
        item_length[0], item_pack[0], item_offset[0], item_count[0], source_rows, row_count, capacity
    )

    def to_packs(values):
        return jnp.einsum("bpsr,brw->bpsw", send, values, preferred_element_type=F32).astype(BF16)

    payload = jnp.concatenate([to_packs(x_source), to_packs(skip_source)], axis=-1)
    own_gains = gains.shape[1]
    low_gains = jnp.zeros((8, 128), F32).at[:2, :own_gains].set(gains.astype(BF16).astype(F32))
    results = forward_all(
        (w_skip, w_qkv, w_out, w_up, w_down), payload, low_gains,
        jnp.moveaxis(back.reshape(micro, n_dp * capacity, row_count), 1, 2), source,
    )
    fulls, saved, out_frames, gains_all = results[:5], results[5:15], results[15], results[16]
    fulls = [full.reshape(-1, full.shape[-1]) for full in fulls]
    results = backward_all(
        fulls, saved, out_cotangent.reshape(rows, width), weight.reshape(rows, 1), gains_all,
        back.reshape(micro, n_dp * capacity, row_count), source,
    )
    gradients, returned, grad_gains, squares = results[:5], results[5], results[6], results[7]
    in_gradient = jnp.einsum(
        "bsr,bsw->brw", send.reshape(micro, n_dp * capacity, source_rows), returned,
        preferred_element_type=F32,
    ).astype(BF16)
    input_gradient, skip_gradient = in_gradient[..., :width], in_gradient[..., width:]
    grad_gains = grad_gains[:2]
    total_squares = jnp.sum(squares) + jnp.sum(grad_gains * grad_gains)
    gradient_norm = jnp.sqrt(total_squares)
    grad_gains = pick(grad_gains.reshape(2, n_fsdp, own_gains), fsdp, 1)
    gradients = [gradient.astype(F32) for gradient in gradients] + [grad_gains]
    param_count = 6 * D * D + 2 * D * FF + 2 * D
    clip = jnp.minimum(1.0, 0.02 * math.sqrt(param_count) / gradient_norm)
    grad_skip, grad_qkv, grad_out, grad_up, grad_down, grad_gains = [clip * g for g in gradients]
    results = [out_frames.reshape(micro, row_count, width), input_gradient, skip_gradient]
    results.append(gradient_norm.reshape(1))
    results.extend(adam_update(gains, gains_first, gains_second, grad_gains, 0.3, 0.0))
    for master, first, second, gradient, fan_in in (
        (w_skip, first_skip, second_skip, grad_skip, 2 * D),
        (w_qkv, first_qkv, second_qkv, grad_qkv, D),
        (w_out, first_out, second_out, grad_out, D // 16),
        (w_up, first_up, second_up, grad_up, D),
        (w_down, first_down, second_down, grad_down, FF),
    ):
        new = adam_update(master, first, second, gradient, 0.5 / math.sqrt(fan_in), WEIGHT_DECAY)
        results.extend(new)
        results.append(new[0].astype(BF16))
    return tuple(results)


def solution(mesh):
    frames = P(None, ("dp", "fsdp"), None)
    plan = P("fsdp", None, None, None)
    gain, weight = P(None, "fsdp"), P("fsdp", None)
    return jax.shard_map(
        on_device,
        mesh=mesh,
        in_specs=(frames,) * 3 + (plan,) * 4 + ((gain,) + (weight,) * 5) * 3,
        out_specs=(frames,) * 3 + (P(),) + (gain,) * 3 + (weight,) * 20,
        check_vma=False,
    )
```

```python
from functools import partial
import math

import jax
import jax.numpy as jnp
from jax import lax
from jax.experimental import pallas as pl
from jax.experimental.pallas import tpu as pltpu
from jax.sharding import PartitionSpec as P

D = 1024
HEADS = 16
HD = 64
FF = 4096
STEP = 5
CORES = 2
OUTER = 4

BETA_FIRST = 0.5
BETA_SECOND = 0.5
ADAM_EPSILON = 1e-08
WEIGHT_DECAY = 0.01
NORM_EPSILON = 1e-05

BF16 = jnp.bfloat16
F32 = jnp.float32
MESH = pl.DeviceIdType.MESH

GATHER_UNITS = (
    (0, 0, 2, False), (0, 1, 2, False), (1, 0, 2, True), (1, 1, 2, True), (2, 0, 1, False),
    (3, 0, 2, True), (3, 1, 2, True),
    (4, 0, 4, False), (4, 1, 4, False), (4, 2, 4, False), (4, 3, 4, False),
)
WINDOW, OWN_FIRST = 3, 4
VMEM_LIMIT = 63 * 2**20
REDUCE_UNITS = (
    (4, 0, 2, False), (4, 1, 2, False), (3, 0, 2, True), (3, 1, 2, True), (2, 0, 1, False),
    (1, 0, 2, False), (1, 1, 2, False),
    (0, 0, 4, False), (0, 1, 4, False), (0, 2, 4, False), (0, 3, 4, False),
)


def sizes():
    n_dp, n_fsdp = lax.axis_size("dp"), lax.axis_size("fsdp")
    return n_dp // CORES, CORES, OUTER, n_fsdp // OUTER


def place():
    rows, cores, outer, inner = sizes()
    dp, fsdp = lax.axis_index("dp"), lax.axis_index("fsdp")
    return dp // cores, lax.rem(dp, cores), fsdp // inner, lax.rem(fsdp, inner)


def turn(value, step, size):
    return lax.rem(value + (step + size) % size, size)


class Remote:
    def __init__(self, src, dst, land, device, **sems):
        def describe(target):
            return pltpu.make_async_remote_copy(
                src_ref=src, dst_ref=target, device_id=device, device_id_type=MESH, **sems
            )

        self.given, self.describe, self.land, self.left = describe(dst), describe, land, False
        self.given.start()

    def wait_recv(self):
        self.describe(self.land).wait_recv()

    def wait_send(self):
        if not self.left:
            self.given.wait_send()
        self.left = True


class Copies:
    def __init__(self, send_sem, recv_sem, local_sem):
        self.send_sem, self.recv_sem, self.local_sem = send_sem, recv_sem, local_sem
        self.locals, self.sent = 0, []

    def remote(self, src, dst, land, device):
        index = len(self.sent)
        sems = dict(send_sem=self.send_sem.at[index], recv_sem=self.recv_sem.at[index])
        self.sent.append(Remote(src, dst, land, device, **sems))
        return self.sent[-1]

    def local(self, src, dst):
        index = self.locals
        self.locals += 1
        copy = pltpu.make_async_copy(src, dst, self.local_sem.at[index])
        copy.start()
        return copy


def greet(dims, dp, fsdp):
    n_y, n_c, n_a, n_b = dims
    n_dp, n_fsdp = n_y * n_c, n_a * n_b
    barrier = pltpu.get_barrier_semaphore()
    partners = [(turn(dp, k, n_dp), fsdp) for k in range(1, n_dp)]
    partners += [(dp, turn(fsdp, k, n_fsdp)) for k in range(1, n_fsdp)]
    for partner in partners:
        pl.semaphore_signal(barrier, inc=1, device_id=partner, device_id_type=MESH)
    pl.semaphore_wait(barrier, len(partners))


def whole(ref, first=0, width=None):
    n_a, n_b, rows, columns = ref.shape
    width = columns if width is None else width
    return ref[:, :, :, pl.ds(first, width)].reshape(n_a * n_b * rows, width)


def row_loop(rows, chunk, body):
    @pl.loop(0, rows // chunk)
    def _(i):
        body(pl.ds(pl.multiple_of(i * chunk, chunk), chunk))


def norm_into(hidden, gain_row, target, hat, scales, first):
    def body(at):
        centre = hidden[at, :]
        centre = centre - jnp.mean(centre, axis=-1, keepdims=True)
        spread = jnp.mean(centre * centre, axis=-1, keepdims=True)
        scale = lax.rsqrt(spread + NORM_EPSILON)
        normal = centre * scale
        target[at, :] = (normal * gain_row).astype(BF16)
        hat[at, :] = normal.astype(BF16)
        scales[at, pl.ds(first, 64)] = jnp.broadcast_to(scale, (scale.shape[0], 64))

    row_loop(hidden.shape[0], 64, body)


GELU_SCALE = math.sqrt(2.0 / math.pi)


def gelu_and_slope(u):
    square = u * u
    bent = jnp.tanh(GELU_SCALE * (u + 0.044715 * (square * u)))
    half = 0.5 * (1.0 + bent)
    slope = half + (0.5 * GELU_SCALE) * u * (1.0 - bent * bent) * (1.0 + 0.134145 * square)
    return u * half, slope


def head_probs(queries, keys_all, distance, same, slope):
    scores = lax.dot_general(
        queries, keys_all, (((1,), (1,)), ((), ())), preferred_element_type=F32
    )
    scores = jnp.where(same, scores * HD ** (-0.5) - slope * distance, -1e30)
    weights = jnp.exp(scores - jnp.max(scores, axis=-1, keepdims=True))
    return weights / jnp.sum(weights, axis=-1, keepdims=True)


def pair_mask(rows):
    lane = lax.broadcasted_iota(jnp.int32, (rows, 2 * HD), 1)
    return lane < HD


def forward_kernel(dims, *refs):
    n_y, n_c, n_a, n_b = dims
    masters, payload, gains, pack_hot, cotangent, frame_weight, ids_down, ids_across, slopes = (
        refs[:5], *refs[5:13]
    )
    refs = refs[13:]
    fulls_out, refs = refs[:5], refs[5:]
    packed_out, qkv_out, mixed_out, slope_out, act_out, one_out, two_out = refs[:7]
    hat_one_out, hat_two_out, scales_out, low_out, low_far_out, act_far_out = refs[7:13]
    frames_out, gains_out = refs[13:15]
    refs = refs[15:]
    fulls, refs = refs[:5], refs[5:]
    stage, arrived, hot, gains_all, packed, base, one, qkv, mixed, after, two, up, out = refs[:13]
    hat_one, hat_two, scales, slope_buf = refs[13:17]
    send_sem, recv_sem, local_sem = refs[17:]
    dp, fsdp = lax.axis_index("dp"), lax.axis_index("fsdp")
    y, c, a, b = dp // n_c, lax.rem(dp, n_c), fsdp // n_b, lax.rem(fsdp, n_b)
    n_dp, n_fsdp = n_y * n_c, n_a * n_b
    copies = Copies(send_sem, recv_sem, local_sem)
    remote, local = copies.remote, copies.local
    greet(dims, dp, fsdp)
    micro = payload.shape[0]
    slots = payload.shape[2]

    staged = {}

    def load(m):
        rows, columns = masters[m].shape
        view = stage.at[m % 2, pl.ds(0, rows * columns // 1024)]
        if columns == 1024:
            staged[m] = [local(masters[m], view)]
        else:
            parts = columns // 1024
            staged[m] = [
                local(
                    masters[m].at[:, pl.ds(p * 1024, 1024)],
                    stage.at[m % 2, pl.ds(p * rows, rows)],
                )
                for p in range(parts)
            ]

    load(0)
    load(1)
    frames = []
    slab = n_dp * slots

    def slot(group):
        return pl.ds(pl.multiple_of(group * slots, 16), slots)

    gain_copies = []
    own_gains = local(gains, gains_all.at[fsdp])
    cot_copy = local(cotangent, out)
    hot_copy = local(pack_hot, hot)
    for k in range(1, n_dp):
        to, back = turn(dp, k, n_dp), turn(dp, -k, n_dp)
        for i in range(micro):
            frames.append(
                remote(
                    payload.at[i, to], arrived.at[i, slot(dp)], arrived.at[i, slot(back)], (to, fsdp)
                )
            )
    own_frames = [local(payload.at[i, dp], arrived.at[i, slot(dp)]) for i in range(micro)]

    units = []
    for m, part, parts, shared in GATHER_UNITS:
        width = masters[m].shape[1] // parts
        units.append((m, part * width, width, shared and width // (n_c * n_y) % 128 == 0))
    state = [{"x": [], "y": [], "c": []} for _ in units]

    def columns(u, of_c, of_y):
        m, first, width, shared = units[u]
        if shared:
            step = width // (n_c * n_y)
            return pl.ds(pl.multiple_of(first + (of_c * n_y + of_y) * step, 128), step)
        step = width // n_c
        return pl.ds(pl.multiple_of(first + of_c * step, 128), step)

    def convert(m):
        for copy in staged[m]:
            copy.wait()
        rows, width = masters[m].shape

        def body(at):
            for p in range(width // 1024):
                low = stage[m % 2, pl.ds(at.start + p * rows, at.size), :].astype(BF16)
                fulls[m][a, b, at, pl.ds(p * 1024, 1024)] = low

        row_loop(rows, 32, body)

    def pass_on(u, name, block, mask):
        full, cols = fulls[units[u][0]], columns(u, c, y)
        view, source = full.at[block, b, :, cols], block ^ mask
        landing = full.at[source, b, :, cols]
        copy = remote(view, view, landing, (dp, (a ^ mask) * n_b + b))
        state[u][name] = (copy, source)

    def stage_z(u):
        pass_on(u, "far", a, 2)
        pass_on(u, "near", a, 1)

    def spread(u, block_a, block_b, of_y, to_y):
        m, first, width, shared = units[u]
        full = fulls[m]
        view = full.at[block_a, block_b, :, columns(u, c, of_y)]
        if to_y and shared:
            for k in range(1, n_y):
                source = turn(y, -k, n_y)
                landing = full.at[block_a, block_b, :, columns(u, c, source)]
                copy = remote(view, view, landing, (turn(y, k, n_y) * n_c + c, fsdp))
                state[u]["y"].append((copy, block_a, block_b, source))
        landing = full.at[block_a, block_b, :, columns(u, 1 - c, of_y)]
        state[u]["c"].append(remote(view, view, landing, (y * n_c + 1 - c, fsdp)))

    def send_x(u, block_a):
        m = units[u][0]
        cols = columns(u, c, y)
        view = fulls[m].at[block_a, b, :, cols]
        for k in range(1, n_b):
            landing = fulls[m].at[block_a, turn(b, -k, n_b), :, cols]
            state[u]["x"].append(remote(view, view, landing, (dp, a * n_b + turn(b, k, n_b))))

    def stage_own(u):
        send_x(u, a)

    def relay(u, name):
        copy, source = state[u][name]
        copy.wait_recv()
        if name == "far":
            pass_on(u, "last", source, 1)
        send_x(u, source)
        spread(u, source, b, y, True)

    def relay_own(u):
        relay(u, "far")
        relay(u, "near")

    def stage_x(u):
        relay_own(u)
        relay(u, "last")

    def stage_s(u):
        for copy in state[u]["x"]:
            copy.wait_recv()
        for k in range(1, n_b):
            spread(u, slice(None), turn(b, -k, n_b), y, True)

    def stage_c(u):
        for copy, block_a, block_b, source in state[u]["y"]:
            copy.wait_recv()
            spread(u, block_a, block_b, source, False)

    outgoing = []

    def finish(u):
        m, first, width, shared = units[u]
        for copy in state[u]["c"]:
            copy.wait_recv()
        cols = pl.ds(first, width)
        outgoing.append(local(fulls[m].at[:, :, :, cols], fulls_out[m].at[:, :, :, cols]))

    for m in range(5):
        convert(m)
        if m + 2 < 5:
            load(m + 2)
        for u in range(len(units)):
            if units[u][0] == m and u < WINDOW:
                stage_z(u)
            if units[u][0] == m and u < OWN_FIRST:
                stage_own(u)
        if m == 0:
            for k in range(1, n_fsdp):
                to, back = turn(fsdp, k, n_fsdp), turn(fsdp, -k, n_fsdp)
                gain_copies.append(
                    remote(gains, gains_all.at[fsdp], gains_all.at[back], (dp, to))
                )

    count = len(units)

    def comm(u):
        if u < count:
            stage_x(u)
        if u + WINDOW < count:
            stage_z(u + WINDOW)
        if OWN_FIRST <= u + WINDOW < count:
            stage_own(u + WINDOW)
        if u == 6 and WINDOW == 3:
            stage_z(10)
            stage_own(10)
        if u >= 1:
            stage_s(u - 1)

    tokens, width = base.shape
    per_pack = tokens // micro

    def make_packed():
        for copy in frames:
            copy.wait_recv()
        for copy in own_frames:
            copy.wait()
        hot_copy.wait()
        for i in range(micro):
            for half in range(2):
                cols = pl.ds(half * 1024, 1024)
                packed[pl.ds(i * per_pack, per_pack), cols] = jnp.dot(
                    hot[i], arrived[i, :, cols], preferred_element_type=F32
                ).astype(BF16)
        outgoing.append(local(packed, packed_out))

    gain_rows = []

    def make_gains():
        for copy in gain_copies:
            copy.wait_recv()
        own_gains.wait()
        outgoing.append(local(gains_all, gains_out))
        own = D // n_fsdp
        for row in range(2):
            gain_rows.append(
                jnp.concatenate([gains_all[f, pl.ds(row, 1), pl.ds(0, own)] for f in range(n_fsdp)], axis=1)
            )

    def make_base():
        for first in (0, 512):
            base[:, pl.ds(first, 512)] = jnp.dot(
                packed[...], whole(fulls[0], first, 512), preferred_element_type=F32
            )
        norm_into(base, gain_rows[0], one, hat_one, scales, 0)
        outgoing.append(local(hat_one, hat_one_out))
        outgoing.append(local(one, one_out))

    def make_qkv():
        for first in range(0, 3 * D, 512):
            qkv[:, pl.ds(first, 512)] = jnp.dot(
                one[...], whole(fulls[1], first, 512), preferred_element_type=F32
            ).astype(BF16)
        outgoing.append(local(qkv, qkv_out))

    def attend(i, first=0, last=HEADS // 2):
        rows = pl.ds(i * per_pack, per_pack)
        position = lax.broadcasted_iota(jnp.int32, (per_pack, per_pack), 0)
        distance = jnp.abs(
            position - lax.broadcasted_iota(jnp.int32, (per_pack, per_pack), 1)
        ).astype(F32)
        first_head = pair_mask(per_pack)

        @pl.loop(first, last)
        def _(pair):
            def cols(part):
                return pl.ds(pl.multiple_of(part * D + pair * 2 * HD, 128), 2 * HD)

            same = ids_down[i] == ids_across[i]
            queries, keys_all, values_all = (qkv[rows, cols(part)] for part in range(3))
            results = []
            for head in range(2):
                mine = first_head if head == 0 else jnp.logical_not(first_head)
                slope = slopes[pl.ds(2 * pair + head, 1), :]
                probs = head_probs(
                    jnp.where(mine, queries, jnp.zeros_like(queries)), keys_all, distance, same, slope
                )
                results.append(
                    jnp.dot(probs.astype(BF16), values_all, preferred_element_type=F32)
                )
            mixed[rows, cols(0)] = jnp.where(first_head, results[0], results[1]).astype(BF16)

    def make_after():
        outgoing.append(local(mixed, mixed_out))
        for first in (0, 512):
            cols = pl.ds(first, 512)
            after[:, cols] = base[:, cols] + jnp.dot(
                mixed[...], whole(fulls[2], first, 512), preferred_element_type=F32
            )
        norm_into(after, gain_rows[1], two, hat_two, scales, 64)
        outgoing.append(local(hat_two, hat_two_out))
        outgoing.append(local(scales, scales_out))
        outgoing.append(local(two, two_out))

    slope_copies = [None, None]
    half_ff = FF // 2

    def make_up(j):
        slot_now = j % 2
        cols = pl.ds(j * 512, 512)
        up[...] = jnp.dot(two[...], whole(fulls[3], j * 512, 512), preferred_element_type=F32)
        if slope_copies[slot_now] is not None:
            slope_copies[slot_now].wait()
        half, within = j * 512 // half_ff, j * 512 % half_ff

        def body(at):
            value, slope = gelu_and_slope(up[at, :])
            arrived[half, at, pl.ds(within, 512)] = value.astype(BF16)
            slope_buf[slot_now, at, :] = slope.astype(BF16)

        row_loop(tokens, 64, body)
        slope_copies[slot_now] = local(slope_buf.at[slot_now], slope_out.at[:, cols])

    other_core = (y * n_c + 1 - c, fsdp)
    crossing = []

    def send_act(half):
        cols = pl.ds(half * half_ff, half_ff)
        outgoing.append(local(arrived.at[half], act_out.at[:, cols]))
        there = act_far_out.at[:, cols]
        crossing.append(remote(arrived.at[half], there, there, other_core))

    low_copies = []

    def make_low():
        cot_copy.wait()

        def body(at):
            out[at, :] = (frame_weight[at, :] * out[at, :].astype(F32)).astype(BF16)

        row_loop(tokens, 64, body)
        low_copies.append(local(out, low_out))
        step = D // n_c
        others = pl.ds(pl.multiple_of((1 - c) * step, 128), step)
        crossing.append(remote(out.at[:, others], low_far_out, low_far_out, other_core))

    def low_left():
        low_copies[0].wait()
        crossing[0].wait_send()

    def make_out(first, step):
        cols = pl.ds(first, step)
        weight = whole(fulls[4], first, step)
        total = after[:, cols] + jnp.dot(
            arrived[0], weight[:half_ff], preferred_element_type=F32
        )
        total += jnp.dot(arrived[1], weight[half_ff:], preferred_element_type=F32)
        out[:, cols] = total.astype(BF16)

    comm(0)
    comm(1)
    comm(2)
    make_gains()
    make_low()
    comm(3)
    make_packed()
    finish(0)
    finish(1)
    make_base()
    comm(4)
    comm(5)
    comm(6)
    stage_c(2)
    relay_own(7)
    stage_c(3)
    finish(2)
    finish(3)
    make_qkv()
    attend(0, 0, 4)
    relay(7, "last")
    relay_own(8)
    stage_s(6)
    attend(0, 4, 8)
    relay(8, "last")
    relay_own(9)
    attend(1, 0, 4)
    relay(9, "last")
    relay_own(10)
    stage_s(7)
    stage_c(5)
    attend(1, 4, 8)
    relay(10, "last")
    finish(4)
    stage_s(8)
    make_after()
    finish(5)
    for j in range(4):
        make_up(j)
    send_act(0)
    stage_c(6)
    stage_s(9)
    low_left()
    finish(6)
    for j in range(4, 8):
        make_up(j)
    send_act(1)
    finish(7)
    make_out(0, 256)
    stage_s(10)
    finish(8)
    make_out(256, 256)
    finish(9)
    make_out(512, 256)
    finish(10)
    make_out(768, 256)
    outgoing.append(local(out, frames_out))
    for copy in crossing:
        copy.wait_recv()
    for copy in outgoing + slope_copies:
        copy.wait()
    for copy in copies.sent:
        copy.wait_send()


def forward_all(masters, payload, gains, pack_hot, cotangent, frame_weight, source):
    dims = sizes()
    n_y, n_c, n_a, n_b = dims
    n_fsdp = n_a * n_b
    micro, n_dp, slots, _ = payload.shape
    per_pack = source.shape[1]
    tokens = micro * per_pack
    total = micro * (n_y * n_c - 1) + n_fsdp - 1 + 3
    for _, _, _, shared in GATHER_UNITS:
        groups = n_a - 1 + n_b - 1
        total += (n_a - 1) + n_a * (n_b - 1)
        total += (n_y - 1) * groups + n_y * groups if shared else groups
    shape = jax.ShapeDtypeStruct
    full_shapes = [(n_a, n_b) + master.shape for master in masters]
    out_shape = [shape(s, BF16) for s in full_shapes]
    out_shape += [
        shape((tokens, 2 * D), BF16), shape((tokens, 3 * D), BF16), shape((tokens, D), BF16),
        shape((tokens, FF), BF16), shape((tokens, FF), BF16),
        shape((tokens, D), BF16), shape((tokens, D), BF16),
        shape((tokens, D), BF16), shape((tokens, D), BF16),
        shape((tokens, 128), F32),
        shape((tokens, D), BF16), shape((tokens, D // n_c), BF16), shape((tokens, FF), BF16),
        shape((tokens, D), BF16), shape((n_fsdp,) + gains.shape, F32),
    ]
    anywhere = pl.BlockSpec(memory_space=pl.ANY)
    inside = pl.BlockSpec(memory_space=pltpu.VMEM)
    slopes = jnp.exp2(-8.0 * (jnp.arange(HEADS, dtype=F32) + 1.0) / HEADS)
    slopes = jnp.broadcast_to(slopes[:, None], (HEADS, per_pack))
    stage_rows = max(m.shape[0] * m.shape[1] // 1024 for m in masters)
    results = pl.pallas_call(
        partial(forward_kernel, dims),
        out_shape=out_shape,
        in_specs=[anywhere] * 9 + [inside] * 4,
        out_specs=[anywhere] * len(out_shape),
        scratch_shapes=[pltpu.VMEM(s, BF16) for s in full_shapes]
        + [
            pltpu.VMEM((2, stage_rows, 1024), F32),
            pltpu.VMEM((micro, n_dp * slots, 2 * D), BF16),
            pltpu.VMEM((micro, per_pack, n_dp * slots), BF16),
            pltpu.VMEM((n_fsdp,) + gains.shape, F32),
            pltpu.VMEM((tokens, 2 * D), BF16),
            pltpu.VMEM((tokens, D), F32),
            pltpu.VMEM((tokens, D), BF16),
            pltpu.VMEM((tokens, 3 * D), BF16),
            pltpu.VMEM((tokens, D), BF16),
            pltpu.VMEM((tokens, D), F32),
            pltpu.VMEM((tokens, D), BF16),
            pltpu.VMEM((tokens, 512), F32),
            pltpu.VMEM((tokens, D), BF16),
            pltpu.VMEM((tokens, D), BF16),
            pltpu.VMEM((tokens, D), BF16),
            pltpu.VMEM((tokens, 128), F32),
            pltpu.VMEM((2, tokens, 512), BF16),
            pltpu.SemaphoreType.DMA((total,)),
            pltpu.SemaphoreType.DMA((total,)),
            pltpu.SemaphoreType.DMA((64,)),
        ],
        compiler_params=pltpu.CompilerParams(
            collective_id=0, has_side_effects=True, vmem_limit_bytes=VMEM_LIMIT
        ),
        name="gather_and_forward",
    )(
        *masters, payload, gains, pack_hot, cotangent, frame_weight,
        source[:, :, None], source[:, None, :], slopes,
    )
    return results


def norm_back(hat, scale, gain_row, gradient):
    scaled = gradient * gain_row
    back = scale * (
        scaled
        - jnp.mean(scaled, axis=-1, keepdims=True)
        - hat * jnp.mean(scaled * hat, axis=-1, keepdims=True)
    )
    return back, jnp.sum(gradient * hat, axis=0, keepdims=True)


RING = 4


def backward_kernel(dims, shapes, *refs):
    n_y, n_c, n_a, n_b = dims
    fulls, refs = refs[:5], refs[5:]
    (packed, qkv, mixed, slope, act, one, two, hat_one, hat_two, scales, low_in, low_far_in, act_far,
     cotangent, frame_weight, gains_all, back_hot, ids_down, ids_across, slopes) = refs[:20]
    refs = refs[20:]
    outs, returned, small_out, refs = refs[:5], refs[5], refs[6], refs[7:]
    sums, finals, refs = refs[:5], refs[5:10], refs[10:]
    (pool, low_far, wide, wide_far, left_far, ring, slope_buf, acc, hidden,
     cot, low, hat, gain_buf, gain_land, small, small_total) = refs[:16]
    refs = refs[16:]
    landing, refs = refs[: 3 * len(REDUCE_UNITS)], refs[3 * len(REDUCE_UNITS) :]
    send_sem, recv_sem, local_sem, credit = refs
    dp, fsdp = lax.axis_index("dp"), lax.axis_index("fsdp")
    y, c, a, b = dp // n_c, lax.rem(dp, n_c), fsdp // n_b, lax.rem(fsdp, n_b)
    n_dp, n_fsdp = n_y * n_c, n_a * n_b
    other_core = (y * n_c + 1 - c, fsdp)
    copies = Copies(send_sem, recv_sem, local_sem)
    remote, local = copies.remote, copies.local
    greet(dims, dp, fsdp)
    tokens = cot.shape[0]
    micro = ids_down.shape[0]
    per_pack = tokens // micro
    near, far = pl.ds(0, tokens), pl.ds(tokens, tokens)

    order = []
    for block in range(4):
        order += [(4, block * 1024, 0), (4, block * 1024, 512)]
        order += [(3, 0, block * 1024), (3, 0, block * 1024 + 512)]
    order += [(2, 0, 0), (2, 0, 512)]
    order += [(1, 0, first) for first in range(0, 3 * D, 512)]
    order += [(0, first, second) for first in (0, 1024) for second in (0, 512)]
    ring_copies = {}
    ring_state = [0, 0]

    def ring_load():
        index = ring_state[0]
        if index < len(order):
            m, first, second = order[index]
            ring_copies[index] = local(
                fulls[m].at[pl.ds(first, 1024), pl.ds(second, 512)], ring.at[index % RING]
            )
            ring_state[0] += 1

    def ring_next():
        index = ring_state[1]
        ring_state[1] += 1
        ring_copies.pop(index).wait()
        return ring.at[index % RING]

    def far_half(width):
        return pl.ds(pl.multiple_of((1 - c) * width, 128), width)

    half_ff = FF // 2
    low_copies = [local(low_in, low), local(low_far_in, low_far)]
    act_copies = []
    for half in range(2):
        cols = pl.ds(half * half_ff, half_ff)
        act_copies.append(local(act.at[:, cols], pool.at[half, near]))
        act_copies.append(local(act_far.at[:, cols], pool.at[half, far]))
    for _ in range(RING):
        ring_load()
    slope_copies = {}

    def slope_load(j):
        slope_copies[j] = local(slope.at[:, pl.ds(j * 512, 512)], slope_buf.at[j % 2])

    slope_load(0)
    slope_load(1)
    cot_copy = local(cotangent, cot)
    hat_copy = local(hat_two, hat)
    two_away = remote(two, left_far, left_far, other_core)

    units = []
    for m, part, parts, shared in REDUCE_UNITS:
        width = shapes[m][1] // n_c // parts
        units.append((m, part * width, width, shared))
    state = [{} for _ in units]

    def piece(unit, of_y):
        m, first, width, shared = unit
        if shared:
            step = width // n_y
            return pl.ds(pl.multiple_of(first + of_y * step, 128), step), step
        return pl.ds(first, width), width

    def product(u, left_near, left_other, right_near, right_far):
        m, first, width, shared = units[u]
        rows = sums[m].shape[2]
        group = max(1, 512 // (n_b * rows))
        tile = group * n_b * rows
        half = shapes[m][1] // n_c
        mine = pl.ds(pl.multiple_of(c * half + first, 128), width)

        @pl.loop(0, n_a // group)
        def _(i):
            contract = (((0,), (0,)), ((), ()))
            value = lax.dot_general(
                left_near(i, tile), right_near[:, mine], contract, preferred_element_type=F32
            )
            value += lax.dot_general(
                left_other(i, tile), right_far[:, pl.ds(first, width)], contract,
                preferred_element_type=F32,
            )
            sums[m][pl.ds(i * group, group), :, :, pl.ds(first, width)] = value.astype(BF16).reshape(
                group, n_b, rows, width
            )

    def tiles(ref, rows, first):
        def pick_tile(i, tile):
            return ref[rows, pl.ds(pl.multiple_of(first + i * tile, 128), tile)]

        return pick_tile

    def pool_tiles(rows):
        def pick_tile(i, tile):
            per = half_ff // tile
            return pool[i // per, rows, pl.ds(pl.multiple_of(lax.rem(i, per) * tile, 128), tile)]

        return pick_tile

    def chunks(outer, rows, body):
        chunk = min(64, rows)
        per = rows // chunk

        @pl.loop(0, outer * per)
        def _(i):
            body(i // per, pl.ds(pl.multiple_of(lax.rem(i, per) * chunk, 16), chunk))


    def y_send(u):
        m, first, width, shared = units[u]
        for k in range(1, n_y):
            cols, step = piece(units[u], turn(y, k, n_y))
            there = landing[3 * u].at[k - 1]
            state[u].setdefault("y", []).append(
                remote(sums[m].at[:, :, :, cols], there, there, (turn(y, k, n_y) * n_c + c, fsdp))
            )

    def y_add(u):
        m = units[u][0]
        for copy in state[u]["y"]:
            copy.wait_recv()
        cols, step = piece(units[u], y)

        def body(outer, rows):
            at = (outer // n_b, lax.rem(outer, n_b), rows, cols)
            value = sums[m][at].astype(F32)
            for k in range(1, n_y):
                value += landing[3 * u][k - 1, outer // n_b, lax.rem(outer, n_b), rows, :].astype(F32)
            sums[m][at] = value.astype(BF16)

        chunks(n_a * n_b, sums[m].shape[2], body)

    def x_land(u):
        return landing[3 * u + 1] if units[u][3] else landing[3 * u]

    def z_land(u):
        return landing[3 * u + 2] if units[u][3] else landing[3 * u + 1]

    def x_send(u):
        m = units[u][0]
        cols, step = piece(units[u], y)
        state[u]["x"] = []
        for k in range(1, n_b):
            there = x_land(u).at[k - 1]
            to = turn(b, k, n_b)
            state[u]["x"].append(
                remote(sums[m].at[:, to, :, cols], there, there, (dp, a * n_b + to))
            )

    def x_add(u):
        m = units[u][0]
        for copy in state[u]["x"]:
            copy.wait_recv()
        cols, step = piece(units[u], y)

        def body(outer, rows):
            value = sums[m][outer, b, rows, cols].astype(F32)
            for k in range(1, n_b):
                value += x_land(u)[k - 1, outer, rows, :].astype(F32)
            sums[m][outer, b, rows, cols] = value.astype(BF16)

        chunks(n_a, sums[m].shape[2], body)

    def z_send(u):
        m = units[u][0]
        cols, step = piece(units[u], y)
        device = (dp, (a ^ 1) * n_b + b)
        state[u]["z"] = []
        for slot_at, block in ((0, a ^ 1), (1, a ^ 3)):
            there = z_land(u).at[slot_at]
            state[u]["z"].append(remote(sums[m].at[block, b, :, cols], there, there, device))

    def zz(u):
        m = units[u][0]
        for copy in state[u]["z"]:
            copy.wait_recv()
        cols, step = piece(units[u], y)

        def body(outer, rows):
            block = a ^ (2 * outer)
            value = sums[m][block, b, rows, cols].astype(F32)
            value += z_land(u)[outer, rows, :].astype(F32)
            sums[m][block, b, rows, cols] = value.astype(BF16)

        chunks(2, sums[m].shape[2], body)
        there = z_land(u).at[2]
        device = (dp, (a ^ 2) * n_b + b)
        state[u]["w"] = remote(sums[m].at[a ^ 2, b, :, cols], there, there, device)

    def z_add(u):
        m, first, width, shared = units[u]
        state[u]["w"].wait_recv()
        cols, step = piece(units[u], y)
        half = shapes[m][1] // n_c

        def body(outer, rows):
            value = sums[m][a, b, rows, cols].astype(F32) + z_land(u)[2, rows, :].astype(F32)
            if shared:
                at = pl.ds(pl.multiple_of(c * half + first + y * step, 128), step)
                finals[m][rows, at] = value.astype(BF16)
            elif n_y == 2:
                sums[m][a, b, rows, cols] = value.astype(BF16)
            else:
                landing[3 * u + 2][y, rows, :] = value.astype(BF16)

        chunks(1, sums[m].shape[2], body)

    def last_send(u):
        m, first, width, shared = units[u]
        half = shapes[m][1] // n_c
        state[u]["last"] = []
        for k in range(1, n_y):
            device = (turn(y, k, n_y) * n_c + c, fsdp)
            from_y = turn(y, -k, n_y)
            if shared:
                step = width // n_y
                mine = pl.ds(pl.multiple_of(c * half + first + y * step, 128), step)
                theirs = pl.ds(pl.multiple_of(c * half + first + from_y * step, 128), step)
                view = finals[m].at[:, mine]
                state[u]["last"].append(remote(view, view, finals[m].at[:, theirs], device))
            elif n_y == 2:
                view, there = sums[m].at[a, b, :, piece(units[u], y)[0]], landing[3 * u + 2].at[0]
                state[u]["last"].append(remote(view, there, there, device))
            else:
                view = landing[3 * u + 2].at[y]
                state[u]["last"].append(remote(view, view, landing[3 * u + 2].at[from_y], device))

    def last_add(u):
        m, first, width, shared = units[u]
        half = shapes[m][1] // n_c
        for copy in state[u]["last"]:
            copy.wait_recv()
        at = pl.ds(pl.multiple_of(c * half + first, 128), width)
        if not shared:

            def body(outer, rows):
                value = landing[3 * u + 2][0, rows, :].astype(F32)
                if n_y == 2:
                    value += sums[m][a, b, rows, pl.ds(first, width)].astype(F32)
                for k in range(1, n_y if n_y > 2 else 0):
                    value += landing[3 * u + 2][k, rows, :].astype(F32)
                finals[m][rows, at] = value.astype(BF16)

            chunks(1, sums[m].shape[2], body)
        view = finals[m].at[:, at]
        theirs = pl.ds(pl.multiple_of((1 - c) * half + first, 128), width)
        state[u]["core"] = remote(view, view, finals[m].at[:, theirs], other_core)

    def xz(u):
        x_add(u)
        z_send(u)

    def yx(u):
        y_add(u)
        x_send(u)

    def zl(u):
        z_add(u)
        last_send(u)


    masks = [1 << i for i in range(n_y.bit_length() - 1)]
    dp_partners = [other_core] + [((y ^ mask) * n_c + c, fsdp) for mask in masks]
    gain_copies = {}

    def gain_step(step):
        if step > 0:
            gain_copies[step - 1].wait_recv()
            gain_buf[step] = gain_buf[step - 1] + gain_land[step - 1]
        if step < len(dp_partners):
            there = gain_land.at[step]
            gain_copies[step] = remote(gain_buf.at[step], there, there, dp_partners[step])

    def add_gain(row, value):
        for part in range(4):
            gain_buf[0, pl.ds(4 * row + part, 1), :] += value[:, part * 256 : part * 256 + 256]

    def give_credit(index):
        pl.semaphore_signal(credit.at[index], inc=1, device_id=other_core, device_id_type=MESH)


    own = D // n_fsdp

    def gain_row(row):
        return jnp.concatenate(
            [gains_all[f, pl.ds(row, 1), pl.ds(0, own)] for f in range(n_fsdp)], axis=1
        )

    def dot_right(left, right):
        return lax.dot_general(left, right, (((1,), (1,)), ((), ())), preferred_element_type=F32)

    def add_product(left, weight, first):
        for start in (0, 512):
            cols = pl.ds(start, 512)
            value = dot_right(left, weight[cols, :])
            acc[:, cols] = value if first else acc[:, cols] + value

    def feed_forward(block):
        down = (ring_next(), ring_next())
        for part in range(2):
            j = 2 * block + part
            slope_copies[j].wait()
            rows = pl.ds(part * 512, 512)
            d_act = dot_right(low[:, :512], down[0][rows, :])
            d_act += dot_right(low[:, 512:], down[1][rows, :])
            wide[:, pl.ds(j * 512, 512)] = (d_act * slope_buf[j % 2].astype(F32)).astype(BF16)
            if j + 2 < 8:
                slope_load(j + 2)
        ring_load()
        ring_load()
        for part in range(2):
            j = 2 * block + part
            add_product(wide[:, pl.ds(j * 512, 512)], ring_next(), j == 0)
            ring_load()

    for copy in low_copies + act_copies:
        copy.wait()
    for u in (0, 1):
        product(u, pool_tiles(near), pool_tiles(far), low, low_far)
        x_send(u)
    give_credit(0)
    left_here = [
        local(two, pool.at[0, near, pl.ds(0, D)]),
        local(one, pool.at[0, near, pl.ds(D, D)]),
    ]
    qkv_here = [
        local(qkv.at[:, pl.ds(0, D)], pool.at[1, near, pl.ds(0, D)]),
        local(qkv.at[:, pl.ds(D, D)], pool.at[1, near, pl.ds(D, D)]),
        local(qkv.at[:, pl.ds(2 * D, D)], pool.at[1, far, pl.ds(0, D)]),
        local(mixed, pool.at[1, far, pl.ds(D, D)]),
    ]
    for block in range(4):
        feed_forward(block)
    pl.semaphore_wait(credit.at[0], 1)
    there = pool.at[0, far, pl.ds(0, D)]
    mixed_away = remote(mixed, there, there, other_core)
    wide_away = remote(wide.at[:, far_half(half_ff)], wide_far, wide_far, other_core)
    hat_copy.wait()
    cot_copy.wait()
    gain_buf[0] = jnp.zeros_like(gain_buf[0])
    gain_two = gain_row(1)

    def after_body(at):
        back, grad_gain = norm_back(
            hat[at, :].astype(F32), scales[at, pl.ds(64, 1)], gain_two, acc[at, :]
        )
        d_after = frame_weight[at, :] * cot[at, :].astype(F32) + back
        hidden[at, :] = d_after
        low[at, :] = d_after.astype(BF16)
        add_gain(1, grad_gain)

    row_loop(tokens, 64, after_body)
    after_away = remote(low.at[:, far_half(D // n_c)], low_far, low_far, other_core)
    hat_copy = local(hat_one, hat)
    pair = (ring_next(), ring_next())
    for start in (0, 512):
        cols = pl.ds(start, 512)
        value = dot_right(low[:, :512], pair[0][cols, :]) + dot_right(low[:, 512:], pair[1][cols, :])
        cot[:, cols] = value.astype(BF16)
    ring_load()
    ring_load()
    for copy in left_here + qkv_here:
        copy.wait()
    two_away.wait_recv()
    wide_away.wait_recv()
    for u in (2, 3):
        product(u, tiles(pool.at[0], near, 0), tiles(left_far, near, 0), wide, wide_far)
        y_send(u)
    mixed_away.wait_recv()
    after_away.wait_recv()
    product(4, tiles(pool.at[1], far, D), tiles(pool.at[0], far, 0), low, low_far)
    give_credit(1)
    x_send(4)
    wide_away.wait_send()
    pl.semaphore_wait(credit.at[1], 1)
    packed_away = remote(packed, pool.at[0, far], pool.at[0, far], other_core)
    one_away = remote(one, left_far, left_far, other_core)

    def attend_back(i, first_pair=0, last_pair=HEADS // 2):
        rows = pl.ds(i * per_pack, per_pack)
        rows_far = pl.ds(tokens + i * per_pack, per_pack)
        position = lax.broadcasted_iota(jnp.int32, (per_pack, per_pack), 0)
        distance = jnp.abs(
            position - lax.broadcasted_iota(jnp.int32, (per_pack, per_pack), 1)
        ).astype(F32)
        first_head = pair_mask(per_pack)

        @pl.loop(first_pair, last_pair)
        def _(pair):
            def cols(first):
                return pl.ds(pl.multiple_of(first + pair * 2 * HD, 128), 2 * HD)

            same = ids_down[i] == ids_across[i]
            queries, keys_all = pool[1, rows, cols(0)], pool[1, rows, cols(D)]
            values_all = pool[1, rows_far, cols(0)]
            d_mixed = cot[rows, cols(0)]
            zero = jnp.zeros_like(queries)
            total = [None, None, None]
            for head in range(2):
                mine = first_head if head == 0 else jnp.logical_not(first_head)
                query, key, d_head = (
                    jnp.where(mine, value, zero) for value in (queries, keys_all, d_mixed)
                )
                probs = head_probs(
                    query, keys_all, distance, same, slopes[pl.ds(2 * pair + head, 1), :]
                )
                d_probs = dot_right(d_head, values_all)
                carried = jnp.sum(probs * d_probs, axis=-1, keepdims=True)
                d_scores = (probs * (d_probs - carried)).astype(BF16)
                contract = (((0,), (0,)), ((), ()))
                parts = (
                    jnp.dot(d_scores, key, preferred_element_type=F32),
                    lax.dot_general(d_scores, query, contract, preferred_element_type=F32),
                    lax.dot_general(
                        probs.astype(BF16), d_head, contract, preferred_element_type=F32
                    ),
                )
                total = [p if t is None else t + p for t, p in zip(total, parts)]
            wide[rows, cols(0)] = (total[0] * HD ** (-0.5)).astype(BF16)
            wide[rows, cols(D)] = (total[1] * HD ** (-0.5)).astype(BF16)
            wide[rows, cols(2 * D)] = total[2].astype(BF16)

    xz(0)
    attend_back(0)
    attend_back(1, 0, 4)
    zz(0)
    attend_back(1, 4, 8)
    qkv_half = 3 * D // n_c
    qkv_view = wide_far.at[:, pl.ds(0, qkv_half)]
    qkv_away = remote(wide.at[:, far_half(qkv_half)], qkv_view, qkv_view, other_core)
    for part in range(6):
        add_product(wide[:, pl.ds(part * 512, 512)], ring_next(), part == 0)
        ring_load()
    xz(1)
    yx(2)
    one_away.wait_recv()
    qkv_away.wait_recv()
    for u in (5, 6):
        product(u, tiles(pool.at[0], near, D), tiles(left_far, near, 0), wide, wide_far)
        x_send(u)
    packed_here = local(packed, pool.at[0, near])
    hat_copy.wait()
    after_away.wait_send()
    gain_one = gain_row(0)

    def base_body(at):
        back, grad_gain = norm_back(
            hat[at, :].astype(F32), scales[at, pl.ds(0, 1)], gain_one, acc[at, :]
        )
        low[at, :] = (hidden[at, :] + back).astype(BF16)
        add_gain(0, grad_gain)

    row_loop(tokens, 64, base_body)
    xz(4)
    zl(0)
    base_away = remote(low.at[:, far_half(D // n_c)], low_far, low_far, other_core)
    gain_step(0)
    qkv_away.wait_send()
    for half in range(2):
        pair = (ring_next(), ring_next())
        for start in (0, 512):
            cols = pl.ds(start, 512)
            value = dot_right(low[:, :512], pair[0][cols, :])
            value += dot_right(low[:, 512:], pair[1][cols, :])
            wide[:, pl.ds(half * 1024 + start, 512)] = value.astype(BF16)
        ring_load()
        ring_load()
    zz(1)
    packed_here.wait()
    packed_away.wait_recv()
    base_away.wait_recv()
    for u in (7, 8, 9, 10):
        product(u, tiles(pool.at[0], near, 0), tiles(pool.at[0], far, 0), low, low_far)
    zl(1)
    zz(4)
    xz(2)
    slots = back_hot.shape[1] // n_dp
    slab = n_dp * slots
    for i in range(micro):
        for half in range(2):
            cols = pl.ds(half * 1024, 1024)
            pool[1, pl.ds(i * slab, slab), cols] = jnp.dot(
                back_hot[i], wide[pl.ds(i * per_pack, per_pack), cols], preferred_element_type=F32
            ).astype(BF16)
    yx(3)
    for u in (7, 8, 9, 10):
        x_send(u)
    zl(4)
    gain_step(1)
    frames = []

    def slot(group, base=0):
        return pl.ds(pl.multiple_of(base + group * slots, 16), slots)

    for k in range(1, n_dp):
        to, back = turn(dp, k, n_dp), turn(dp, -k, n_dp)
        for i in range(micro):
            frames.append(
                remote(
                    pool.at[1, slot(to, i * slab)], returned.at[i, slot(dp)],
                    returned.at[i, slot(back)], (to, fsdp),
                )
            )
    own_frames = [local(pool.at[1, slot(dp, i * slab)], returned.at[i, slot(dp)]) for i in range(micro)]
    steps = [
        (zz, 2), (xz, 5), (zl, 2), (zz, 5), (last_add, 0), (xz, 6), (zl, 5), (last_add, 1),
        (zz, 6), (xz, 3), (zl, 6), (xz, 7), (zz, 3), (xz, 8), (zz, 7), (zl, 3), (last_add, 4),
        (xz, 9), (zl, 7), (zz, 8), (xz, 10), (zl, 8), (zz, 9), (zl, 9), (zz, 10), (last_add, 2),
        (last_add, 5), (zl, 10), (last_add, 6), (last_add, 3), (last_add, 7), (last_add, 8),
        (last_add, 9), (last_add, 10),
    ]
    for index, (do, u) in enumerate(steps):
        do(u)
        if index > 14 and index % 4 == 0 and index // 4 - 2 <= len(dp_partners):
            gain_step(index // 4 - 2)
    outgoing = []
    small[fsdp, :, pl.ds(256, 128)] = jnp.zeros((8, 128), F32)
    small[fsdp, :, pl.ds(0, 256)] = gain_buf[len(dp_partners)]

    def add_squares(m):
        rows, columns = finals[m].shape
        chunk = min(32, rows)

        @pl.loop(0, rows // chunk)
        def _(i):
            at = pl.ds(pl.multiple_of(i * chunk, chunk), chunk)
            for first in range(0, columns, 1024):
                value = finals[m][at, pl.ds(first, 1024)].astype(F32)
                value = (value * value).reshape(chunk // 8, 8, 8, 128)
                small[fsdp, :, pl.ds(256, 128)] += jnp.sum(value, axis=(0, 2))

    for m in (4, 3, 2, 1, 0):
        for u in range(len(units)):
            if units[u][0] == m:
                state[u]["core"].wait_recv()
        outgoing.append(local(finals[m], outs[m]))
        add_squares(m)
    view = small.at[fsdp]
    tail = []
    for k in range(1, n_fsdp):
        to, back = turn(fsdp, k, n_fsdp), turn(fsdp, -k, n_fsdp)
        tail.append(remote(view, view, small.at[back], (dp, to)))
    for copy in tail:
        copy.wait_recv()
    total = small[0]
    for f in range(1, n_fsdp):
        total = total + small[f]
    small_total[...] = total
    outgoing.append(local(small_total, small_out))
    for copy in frames:
        copy.wait_recv()
    for copy in own_frames + outgoing:
        copy.wait()
    for copy in copies.sent:
        copy.wait_send()


def backward_all(fulls, saved, cotangent, frame_weight, gains_all, back_hot, source):
    dims = sizes()
    n_y, n_c, n_a, n_b = dims
    n_fsdp = n_a * n_b
    tokens = cotangent.shape[0]
    micro, slab, per_pack = back_hot.shape
    shapes = [full.shape for full in fulls]
    shape = jax.ShapeDtypeStruct
    anywhere = pl.BlockSpec(memory_space=pl.ANY)
    inside = pl.BlockSpec(memory_space=pltpu.VMEM)
    steps = (n_y * n_c).bit_length() - 1
    scratch = [pltpu.VMEM((n_a, n_b, r // n_fsdp, w // n_c), BF16) for r, w in shapes]
    scratch += [pltpu.VMEM((r // n_fsdp, w), BF16) for r, w in shapes]
    scratch += [
        pltpu.VMEM((2, 2 * tokens, FF // 2), BF16),
        pltpu.VMEM((tokens, D // n_c), BF16),
        pltpu.VMEM((tokens, FF), BF16),
        pltpu.VMEM((tokens, FF // n_c), BF16),
        pltpu.VMEM((tokens, D), BF16),
        pltpu.VMEM((RING, 1024, 512), BF16),
        pltpu.VMEM((2, tokens, 512), BF16),
        pltpu.VMEM((tokens, D), F32),
        pltpu.VMEM((tokens, D), F32),
        pltpu.VMEM((tokens, D), BF16),
        pltpu.VMEM((tokens, D), BF16),
        pltpu.VMEM((tokens, D), BF16),
        pltpu.VMEM((steps + 1, 8, 256), F32),
        pltpu.VMEM((steps, 8, 256), F32),
        pltpu.VMEM((n_fsdp, 8, 384), F32),
        pltpu.VMEM((8, 384), F32),
    ]
    for m, part, parts, shared in REDUCE_UNITS:
        rows, width = shapes[m][0] // n_fsdp, shapes[m][1] // n_c // parts
        if shared:
            step = width // n_y
            scratch += [
                pltpu.VMEM((n_y - 1, n_a, n_b, rows, step), BF16),
                pltpu.VMEM((n_b - 1, n_a, rows, step), BF16),
                pltpu.VMEM((3, rows, step), BF16),
            ]
        else:
            scratch += [
                pltpu.VMEM((n_b - 1, n_a, rows, width), BF16),
                pltpu.VMEM((3, rows, width), BF16),
                pltpu.VMEM((1 if n_y == 2 else n_y, rows, width), BF16),
            ]
    total = 10 + micro * (n_y * n_c - 1) + steps + n_fsdp - 1
    for _, _, _, shared in REDUCE_UNITS:
        total += (n_b - 1) + (n_a - 1) + (n_y - 1) + 1 + (n_y - 1 if shared else 0)
    scratch += [
        pltpu.SemaphoreType.DMA((total,)),
        pltpu.SemaphoreType.DMA((total,)),
        pltpu.SemaphoreType.DMA((72,)),
        pltpu.SemaphoreType.REGULAR((2,)),
    ]
    out_shape = [shape((r // n_fsdp, w), BF16) for r, w in shapes]
    out_shape += [
        shape((micro, slab, 2 * D), BF16), shape((8, 384), F32),
    ]
    slopes = jnp.exp2(-8.0 * (jnp.arange(HEADS, dtype=F32) + 1.0) / HEADS)
    slopes = jnp.broadcast_to(slopes[:, None], (HEADS, per_pack))
    results = pl.pallas_call(
        partial(backward_kernel, dims, shapes),
        out_shape=out_shape,
        in_specs=[anywhere] * 14 + [inside] + [anywhere] * 4 + [inside] * 6,
        out_specs=[anywhere] * len(out_shape),
        scratch_shapes=scratch,
        compiler_params=pltpu.CompilerParams(
            collective_id=1, has_side_effects=True, vmem_limit_bytes=VMEM_LIMIT
        ),
        name="backward_and_reduce",
    )(
        *fulls, *saved, cotangent, frame_weight, gains_all, back_hot,
        source[:, :, None], source[:, None, :], slopes,
    )
    return results


def pick(value, index, axis):
    return lax.dynamic_index_in_dim(value, index, axis, keepdims=False)


def adam_update(master, first, second, gradient, rate, decay):
    first_new = BETA_FIRST * first + (1.0 - BETA_FIRST) * gradient
    second_new = BETA_SECOND * second + (1.0 - BETA_SECOND) * gradient * gradient
    first_hat = first_new / (1.0 - BETA_FIRST**STEP)
    second_hat = second_new / (1.0 - BETA_SECOND**STEP)
    master_new = master - rate * (
        first_hat / (jnp.sqrt(second_hat) + ADAM_EPSILON) + decay * master
    )
    return (master_new, first_new, second_new)


def one_hot(indices, filled, size):
    hit = indices[..., None] == jnp.arange(size, dtype=jnp.int32)
    return (hit & filled[..., None]).astype(BF16)


def frame_plans(lengths, packs, offsets, counts, source_rows, row_count, capacity):
    n_dp = lax.axis_size("dp")
    own = lax.axis_index("dp")
    slot = jnp.arange(capacity, dtype=jnp.int32)
    ids = jnp.arange(n_dp, dtype=jnp.int32)
    own_lengths, own_packs = pick(lengths, own, 1), pick(packs, own, 1)
    starts = jnp.cumsum(own_lengths, axis=1) - own_lengths
    matches = own_packs[:, None, :] == ids[None, :, None]
    length_to = jnp.sum(jnp.where(matches, own_lengths[:, None, :], 0), axis=2)
    start_to = jnp.sum(jnp.where(matches, starts[:, None, :], 0), axis=2)
    filled = slot < length_to[..., None]
    send = one_hot(start_to[..., None] + slot, filled, source_rows)
    here = packs == own

    def chosen(values):
        return jnp.sum(jnp.where(here, values, 0), axis=2)

    length_from, offset_from, count_from = chosen(lengths), chosen(offsets), chosen(counts)
    filled = slot < length_from[..., None]
    back = one_hot(offset_from[..., None] + slot, filled, row_count)
    position = jnp.arange(row_count, dtype=jnp.int32)
    inside = (position[None, :, None] >= offset_from[:, None, :]) & (
        position[None, :, None] < (offset_from + length_from)[:, None, :]
    )

    def select(values):
        return jnp.sum(jnp.where(inside, values[:, None, :], 0), axis=2)

    source = select(jnp.broadcast_to(ids, offset_from.shape))
    weight = select(count_from).astype(F32) / select(length_from).astype(F32)
    return send, back, source, weight


def on_device(
    x_source, skip_source, out_cotangent, item_length, item_pack, item_offset, item_count,
    gains, w_skip, w_qkv, w_out, w_up, w_down,
    gains_first, first_skip, first_qkv, first_out, first_up, first_down,
    gains_second, second_skip, second_qkv, second_out, second_up, second_down,
):
    n_y, n_c, n_a, n_b = sizes()
    n_dp, n_fsdp = n_y * n_c, n_a * n_b
    y, c, a, b = place()
    dp, fsdp = lax.axis_index("dp"), lax.axis_index("fsdp")
    micro, source_rows, width = x_source.shape
    row_count = out_cotangent.shape[1]
    capacity = source_rows // n_dp
    rows = micro * row_count

    send, back, source, weight = frame_plans(
        item_length[0], item_pack[0], item_offset[0], item_count[0], source_rows, row_count, capacity
    )

    def to_packs(values):
        return jnp.einsum("bpsr,brw->bpsw", send, values, preferred_element_type=F32).astype(BF16)

    payload = jnp.concatenate([to_packs(x_source), to_packs(skip_source)], axis=-1)
    own_gains = gains.shape[1]
    low_gains = jnp.zeros((8, 128), F32).at[:2, :own_gains].set(gains.astype(BF16).astype(F32))
    cotangent, frame_weight = out_cotangent.reshape(rows, width), weight.reshape(rows, 1)
    results = forward_all(
        (w_skip, w_qkv, w_out, w_up, w_down), payload, low_gains,
        jnp.moveaxis(back.reshape(micro, n_dp * capacity, row_count), 1, 2),
        cotangent, frame_weight, source,
    )
    fulls, saved, out_frames, gains_all = results[:5], results[5:18], results[18], results[19]
    fulls = [full.reshape(-1, full.shape[-1]) for full in fulls]
    results = backward_all(
        fulls, saved, cotangent, frame_weight, gains_all,
        back.reshape(micro, n_dp * capacity, row_count), source,
    )
    gradients, returned, small = results[:5], results[5], results[6]
    grad_gains, squares = small[:, :256].reshape(2, width), small[:, 256:]
    in_gradient = jnp.einsum(
        "bsr,bsw->brw", send.reshape(micro, n_dp * capacity, source_rows), returned,
        preferred_element_type=F32,
    ).astype(BF16)
    input_gradient, skip_gradient = in_gradient[..., :width], in_gradient[..., width:]
    total_squares = jnp.sum(squares) + jnp.sum(grad_gains * grad_gains)
    gradient_norm = jnp.sqrt(total_squares)
    grad_gains = pick(grad_gains.reshape(2, n_fsdp, own_gains), fsdp, 1)
    gradients = [gradient.astype(F32) for gradient in gradients] + [grad_gains]
    param_count = 6 * D * D + 2 * D * FF + 2 * D
    clip = jnp.minimum(1.0, 0.02 * math.sqrt(param_count) / gradient_norm)
    grad_skip, grad_qkv, grad_out, grad_up, grad_down, grad_gains = [clip * g for g in gradients]
    results = [out_frames.reshape(micro, row_count, width), input_gradient, skip_gradient]
    results.append(gradient_norm.reshape(1))
    results.extend(adam_update(gains, gains_first, gains_second, grad_gains, 0.3, 0.0))
    for master, first, second, gradient, fan_in in (
        (w_skip, first_skip, second_skip, grad_skip, 2 * D),
        (w_qkv, first_qkv, second_qkv, grad_qkv, D),
        (w_out, first_out, second_out, grad_out, D // 16),
        (w_up, first_up, second_up, grad_up, D),
        (w_down, first_down, second_down, grad_down, FF),
    ):
        new = adam_update(master, first, second, gradient, 0.5 / math.sqrt(fan_in), WEIGHT_DECAY)
        results.extend(new)
        results.append(new[0].astype(BF16))
    return tuple(results)


def solution(mesh):
    frames = P(None, ("dp", "fsdp"), None)
    plan = P("fsdp", None, None, None)
    gain, weight = P(None, "fsdp"), P("fsdp", None)
    return jax.shard_map(
        on_device,
        mesh=mesh,
        in_specs=(frames,) * 3 + (plan,) * 4 + ((gain,) + (weight,) * 5) * 3,
        out_specs=(frames,) * 3 + (P(),) + (gain,) * 3 + (weight,) * 20,
        check_vma=False,
    )
```

```python
from functools import partial
import math

import jax
import jax.numpy as jnp
from jax import lax
from jax.experimental import pallas as pl
from jax.experimental.pallas import tpu as pltpu
from jax.sharding import PartitionSpec as P

D = 1024
HEADS = 16
HD = 64
FF = 4096
STEP = 5
CORES = 2
OUTER = 4

BETA_FIRST = 0.5
BETA_SECOND = 0.5
ADAM_EPSILON = 1e-08
WEIGHT_DECAY = 0.01
NORM_EPSILON = 1e-05

BF16 = jnp.bfloat16
F32 = jnp.float32
MESH = pl.DeviceIdType.MESH

GATHER_UNITS = (
    (0, 0, 2, False), (0, 1, 2, False), (1, 0, 2, True), (1, 1, 2, True), (2, 0, 1, False),
    (3, 0, 2, True), (3, 1, 2, True),
    (4, 0, 4, False), (4, 1, 4, False), (4, 2, 4, False), (4, 3, 4, False),
)
WINDOW, OWN_FIRST = 3, 4
VMEM_LIMIT = 63 * 2**20
REDUCE_UNITS = (
    (4, 0, 4, False), (4, 1, 4, False), (4, 2, 4, False), (4, 3, 4, False),
    (3, 0, 2, True), (3, 1, 2, True), (2, 0, 1, False),
    (1, 0, 2, False), (1, 1, 2, False),
    (0, 0, 4, False), (0, 1, 4, False), (0, 2, 4, False), (0, 3, 4, False),
)


def sizes():
    n_dp, n_fsdp = lax.axis_size("dp"), lax.axis_size("fsdp")
    return n_dp // CORES, CORES, OUTER, n_fsdp // OUTER


def turn(value, step, size):
    return lax.rem(value + (step + size) % size, size)


class Remote:
    def __init__(self, src, dst, land, device, **sems):
        def describe(target):
            return pltpu.make_async_remote_copy(
                src_ref=src, dst_ref=target, device_id=device, device_id_type=MESH, **sems
            )

        self.given, self.describe, self.land, self.left = describe(dst), describe, land, False
        self.given.start()

    def wait_recv(self):
        self.describe(self.land).wait_recv()

    def wait_send(self):
        if not self.left:
            self.given.wait_send()
        self.left = True


class Copies:
    def __init__(self, send_sem, recv_sem, local_sem):
        self.send_sem, self.recv_sem, self.local_sem = send_sem, recv_sem, local_sem
        self.locals, self.sent = 0, []

    def remote(self, src, dst, land, device):
        index = len(self.sent)
        sems = dict(send_sem=self.send_sem.at[index], recv_sem=self.recv_sem.at[index])
        self.sent.append(Remote(src, dst, land, device, **sems))
        return self.sent[-1]

    def local(self, src, dst):
        index = self.locals
        self.locals += 1
        copy = pltpu.make_async_copy(src, dst, self.local_sem.at[index])
        copy.start()
        return copy


def greet(dims, dp, fsdp):
    n_y, n_c, n_a, n_b = dims
    n_dp, n_fsdp = n_y * n_c, n_a * n_b
    barrier = pltpu.get_barrier_semaphore()
    partners = [(turn(dp, k, n_dp), fsdp) for k in range(1, n_dp)]
    partners += [(dp, turn(fsdp, k, n_fsdp)) for k in range(1, n_fsdp)]
    for partner in partners:
        pl.semaphore_signal(barrier, inc=1, device_id=partner, device_id_type=MESH)
    pl.semaphore_wait(barrier, len(partners))


def whole(ref, first=0, width=None):
    n_a, n_b, rows, columns = ref.shape
    width = columns if width is None else width
    return ref[:, :, :, pl.ds(first, width)].reshape(n_a * n_b * rows, width)


def row_loop(rows, chunk, body):
    @pl.loop(0, rows // chunk)
    def _(i):
        body(pl.ds(pl.multiple_of(i * chunk, chunk), chunk))


def norm_into(hidden, gain_row, target, hat, scales, first):
    def body(at):
        centre = hidden[at, :]
        centre = centre - jnp.mean(centre, axis=-1, keepdims=True)
        spread = jnp.mean(centre * centre, axis=-1, keepdims=True)
        scale = lax.rsqrt(spread + NORM_EPSILON)
        normal = centre * scale
        target[at, :] = (normal * gain_row).astype(BF16)
        hat[at, :] = normal.astype(BF16)
        scales[at, pl.ds(first, 64)] = jnp.broadcast_to(scale, (scale.shape[0], 64))

    row_loop(hidden.shape[0], 64, body)


GELU_SCALE = math.sqrt(2.0 / math.pi)


def gelu_and_slope(u):
    square = u * u
    bent = jnp.tanh(GELU_SCALE * (u + 0.044715 * (square * u)))
    half = 0.5 * (1.0 + bent)
    slope = half + (0.5 * GELU_SCALE) * u * (1.0 - bent * bent) * (1.0 + 0.134145 * square)
    return u * half, slope


def head_probs(queries, keys_all, distance, same, slope):
    scores = lax.dot_general(
        queries, keys_all, (((1,), (1,)), ((), ())), preferred_element_type=F32
    )
    scores = jnp.where(same, scores * HD ** (-0.5) - slope * distance, -1e30)
    weights = jnp.exp(scores - jnp.max(scores, axis=-1, keepdims=True))
    return weights / jnp.sum(weights, axis=-1, keepdims=True)


def head_slope(head, columns):
    number = jnp.full((1, columns), head + 1, jnp.int32).astype(F32)
    return jnp.exp2(number * (-8.0 / HEADS))


def pair_mask(rows):
    lane = lax.broadcasted_iota(jnp.int32, (rows, 2 * HD), 1)
    return lane < HD


def forward_kernel(dims, *refs):
    n_y, n_c, n_a, n_b = dims
    lengths, packs, offsets, counts = refs[:4]
    masters, x_source, skip_source, gains, cotangent = refs[4:9], *refs[9:13]
    refs = refs[13:]
    fulls_out, refs = refs[:5], refs[5:]
    packed_out, qkv_out, mixed_out, slope_out, act_out, one_out, two_out = refs[:7]
    hat_one_out, hat_two_out, scales_out, low_out, low_far_out, act_far_out = refs[7:13]
    weights_out, frames_out, gains_out = refs[13:16]
    refs = refs[16:]
    fulls, refs = refs[:5], refs[5:]
    stage, arrived, hot, gains_all, packed, base, one, qkv, mixed, after, two, up, out = refs[:13]
    hat_one, hat_two, scales, slope_buf, weights = refs[13:18]
    send_sem, recv_sem, local_sem = refs[18:]
    dp, fsdp = lax.axis_index("dp"), lax.axis_index("fsdp")
    y, c, a, b = dp // n_c, lax.rem(dp, n_c), fsdp // n_b, lax.rem(fsdp, n_b)
    n_dp, n_fsdp = n_y * n_c, n_a * n_b
    copies = Copies(send_sem, recv_sem, local_sem)
    remote, local = copies.remote, copies.local
    sources = [(qkv, 0), (qkv, 1), (qkv, 2), (mixed, 0)]
    source_copies = []
    for index, (ref, part) in enumerate(sources):
        origin = (x_source, skip_source)[index // 2].at[index % 2]
        source_copies.append(local(origin, ref.at[:, pl.ds(part * D, D)]))
    cot_copy = local(cotangent, out)
    greet(dims, dp, fsdp)
    micro, source_rows = x_source.shape[:2]
    slots = source_rows // n_dp

    staged = {}

    def load(m):
        rows, columns = masters[m].shape
        view = stage.at[m % 2, pl.ds(0, rows * columns // 1024)]
        if columns == 1024:
            staged[m] = [local(masters[m], view)]
        else:
            parts = columns // 1024
            staged[m] = [
                local(
                    masters[m].at[:, pl.ds(p * 1024, 1024)],
                    stage.at[m % 2, pl.ds(p * rows, rows)],
                )
                for p in range(parts)
            ]

    load(0)
    load(1)
    frames = []
    own_frames = []

    def slot(group):
        return pl.ds(pl.multiple_of(group * slots, 16), slots)

    outbound = {
        (0, 0): (packed, 0), (0, 1): (packed, D), (1, 0): (hat_one, 0), (1, 1): (hat_two, 0),
    }

    def make_payload():
        for copy in source_copies:
            copy.wait()
        for i in range(micro):
            starts, taken = plan_send(lengths, packs, i, dp, n_dp)
            for pack in range(n_dp):
                hot[pl.ds(pack * slots, slots), :] = hot_block(
                    (slots, source_rows), 0, starts[pack], taken[pack]
                )
            for half in range(2):
                ref, part = sources[2 * half + i]
                target, first = outbound[i, half]
                target[:, pl.ds(first, D)] = jnp.dot(
                    hot[...], ref[:, pl.ds(part * D, D)], preferred_element_type=F32
                ).astype(BF16)
            for k in range(n_dp):
                to, back = turn(dp, k, n_dp), turn(dp, -k, n_dp)
                for half in range(2):
                    ref, first = outbound[i, half]
                    view = ref.at[slot(to), pl.ds(first, D)]
                    cols = pl.ds(half * D, D)
                    if k == 0:
                        own_frames.append(local(view, arrived.at[i, slot(dp), cols]))
                    else:
                        frames.append(
                            remote(
                                view, arrived.at[i, slot(dp), cols], arrived.at[i, slot(back), cols],
                                (to, fsdp),
                            )
                        )

    def make_gain_rows():
        gains_all[fsdp] = jnp.zeros(gains_all.shape[1:], F32)
        own = gains.shape[1]
        gains_all[fsdp, pl.ds(0, 2), pl.ds(0, own)] = gains[...].astype(BF16).astype(F32)
        for k in range(1, n_fsdp):
            to, back = turn(fsdp, k, n_fsdp), turn(fsdp, -k, n_fsdp)
            gain_copies.append(
                remote(gains_all.at[fsdp], gains_all.at[fsdp], gains_all.at[back], (dp, to))
            )

    gain_copies = []

    units = []
    for m, part, parts, shared in GATHER_UNITS:
        width = masters[m].shape[1] // parts
        units.append((m, part * width, width, shared and width // (n_c * n_y) % 128 == 0))
    state = [{"x": [], "y": [], "c": []} for _ in units]

    def columns(u, of_c, of_y):
        m, first, width, shared = units[u]
        if shared:
            step = width // (n_c * n_y)
            return pl.ds(pl.multiple_of(first + (of_c * n_y + of_y) * step, 128), step)
        step = width // n_c
        return pl.ds(pl.multiple_of(first + of_c * step, 128), step)

    def convert(m):
        for copy in staged[m]:
            copy.wait()
        rows, width = masters[m].shape

        def body(at):
            for p in range(width // 1024):
                low = stage[m % 2, pl.ds(at.start + p * rows, at.size), :].astype(BF16)
                fulls[m][a, b, at, pl.ds(p * 1024, 1024)] = low

        row_loop(rows, 32, body)

    def pass_on(u, name, block, mask):
        full, cols = fulls[units[u][0]], columns(u, c, y)
        view, source = full.at[block, b, :, cols], block ^ mask
        landing = full.at[source, b, :, cols]
        copy = remote(view, view, landing, (dp, (a ^ mask) * n_b + b))
        state[u][name] = (copy, source)

    def stage_z(u):
        pass_on(u, "far", a, 2)
        pass_on(u, "near", a, 1)

    def spread(u, block_a, block_b, of_y, to_y):
        m, first, width, shared = units[u]
        full = fulls[m]
        view = full.at[block_a, block_b, :, columns(u, c, of_y)]
        if to_y and shared:
            for k in range(1, n_y):
                source = turn(y, -k, n_y)
                landing = full.at[block_a, block_b, :, columns(u, c, source)]
                copy = remote(view, view, landing, (turn(y, k, n_y) * n_c + c, fsdp))
                state[u]["y"].append((copy, block_a, block_b, source))
        landing = full.at[block_a, block_b, :, columns(u, 1 - c, of_y)]
        state[u]["c"].append(remote(view, view, landing, (y * n_c + 1 - c, fsdp)))

    def send_x(u, block_a):
        m = units[u][0]
        cols = columns(u, c, y)
        view = fulls[m].at[block_a, b, :, cols]
        for k in range(1, n_b):
            landing = fulls[m].at[block_a, turn(b, -k, n_b), :, cols]
            state[u]["x"].append(remote(view, view, landing, (dp, a * n_b + turn(b, k, n_b))))

    def stage_own(u):
        send_x(u, a)

    def relay(u, name):
        copy, source = state[u][name]
        copy.wait_recv()
        if name == "far":
            pass_on(u, "last", source, 1)
        send_x(u, source)
        spread(u, source, b, y, True)

    def relay_own(u):
        relay(u, "far")
        relay(u, "near")

    def stage_x(u):
        relay_own(u)
        relay(u, "last")

    def stage_s(u):
        for copy in state[u]["x"]:
            copy.wait_recv()
        for k in range(1, n_b):
            spread(u, slice(None), turn(b, -k, n_b), y, True)

    def stage_c(u):
        for copy, block_a, block_b, source in state[u]["y"]:
            copy.wait_recv()
            spread(u, block_a, block_b, source, False)

    outgoing = []

    def finish(u):
        m, first, width, shared = units[u]
        for copy in state[u]["c"]:
            copy.wait_recv()
        cols = pl.ds(first, width)
        outgoing.append(local(fulls[m].at[:, :, :, cols], fulls_out[m].at[:, :, :, cols]))

    for m in range(5):
        convert(m)
        if m + 2 < 5:
            load(m + 2)
        for u in range(len(units)):
            if units[u][0] == m and u < WINDOW:
                stage_z(u)
            if units[u][0] == m and u < OWN_FIRST:
                stage_own(u)
        if m == 0:
            make_payload()
            make_gain_rows()

    count = len(units)

    def comm(u):
        if u < count:
            stage_x(u)
        if u + WINDOW < count:
            stage_z(u + WINDOW)
        if OWN_FIRST <= u + WINDOW < count:
            stage_own(u + WINDOW)
        if u == 6 and WINDOW == 3:
            stage_z(10)
            stage_own(10)
        if u >= 1:
            stage_s(u - 1)

    tokens, width = base.shape
    per_pack = tokens // micro

    def make_packed():
        for copy in frames:
            copy.wait_recv()
        for copy in own_frames:
            copy.wait()
        for copy in frames:
            copy.wait_send()
        for i in range(micro):
            offset, length = plan_pack(offsets, packs, i, dp, n_dp), plan_pack(lengths, packs, i, dp, n_dp)
            spots.append((offset, length))
            at = pl.ds(i * per_pack, per_pack)
            for source in range(n_dp):
                hot[at, pl.ds(source * slots, slots)] = hot_block(
                    (per_pack, slots), 1, offset[source], length[source]
                )
            for half in range(2):
                cols = pl.ds(half * 1024, 1024)
                packed[at, cols] = jnp.dot(
                    hot[at, :], arrived[i, :, cols], preferred_element_type=F32
                ).astype(BF16)
        outgoing.append(local(packed, packed_out))

    spots = []
    gain_rows = []

    def make_gains():
        for copy in gain_copies:
            copy.wait_recv()
        outgoing.append(local(gains_all, gains_out))
        own = D // n_fsdp
        for row in range(2):
            gain_rows.append(
                jnp.concatenate([gains_all[f, pl.ds(row, 1), pl.ds(0, own)] for f in range(n_fsdp)], axis=1)
            )

    def make_base():
        for first in (0, 512):
            base[:, pl.ds(first, 512)] = jnp.dot(
                packed[...], whole(fulls[0], first, 512), preferred_element_type=F32
            )
        norm_into(base, gain_rows[0], one, hat_one, scales, 0)
        outgoing.append(local(hat_one, hat_one_out))
        outgoing.append(local(one, one_out))

    def make_qkv():
        for first in range(0, 3 * D, 512):
            qkv[:, pl.ds(first, 512)] = jnp.dot(
                one[...], whole(fulls[1], first, 512), preferred_element_type=F32
            ).astype(BF16)
        outgoing.append(local(qkv, qkv_out))

    def attend(i, first=0, last=HEADS // 2):
        rows = pl.ds(i * per_pack, per_pack)
        position = lax.broadcasted_iota(jnp.int32, (per_pack, per_pack), 0)
        distance = jnp.abs(
            position - lax.broadcasted_iota(jnp.int32, (per_pack, per_pack), 1)
        ).astype(F32)
        first_head = pair_mask(per_pack)
        same = same_item(*spots[i], per_pack)

        @pl.loop(first, last)
        def _(pair):
            def cols(part):
                return pl.ds(pl.multiple_of(part * D + pair * 2 * HD, 128), 2 * HD)

            queries, keys_all, values_all = (qkv[rows, cols(part)] for part in range(3))
            results = []
            for head in range(2):
                mine = first_head if head == 0 else jnp.logical_not(first_head)
                slope = head_slope(2 * pair + head, per_pack)
                probs = head_probs(
                    jnp.where(mine, queries, jnp.zeros_like(queries)), keys_all, distance, same, slope
                )
                results.append(
                    jnp.dot(probs.astype(BF16), values_all, preferred_element_type=F32)
                )
            mixed[rows, cols(0)] = jnp.where(first_head, results[0], results[1]).astype(BF16)

    def make_after():
        outgoing.append(local(mixed, mixed_out))
        for first in (0, 512):
            cols = pl.ds(first, 512)
            after[:, cols] = base[:, cols] + jnp.dot(
                mixed[...], whole(fulls[2], first, 512), preferred_element_type=F32
            )
        norm_into(after, gain_rows[1], two, hat_two, scales, 64)
        outgoing.append(local(hat_two, hat_two_out))
        outgoing.append(local(scales, scales_out))
        outgoing.append(local(two, two_out))

    slope_copies = [None, None]
    half_ff = FF // 2

    def make_up(j):
        slot_now = j % 2
        cols = pl.ds(j * 512, 512)
        up[...] = jnp.dot(two[...], whole(fulls[3], j * 512, 512), preferred_element_type=F32)
        if slope_copies[slot_now] is not None:
            slope_copies[slot_now].wait()
        half, within = j * 512 // half_ff, j * 512 % half_ff

        def body(at):
            value, slope = gelu_and_slope(up[at, :])
            arrived[half, at, pl.ds(within, 512)] = value.astype(BF16)
            slope_buf[slot_now, at, :] = slope.astype(BF16)

        row_loop(tokens, 64, body)
        slope_copies[slot_now] = local(slope_buf.at[slot_now], slope_out.at[:, cols])

    other_core = (y * n_c + 1 - c, fsdp)
    crossing = []

    def send_act(half):
        cols = pl.ds(half * half_ff, half_ff)
        outgoing.append(local(arrived.at[half], act_out.at[:, cols]))
        there = act_far_out.at[:, cols]
        crossing.append(remote(arrived.at[half], there, there, other_core))

    low_copies = []

    def make_low():
        cot_copy.wait()
        for i in range(micro):
            rows = pl.ds(i * per_pack, per_pack)
            offset, length, count = (
                plan_pack(values, packs, i, dp, n_dp) for values in (offsets, lengths, counts)
            )
            over = spans((per_pack, 1), 0, offset, length, count).astype(F32)
            weight = over / spans((per_pack, 1), 0, offset, length, length).astype(F32)
            weights[rows, :] = jnp.broadcast_to(weight, (per_pack, 128))

        def body(at):
            out[at, :] = (weights[at, pl.ds(0, 1)] * out[at, :].astype(F32)).astype(BF16)

        row_loop(tokens, 64, body)
        outgoing.append(local(weights, weights_out))
        low_copies.append(local(out, low_out))
        step = D // n_c
        others = pl.ds(pl.multiple_of((1 - c) * step, 128), step)
        crossing.append(remote(out.at[:, others], low_far_out, low_far_out, other_core))

    def low_left():
        low_copies[0].wait()
        crossing[0].wait_send()

    def make_out(first, step):
        cols = pl.ds(first, step)
        weight = whole(fulls[4], first, step)
        total = after[:, cols] + jnp.dot(
            arrived[0], weight[:half_ff], preferred_element_type=F32
        )
        total += jnp.dot(arrived[1], weight[half_ff:], preferred_element_type=F32)
        out[:, cols] = total.astype(BF16)

    comm(0)
    comm(1)
    comm(2)
    make_gains()
    make_low()
    comm(3)
    make_packed()
    finish(0)
    finish(1)
    make_base()
    comm(4)
    comm(5)
    comm(6)
    stage_c(2)
    relay_own(7)
    stage_c(3)
    finish(2)
    finish(3)
    make_qkv()
    attend(0, 0, 4)
    relay(7, "last")
    relay_own(8)
    stage_s(6)
    attend(0, 4, 8)
    relay(8, "last")
    relay_own(9)
    attend(1, 0, 4)
    relay(9, "last")
    relay_own(10)
    stage_s(7)
    stage_c(5)
    attend(1, 4, 8)
    relay(10, "last")
    finish(4)
    stage_s(8)
    make_after()
    finish(5)
    for j in range(4):
        make_up(j)
    send_act(0)
    stage_c(6)
    stage_s(9)
    low_left()
    finish(6)
    for j in range(4, 8):
        make_up(j)
    send_act(1)
    finish(7)
    make_out(0, 256)
    stage_s(10)
    finish(8)
    make_out(256, 256)
    finish(9)
    make_out(512, 256)
    finish(10)
    make_out(768, 256)
    outgoing.append(local(out, frames_out))
    for copy in crossing:
        copy.wait_recv()
    for copy in outgoing + slope_copies:
        copy.wait()
    for copy in copies.sent:
        copy.wait_send()


def forward_all(items, masters, x_source, skip_source, gains, cotangent):
    dims = sizes()
    n_y, n_c, n_a, n_b = dims
    n_fsdp = n_a * n_b
    micro, source_rows, _ = x_source.shape
    n_dp = n_y * n_c
    slots = source_rows // n_dp
    tokens = cotangent.shape[0]
    per_pack = tokens // micro
    total = 2 * micro * (n_dp - 1) + n_fsdp - 1 + 3
    for _, _, _, shared in GATHER_UNITS:
        groups = n_a - 1 + n_b - 1
        total += (n_a - 1) + n_a * (n_b - 1)
        total += (n_y - 1) * groups + n_y * groups if shared else groups
    shape = jax.ShapeDtypeStruct
    full_shapes = [(n_a, n_b) + master.shape for master in masters]
    out_shape = [shape(s, BF16) for s in full_shapes]
    out_shape += [
        shape((tokens, 2 * D), BF16), shape((tokens, 3 * D), BF16), shape((tokens, D), BF16),
        shape((tokens, FF), BF16), shape((tokens, FF), BF16),
        shape((tokens, D), BF16), shape((tokens, D), BF16),
        shape((tokens, D), BF16), shape((tokens, D), BF16),
        shape((tokens, 128), F32),
        shape((tokens, D), BF16), shape((tokens, D // n_c), BF16), shape((tokens, FF), BF16),
        shape((tokens, 128), F32), shape((tokens, D), BF16), shape((n_fsdp, 8, 128), F32),
    ]
    anywhere = pl.BlockSpec(memory_space=pl.ANY)
    inside = pl.BlockSpec(memory_space=pltpu.VMEM)
    scalars = pl.BlockSpec(memory_space=pltpu.SMEM)
    stage_rows = max(m.shape[0] * m.shape[1] // 1024 for m in masters)
    results = pl.pallas_call(
        partial(forward_kernel, dims),
        out_shape=out_shape,
        in_specs=[scalars] * 4 + [anywhere] * 7 + [inside, anywhere],
        out_specs=[anywhere] * len(out_shape),
        scratch_shapes=[pltpu.VMEM(s, BF16) for s in full_shapes]
        + [
            pltpu.VMEM((2, stage_rows, 1024), F32),
            pltpu.VMEM((micro, n_dp * slots, 2 * D), BF16),
            pltpu.VMEM((source_rows, source_rows), BF16),
            pltpu.VMEM((n_fsdp, 8, 128), F32),
            pltpu.VMEM((tokens, 2 * D), BF16),
            pltpu.VMEM((tokens, D), F32),
            pltpu.VMEM((tokens, D), BF16),
            pltpu.VMEM((tokens, 3 * D), BF16),
            pltpu.VMEM((tokens, D), BF16),
            pltpu.VMEM((tokens, D), F32),
            pltpu.VMEM((tokens, D), BF16),
            pltpu.VMEM((tokens, 512), F32),
            pltpu.VMEM((tokens, D), BF16),
            pltpu.VMEM((tokens, D), BF16),
            pltpu.VMEM((tokens, D), BF16),
            pltpu.VMEM((tokens, 128), F32),
            pltpu.VMEM((2, tokens, 512), BF16),
            pltpu.VMEM((tokens, 128), F32),
            pltpu.SemaphoreType.DMA((total,)),
            pltpu.SemaphoreType.DMA((total,)),
            pltpu.SemaphoreType.DMA((64,)),
        ],
        compiler_params=pltpu.CompilerParams(
            collective_id=0, has_side_effects=True, vmem_limit_bytes=VMEM_LIMIT
        ),
        name="gather_and_forward",
    )(
        *items, *masters, x_source, skip_source, gains, cotangent,
    )
    return results


def norm_back(hat, scale, gain_row, gradient):
    scaled = gradient * gain_row
    back = scale * (
        scaled
        - jnp.mean(scaled, axis=-1, keepdims=True)
        - hat * jnp.mean(scaled * hat, axis=-1, keepdims=True)
    )
    return back, jnp.sum(gradient * hat, axis=0, keepdims=True)


RING = 4


def backward_kernel(dims, shapes, *refs):
    n_y, n_c, n_a, n_b = dims
    fulls, refs = refs[:5], refs[5:]
    (packed, qkv, mixed, slope, act, one, two, hat_one, hat_two, scales, low_in, low_far_in, act_far,
     frame_weight, cotangent, gains_all, lengths, packs, offsets) = refs[:19]
    refs = refs[19:]
    outs, returned, small_out, refs = refs[:5], refs[5], refs[6], refs[7:]
    sums, finals, refs = refs[:5], refs[5:10], refs[10:]
    (pool, low_far, wide, wide_far, left_far, ring, slope_buf, acc, hidden,
     cot, low, hat, gain_buf, gain_land, small, small_total) = refs[:16]
    refs = refs[16:]
    landing, refs = refs[: 3 * len(REDUCE_UNITS)], refs[3 * len(REDUCE_UNITS) :]
    send_sem, recv_sem, local_sem, credit = refs
    dp, fsdp = lax.axis_index("dp"), lax.axis_index("fsdp")
    y, c, a, b = dp // n_c, lax.rem(dp, n_c), fsdp // n_b, lax.rem(fsdp, n_b)
    n_dp, n_fsdp = n_y * n_c, n_a * n_b
    other_core = (y * n_c + 1 - c, fsdp)
    copies = Copies(send_sem, recv_sem, local_sem)
    remote, local = copies.remote, copies.local
    greet(dims, dp, fsdp)
    tokens = cot.shape[0]
    micro, slab = returned.shape[:2]
    per_pack, slots = tokens // micro, slab // n_dp
    spots = [
        [plan_pack(values, packs, i, dp, n_dp) for values in (offsets, lengths)] for i in range(micro)
    ]
    near, far = pl.ds(0, tokens), pl.ds(tokens, tokens)

    order = []
    for block in range(4):
        order += [(4, block * 1024, 0), (4, block * 1024, 512)]
        order += [(3, 0, block * 1024), (3, 0, block * 1024 + 512)]
    order += [(2, 0, 0), (2, 0, 512)]
    order += [(1, 0, first) for first in range(0, 3 * D, 512)]
    order += [(0, first, second) for first in (0, 1024) for second in (0, 512)]
    ring_copies = {}
    ring_state = [0, 0]

    def ring_load():
        index = ring_state[0]
        if index < len(order):
            m, first, second = order[index]
            ring_copies[index] = local(
                fulls[m].at[pl.ds(first, 1024), pl.ds(second, 512)], ring.at[index % RING]
            )
            ring_state[0] += 1

    def ring_next():
        index = ring_state[1]
        ring_state[1] += 1
        ring_copies.pop(index).wait()
        return ring.at[index % RING]

    def far_half(width):
        return pl.ds(pl.multiple_of((1 - c) * width, 128), width)

    half_ff = FF // 2
    low_copies = [local(low_in, low), local(low_far_in, low_far)]
    act_copies = []
    for half in range(2):
        cols = pl.ds(half * half_ff, half_ff)
        act_copies.append(local(act.at[:, cols], pool.at[half, near]))
        act_copies.append(local(act_far.at[:, cols], pool.at[half, far]))
    for _ in range(RING):
        ring_load()
    slope_copies = {}

    def slope_load(j):
        slope_copies[j] = local(slope.at[:, pl.ds(j * 512, 512)], slope_buf.at[j % 2])

    slope_load(0)
    slope_load(1)
    cot_copy = local(cotangent, cot)
    hat_copy = local(hat_two, hat)
    two_away = remote(two, left_far, left_far, other_core)

    units = []
    for m, part, parts, shared in REDUCE_UNITS:
        width = shapes[m][1] // n_c // parts
        units.append((m, part * width, width, shared))
    state = [{} for _ in units]

    def piece(unit, of_y):
        m, first, width, shared = unit
        if shared:
            step = width // n_y
            return pl.ds(pl.multiple_of(first + of_y * step, 128), step), step
        return pl.ds(first, width), width

    def product(u, left_near, left_other, right_near, right_far, count=1):
        m, first, width, shared = units[u]
        width *= count
        rows = sums[m].shape[2]
        group = max(1, 512 // (n_b * rows))
        tile = group * n_b * rows
        half = shapes[m][1] // n_c
        mine = pl.ds(pl.multiple_of(c * half + first, 128), width)

        @pl.loop(0, n_a // group)
        def _(i):
            contract = (((0,), (0,)), ((), ()))
            value = lax.dot_general(
                left_near(i, tile), right_near[:, mine], contract, preferred_element_type=F32
            )
            value += lax.dot_general(
                left_other(i, tile), right_far[:, pl.ds(first, width)], contract,
                preferred_element_type=F32,
            )
            sums[m][pl.ds(i * group, group), :, :, pl.ds(first, width)] = value.astype(BF16).reshape(
                group, n_b, rows, width
            )

    def tiles(ref, rows, first):
        def pick_tile(i, tile):
            return ref[rows, pl.ds(pl.multiple_of(first + i * tile, 128), tile)]

        return pick_tile

    def pool_tiles(rows):
        def pick_tile(i, tile):
            per = half_ff // tile
            return pool[i // per, rows, pl.ds(pl.multiple_of(lax.rem(i, per) * tile, 128), tile)]

        return pick_tile

    def chunks(outer, rows, body):
        chunk = min(64, rows)
        per = rows // chunk

        @pl.loop(0, outer * per)
        def _(i):
            body(i // per, pl.ds(pl.multiple_of(lax.rem(i, per) * chunk, 16), chunk))


    def y_send(u):
        m, first, width, shared = units[u]
        for k in range(1, n_y):
            cols, step = piece(units[u], turn(y, k, n_y))
            there = landing[3 * u].at[k - 1]
            state[u].setdefault("y", []).append(
                remote(sums[m].at[:, :, :, cols], there, there, (turn(y, k, n_y) * n_c + c, fsdp))
            )

    def y_add(u):
        m = units[u][0]
        for copy in state[u]["y"]:
            copy.wait_recv()
        cols, step = piece(units[u], y)

        def body(outer, rows):
            at = (outer // n_b, lax.rem(outer, n_b), rows, cols)
            value = sums[m][at].astype(F32)
            for k in range(1, n_y):
                value += landing[3 * u][k - 1, outer // n_b, lax.rem(outer, n_b), rows, :].astype(F32)
            sums[m][at] = value.astype(BF16)

        chunks(n_a * n_b, sums[m].shape[2], body)

    def x_land(u):
        return landing[3 * u + 1] if units[u][3] else landing[3 * u]

    def z_land(u):
        return landing[3 * u + 2] if units[u][3] else landing[3 * u + 1]

    def x_send(u):
        m = units[u][0]
        cols, step = piece(units[u], y)
        state[u]["x"] = []
        for k in range(1, n_b):
            there = x_land(u).at[k - 1]
            to = turn(b, k, n_b)
            state[u]["x"].append(
                remote(sums[m].at[:, to, :, cols], there, there, (dp, a * n_b + to))
            )

    def x_add(u):
        m = units[u][0]
        for copy in state[u]["x"]:
            copy.wait_recv()
        cols, step = piece(units[u], y)

        def body(outer, rows):
            value = sums[m][outer, b, rows, cols].astype(F32)
            for k in range(1, n_b):
                value += x_land(u)[k - 1, outer, rows, :].astype(F32)
            sums[m][outer, b, rows, cols] = value.astype(BF16)

        chunks(n_a, sums[m].shape[2], body)

    def z_send(u):
        m = units[u][0]
        cols, step = piece(units[u], y)
        device = (dp, (a ^ 1) * n_b + b)
        state[u]["z"] = []
        for slot_at, block in ((0, a ^ 1), (1, a ^ 3)):
            there = z_land(u).at[slot_at]
            state[u]["z"].append(remote(sums[m].at[block, b, :, cols], there, there, device))

    def zz(u):
        m = units[u][0]
        for copy in state[u]["z"]:
            copy.wait_recv()
        cols, step = piece(units[u], y)

        def body(outer, rows):
            block = a ^ (2 * outer)
            value = sums[m][block, b, rows, cols].astype(F32)
            value += z_land(u)[outer, rows, :].astype(F32)
            sums[m][block, b, rows, cols] = value.astype(BF16)

        chunks(2, sums[m].shape[2], body)
        there = z_land(u).at[2]
        device = (dp, (a ^ 2) * n_b + b)
        state[u]["w"] = remote(sums[m].at[a ^ 2, b, :, cols], there, there, device)

    def z_add(u):
        m, first, width, shared = units[u]
        state[u]["w"].wait_recv()
        cols, step = piece(units[u], y)
        half = shapes[m][1] // n_c

        def body(outer, rows):
            value = sums[m][a, b, rows, cols].astype(F32) + z_land(u)[2, rows, :].astype(F32)
            if shared:
                at = pl.ds(pl.multiple_of(c * half + first + y * step, 128), step)
                finals[m][rows, at] = value.astype(BF16)
            elif n_y == 2:
                sums[m][a, b, rows, cols] = value.astype(BF16)
            else:
                landing[3 * u + 2][y, rows, :] = value.astype(BF16)

        chunks(1, sums[m].shape[2], body)

    def last_send(u):
        m, first, width, shared = units[u]
        half = shapes[m][1] // n_c
        state[u]["last"] = []
        for k in range(1, n_y):
            device = (turn(y, k, n_y) * n_c + c, fsdp)
            from_y = turn(y, -k, n_y)
            if shared:
                step = width // n_y
                mine = pl.ds(pl.multiple_of(c * half + first + y * step, 128), step)
                theirs = pl.ds(pl.multiple_of(c * half + first + from_y * step, 128), step)
                view = finals[m].at[:, mine]
                state[u]["last"].append(remote(view, view, finals[m].at[:, theirs], device))
            elif n_y == 2:
                view, there = sums[m].at[a, b, :, piece(units[u], y)[0]], landing[3 * u + 2].at[0]
                state[u]["last"].append(remote(view, there, there, device))
            else:
                view = landing[3 * u + 2].at[y]
                state[u]["last"].append(remote(view, view, landing[3 * u + 2].at[from_y], device))

    def last_add(u):
        m, first, width, shared = units[u]
        half = shapes[m][1] // n_c
        for copy in state[u]["last"]:
            copy.wait_recv()
        at = pl.ds(pl.multiple_of(c * half + first, 128), width)
        if not shared:

            def body(outer, rows):
                value = landing[3 * u + 2][0, rows, :].astype(F32)
                if n_y == 2:
                    value += sums[m][a, b, rows, pl.ds(first, width)].astype(F32)
                for k in range(1, n_y if n_y > 2 else 0):
                    value += landing[3 * u + 2][k, rows, :].astype(F32)
                finals[m][rows, at] = value.astype(BF16)

            chunks(1, sums[m].shape[2], body)
        view = finals[m].at[:, at]
        theirs = pl.ds(pl.multiple_of((1 - c) * half + first, 128), width)
        state[u]["core"] = remote(view, view, finals[m].at[:, theirs], other_core)

    def xz(u):
        x_add(u)
        z_send(u)

    def yx(u):
        y_add(u)
        x_send(u)

    def zl(u):
        z_add(u)
        last_send(u)


    masks = [1 << i for i in range(n_y.bit_length() - 1)]
    dp_partners = [other_core] + [((y ^ mask) * n_c + c, fsdp) for mask in masks]
    gain_copies = {}

    def gain_step(step):
        if step > 0:
            gain_copies[step - 1].wait_recv()
            gain_buf[step] = gain_buf[step - 1] + gain_land[step - 1]
        if step < len(dp_partners):
            there = gain_land.at[step]
            gain_copies[step] = remote(gain_buf.at[step], there, there, dp_partners[step])

    def add_gain(row, value):
        for part in range(4):
            gain_buf[0, pl.ds(4 * row + part, 1), :] += value[:, part * 256 : part * 256 + 256]

    def give_credit(index):
        pl.semaphore_signal(credit.at[index], inc=1, device_id=other_core, device_id_type=MESH)


    own = D // n_fsdp

    def gain_row(row):
        return jnp.concatenate(
            [gains_all[f, pl.ds(row, 1), pl.ds(0, own)] for f in range(n_fsdp)], axis=1
        )

    def dot_right(left, right):
        return lax.dot_general(left, right, (((1,), (1,)), ((), ())), preferred_element_type=F32)

    def add_product(left, weight, first):
        for start in (0, 512):
            cols = pl.ds(start, 512)
            value = dot_right(left, weight[cols, :])
            acc[:, cols] = value if first else acc[:, cols] + value

    def feed_forward(block):
        down = (ring_next(), ring_next())
        for part in range(2):
            j = 2 * block + part
            slope_copies[j].wait()
            rows = pl.ds(part * 512, 512)
            d_act = dot_right(low[:, :512], down[0][rows, :])
            d_act += dot_right(low[:, 512:], down[1][rows, :])
            wide[:, pl.ds(j * 512, 512)] = (d_act * slope_buf[j % 2].astype(F32)).astype(BF16)
            if j + 2 < 8:
                slope_load(j + 2)
        ring_load()
        ring_load()
        for part in range(2):
            j = 2 * block + part
            add_product(wide[:, pl.ds(j * 512, 512)], ring_next(), j == 0)
            ring_load()

    for copy in low_copies + act_copies:
        copy.wait()
    for u in (0, 2):
        product(u, pool_tiles(near), pool_tiles(far), low, low_far, 2)
        x_send(u)
        x_send(u + 1)
    give_credit(0)
    left_here = [
        local(two, pool.at[0, near, pl.ds(0, D)]),
        local(one, pool.at[0, near, pl.ds(D, D)]),
    ]
    qkv_here = [
        local(qkv.at[:, pl.ds(0, D)], pool.at[1, near, pl.ds(0, D)]),
        local(qkv.at[:, pl.ds(D, D)], pool.at[1, near, pl.ds(D, D)]),
        local(qkv.at[:, pl.ds(2 * D, D)], pool.at[1, far, pl.ds(0, D)]),
        local(mixed, pool.at[1, far, pl.ds(D, D)]),
    ]
    for block in range(4):
        feed_forward(block)
        if block == 2:
            xz(0)
    pl.semaphore_wait(credit.at[0], 1)
    there = pool.at[0, far, pl.ds(0, D)]
    mixed_away = remote(mixed, there, there, other_core)
    wide_away = remote(wide.at[:, far_half(half_ff)], wide_far, wide_far, other_core)
    hat_copy.wait()
    cot_copy.wait()
    gain_buf[0] = jnp.zeros_like(gain_buf[0])
    gain_two = gain_row(1)

    def after_body(at):
        back, grad_gain = norm_back(
            hat[at, :].astype(F32), scales[at, pl.ds(64, 1)], gain_two, acc[at, :]
        )
        d_after = frame_weight[at, pl.ds(0, 1)] * cot[at, :].astype(F32) + back
        hidden[at, :] = d_after
        low[at, :] = d_after.astype(BF16)
        add_gain(1, grad_gain)

    row_loop(tokens, 64, after_body)
    after_away = remote(low.at[:, far_half(D // n_c)], low_far, low_far, other_core)
    hat_copy = local(hat_one, hat)
    pair = (ring_next(), ring_next())
    for start in (0, 512):
        cols = pl.ds(start, 512)
        value = dot_right(low[:, :512], pair[0][cols, :]) + dot_right(low[:, 512:], pair[1][cols, :])
        cot[:, cols] = value.astype(BF16)
    ring_load()
    ring_load()
    xz(1)
    zz(0)
    for copy in left_here + qkv_here:
        copy.wait()
    two_away.wait_recv()
    wide_away.wait_recv()
    for u in (4, 5):
        product(u, tiles(pool.at[0], near, 0), tiles(left_far, near, 0), wide, wide_far)
        y_send(u)
    mixed_away.wait_recv()
    after_away.wait_recv()
    product(6, tiles(pool.at[1], far, D), tiles(pool.at[0], far, 0), low, low_far)
    give_credit(1)
    x_send(6)
    wide_away.wait_send()
    pl.semaphore_wait(credit.at[1], 1)
    packed_away = remote(packed, pool.at[0, far], pool.at[0, far], other_core)
    one_away = remote(one, left_far, left_far, other_core)

    def attend_back(i, first_pair=0, last_pair=HEADS // 2):
        rows = pl.ds(i * per_pack, per_pack)
        rows_far = pl.ds(tokens + i * per_pack, per_pack)
        position = lax.broadcasted_iota(jnp.int32, (per_pack, per_pack), 0)
        distance = jnp.abs(
            position - lax.broadcasted_iota(jnp.int32, (per_pack, per_pack), 1)
        ).astype(F32)
        first_head = pair_mask(per_pack)
        same = same_item(*spots[i], per_pack)

        @pl.loop(first_pair, last_pair)
        def _(pair):
            def cols(first):
                return pl.ds(pl.multiple_of(first + pair * 2 * HD, 128), 2 * HD)

            queries, keys_all = pool[1, rows, cols(0)], pool[1, rows, cols(D)]
            values_all = pool[1, rows_far, cols(0)]
            d_mixed = cot[rows, cols(0)]
            zero = jnp.zeros_like(queries)
            total = [None, None, None]
            for head in range(2):
                mine = first_head if head == 0 else jnp.logical_not(first_head)
                query, key, d_head = (
                    jnp.where(mine, value, zero) for value in (queries, keys_all, d_mixed)
                )
                probs = head_probs(
                    query, keys_all, distance, same, head_slope(2 * pair + head, per_pack)
                )
                d_probs = dot_right(d_head, values_all)
                carried = jnp.sum(probs * d_probs, axis=-1, keepdims=True)
                d_scores = (probs * (d_probs - carried)).astype(BF16)
                contract = (((0,), (0,)), ((), ()))
                parts = (
                    jnp.dot(d_scores, key, preferred_element_type=F32),
                    lax.dot_general(d_scores, query, contract, preferred_element_type=F32),
                    lax.dot_general(
                        probs.astype(BF16), d_head, contract, preferred_element_type=F32
                    ),
                )
                total = [p if t is None else t + p for t, p in zip(total, parts)]
            wide[rows, cols(0)] = (total[0] * HD ** (-0.5)).astype(BF16)
            wide[rows, cols(D)] = (total[1] * HD ** (-0.5)).astype(BF16)
            wide[rows, cols(2 * D)] = total[2].astype(BF16)

    zl(0)
    zz(1)
    attend_back(0, 0, 4)
    xz(2)
    attend_back(0, 4, 8)
    zl(1)
    attend_back(1, 0, 4)
    yx(4)
    zz(2)
    attend_back(1, 4, 8)
    xz(3)
    qkv_half = 3 * D // n_c
    qkv_view = wide_far.at[:, pl.ds(0, qkv_half)]
    qkv_away = remote(wide.at[:, far_half(qkv_half)], qkv_view, qkv_view, other_core)
    for part in range(6):
        add_product(wide[:, pl.ds(part * 512, 512)], ring_next(), part == 0)
        ring_load()
    zl(2)
    one_away.wait_recv()
    qkv_away.wait_recv()
    for u in (7, 8):
        product(u, tiles(pool.at[0], near, D), tiles(left_far, near, 0), wide, wide_far)
        x_send(u)
    packed_here = local(packed, pool.at[0, near])
    hat_copy.wait()
    after_away.wait_send()
    gain_one = gain_row(0)

    def base_body(at):
        back, grad_gain = norm_back(
            hat[at, :].astype(F32), scales[at, pl.ds(0, 1)], gain_one, acc[at, :]
        )
        low[at, :] = (hidden[at, :] + back).astype(BF16)
        add_gain(0, grad_gain)

    row_loop(tokens, 64, base_body)
    zz(3)
    xz(6)
    base_away = remote(low.at[:, far_half(D // n_c)], low_far, low_far, other_core)
    gain_step(0)
    qkv_away.wait_send()
    for half in range(2):
        pair = (ring_next(), ring_next())
        for start in (0, 512):
            cols = pl.ds(start, 512)
            value = dot_right(low[:, :512], pair[0][cols, :])
            value += dot_right(low[:, 512:], pair[1][cols, :])
            wide[:, pl.ds(half * 1024 + start, 512)] = value.astype(BF16)
        ring_load()
        ring_load()
    xz(4)
    zl(3)
    packed_here.wait()
    packed_away.wait_recv()
    base_away.wait_recv()
    for u in (9, 11):
        product(u, tiles(pool.at[0], near, 0), tiles(pool.at[0], far, 0), low, low_far, 2)
    zz(6)
    yx(5)
    for u in (9, 10, 11, 12):
        x_send(u)
    zz(4)
    zl(6)
    for i in range(micro):
        offset, length = spots[i]
        for source in range(n_dp):
            at = pl.ds(i * slab + source * slots, slots)
            block = hot_block((slots, per_pack), 0, offset[source], length[source])
            for half in range(2):
                cols = pl.ds(half * 1024, 1024)
                pool[1, at, cols] = jnp.dot(
                    block, wide[pl.ds(i * per_pack, per_pack), cols], preferred_element_type=F32
                ).astype(BF16)
    gain_step(1)
    frames = []

    def slot(group, base=0):
        return pl.ds(pl.multiple_of(base + group * slots, 16), slots)

    for k in range(1, n_dp):
        to, back = turn(dp, k, n_dp), turn(dp, -k, n_dp)
        for i in range(micro):
            frames.append(
                remote(
                    pool.at[1, slot(to, i * slab)], returned.at[i, slot(dp)],
                    returned.at[i, slot(back)], (to, fsdp),
                )
            )
    own_frames = [local(pool.at[1, slot(dp, i * slab)], returned.at[i, slot(dp)]) for i in range(micro)]
    outgoing = []
    small[fsdp, :, pl.ds(256, 128)] = jnp.zeros((8, 128), F32)

    def add_squares(m):
        rows, columns = finals[m].shape
        chunk = min(32, rows)

        @pl.loop(0, rows // chunk)
        def _(i):
            at = pl.ds(pl.multiple_of(i * chunk, chunk), chunk)
            for first in range(0, columns, 1024):
                value = finals[m][at, pl.ds(first, 1024)].astype(F32)
                value = (value * value).reshape(chunk // 8, 8, 8, 128)
                small[fsdp, :, pl.ds(256, 128)] += jnp.sum(value, axis=(0, 2))

    def close(m):
        for u in range(len(units)):
            if units[u][0] == m:
                state[u]["core"].wait_recv()
        outgoing.append(local(finals[m], outs[m]))
        add_squares(m)

    steps = [
        (xz, 7), (zl, 4), (last_add, 0), (last_add, 1), (zz, 7), (last_add, 2), (last_add, 3), (xz, 8),
        (zl, 7), (last_add, 6), (close, 4), (zz, 8), (xz, 5), (close, 2), (zl, 8), (xz, 9), (zz, 5),
        (xz, 10), (zz, 9), (zl, 5), (xz, 11), (zz, 10), (zl, 9), (xz, 12), (zz, 11), (zl, 10), (zz, 12),
        (zl, 11), (last_add, 4), (last_add, 7), (zl, 12), (last_add, 8), (last_add, 5), (close, 1),
        (last_add, 9), (close, 3), (last_add, 10), (last_add, 11), (last_add, 12), (close, 0),
    ]
    for index, (do, u) in enumerate(steps):
        do(u)
        if index > 14 and index % 4 == 0 and index // 4 - 2 <= len(dp_partners):
            gain_step(index // 4 - 2)
    small[fsdp, :, pl.ds(0, 256)] = gain_buf[len(dp_partners)]
    view = small.at[fsdp]
    tail = []
    for k in range(1, n_fsdp):
        to, back = turn(fsdp, k, n_fsdp), turn(fsdp, -k, n_fsdp)
        tail.append(remote(view, view, small.at[back], (dp, to)))
    for copy in tail:
        copy.wait_recv()
    total = small[0]
    for f in range(1, n_fsdp):
        total = total + small[f]
    small_total[...] = total
    outgoing.append(local(small_total, small_out))
    for copy in frames:
        copy.wait_recv()
    for copy in own_frames + outgoing:
        copy.wait()
    for copy in copies.sent:
        copy.wait_send()


def backward_all(items, fulls, saved, cotangent, gains_all, micro, slab):
    dims = sizes()
    n_y, n_c, n_a, n_b = dims
    n_fsdp = n_a * n_b
    tokens = cotangent.shape[0]
    per_pack = tokens // micro
    shapes = [full.shape for full in fulls]
    shape = jax.ShapeDtypeStruct
    anywhere = pl.BlockSpec(memory_space=pl.ANY)
    inside = pl.BlockSpec(memory_space=pltpu.VMEM)
    scalars = pl.BlockSpec(memory_space=pltpu.SMEM)
    steps = (n_y * n_c).bit_length() - 1
    scratch = [pltpu.VMEM((n_a, n_b, r // n_fsdp, w // n_c), BF16) for r, w in shapes]
    scratch += [pltpu.VMEM((r // n_fsdp, w), BF16) for r, w in shapes]
    scratch += [
        pltpu.VMEM((2, 2 * tokens, FF // 2), BF16),
        pltpu.VMEM((tokens, D // n_c), BF16),
        pltpu.VMEM((tokens, FF), BF16),
        pltpu.VMEM((tokens, FF // n_c), BF16),
        pltpu.VMEM((tokens, D), BF16),
        pltpu.VMEM((RING, 1024, 512), BF16),
        pltpu.VMEM((2, tokens, 512), BF16),
        pltpu.VMEM((tokens, D), F32),
        pltpu.VMEM((tokens, D), F32),
        pltpu.VMEM((tokens, D), BF16),
        pltpu.VMEM((tokens, D), BF16),
        pltpu.VMEM((tokens, D), BF16),
        pltpu.VMEM((steps + 1, 8, 256), F32),
        pltpu.VMEM((steps, 8, 256), F32),
        pltpu.VMEM((n_fsdp, 8, 384), F32),
        pltpu.VMEM((8, 384), F32),
    ]
    for m, part, parts, shared in REDUCE_UNITS:
        rows, width = shapes[m][0] // n_fsdp, shapes[m][1] // n_c // parts
        if shared:
            step = width // n_y
            scratch += [
                pltpu.VMEM((n_y - 1, n_a, n_b, rows, step), BF16),
                pltpu.VMEM((n_b - 1, n_a, rows, step), BF16),
                pltpu.VMEM((3, rows, step), BF16),
            ]
        else:
            scratch += [
                pltpu.VMEM((n_b - 1, n_a, rows, width), BF16),
                pltpu.VMEM((3, rows, width), BF16),
                pltpu.VMEM((1 if n_y == 2 else n_y, rows, width), BF16),
            ]
    total = 10 + micro * (n_y * n_c - 1) + steps + n_fsdp - 1
    for _, _, _, shared in REDUCE_UNITS:
        total += (n_b - 1) + (n_a - 1) + (n_y - 1) + 1 + (n_y - 1 if shared else 0)
    scratch += [
        pltpu.SemaphoreType.DMA((total,)),
        pltpu.SemaphoreType.DMA((total,)),
        pltpu.SemaphoreType.DMA((72,)),
        pltpu.SemaphoreType.REGULAR((2,)),
    ]
    out_shape = [shape((r // n_fsdp, w), BF16) for r, w in shapes]
    out_shape += [
        shape((micro, slab, 2 * D), BF16), shape((8, 384), F32),
    ]
    results = pl.pallas_call(
        partial(backward_kernel, dims, shapes),
        out_shape=out_shape,
        in_specs=[anywhere] * 14 + [inside] + [anywhere] * 3 + [inside, anywhere, inside]
        + [scalars] * 3,
        out_specs=[anywhere] * len(out_shape),
        scratch_shapes=scratch,
        compiler_params=pltpu.CompilerParams(
            collective_id=1, has_side_effects=True, vmem_limit_bytes=VMEM_LIMIT
        ),
        name="backward_and_reduce",
    )(
        *fulls, *saved, cotangent, gains_all, *items[:3],
    )
    return results


def adam_update(master, first, second, gradient, rate, decay):
    first_new = BETA_FIRST * first + (1.0 - BETA_FIRST) * gradient
    second_new = BETA_SECOND * second + (1.0 - BETA_SECOND) * gradient * gradient
    first_hat = first_new / (1.0 - BETA_FIRST**STEP)
    second_hat = second_new / (1.0 - BETA_SECOND**STEP)
    master_new = master - rate * (
        first_hat / (jnp.sqrt(second_hat) + ADAM_EPSILON) + decay * master
    )
    return (master_new, first_new, second_new)


def item_at(items, i, source, slot, n_dp):
    return items[0, i, source, slot]


def plan_send(lengths, packs, i, dp, n_dp):
    starts, counts = [], []
    lows = [item_at(lengths, i, dp, j, n_dp) for j in range(n_dp)]
    targets = [item_at(packs, i, dp, j, n_dp) for j in range(n_dp)]
    for pack in range(n_dp):
        start, taken, before = jnp.int32(0), jnp.int32(0), jnp.int32(0)
        for low, target in zip(lows, targets):
            hit = target == pack
            start += jnp.where(hit, before, 0)
            taken += jnp.where(hit, low, 0)
            before += low
        starts.append(start)
        counts.append(taken)
    return starts, counts


def plan_pack(values, packs, i, dp, n_dp):
    result = []
    for source in range(n_dp):
        total = jnp.int32(0)
        for j in range(n_dp):
            hit = item_at(packs, i, source, j, n_dp) == dp
            total += jnp.where(hit, item_at(values, i, source, j, n_dp), 0)
        result.append(total)
    return result


def hot_block(shape, slot_dim, start, count):
    slot = lax.broadcasted_iota(jnp.int32, shape, slot_dim)
    row = lax.broadcasted_iota(jnp.int32, shape, 1 - slot_dim)
    return jnp.where((row == start + slot) & (slot < count), 1.0, 0.0).astype(BF16)


def spans(shape, dim, offsets, lengths, values):
    at = lax.broadcasted_iota(jnp.int32, shape, dim)
    total = jnp.zeros(shape, jnp.int32)
    for offset, length, value in zip(offsets, lengths, values):
        total += jnp.where((at >= offset) & (at < offset + length), value, 0)
    return total


def same_item(offsets, lengths, rows):
    ids = list(range(len(offsets)))
    return spans((rows, 1), 0, offsets, lengths, ids) == spans((1, rows), 1, offsets, lengths, ids)


DEPTH = 3


def update_kernel(dims, shapes, *refs):
    n_y, n_c, n_a, n_b = dims
    n_dp, n_fsdp = n_y * n_c, n_a * n_b
    lengths, packs, returned, small, gains, gains_first, gains_second = refs[:7]
    refs = refs[7:]
    masters, firsts, seconds, gradients, refs = refs[:5], refs[5:10], refs[10:15], refs[15:20], refs[20:]
    input_out, skip_out, norm_out, gains_out, gains_first_out, gains_second_out = refs[:6]
    refs = refs[6:]
    outs, refs = [refs[4 * m : 4 * m + 4] for m in range(5)], refs[20:]
    came, back, hot, taken, taken_low, given, given_low, in_sem, out_sem, frame_sem = refs
    dp, fsdp = lax.axis_index("dp"), lax.axis_index("fsdp")
    micro, slab, _ = returned.shape
    slots = slab // n_dp
    source_rows = input_out.shape[1]

    pieces = []
    for m, (rows, columns) in enumerate(shapes):
        step = min(128, rows)
        for row in range(0, rows, step):
            for column in range(0, columns, 1024):
                pieces.append((m, pl.ds(row, step), pl.ds(column, 1024), step))

    def take(k):
        m, rows, columns, step = pieces[k]
        slot, at = k % DEPTH, pl.ds(0, step)
        result = [
            pltpu.make_async_copy(
                ref.at[rows, columns], taken.at[slot, index, at], in_sem.at[slot, index]
            )
            for index, ref in enumerate((masters[m], firsts[m], seconds[m]))
        ]
        result.append(
            pltpu.make_async_copy(
                gradients[m].at[rows, columns], taken_low.at[slot, at], in_sem.at[slot, 3]
            )
        )
        return result

    def give(k):
        m, rows, columns, step = pieces[k]
        slot, at = k % DEPTH, pl.ds(0, step)
        result = [
            pltpu.make_async_copy(
                given.at[slot, index, at], outs[m][index].at[rows, columns], out_sem.at[slot, index]
            )
            for index in range(3)
        ]
        result.append(
            pltpu.make_async_copy(
                given_low.at[slot, at], outs[m][3].at[rows, columns], out_sem.at[slot, 3]
            )
        )
        return result

    for k in range(DEPTH):
        for copy in take(k):
            copy.start()
    frame_copies = [
        pltpu.make_async_copy(returned.at[i], came.at[i], frame_sem.at[i]) for i in range(micro)
    ]
    for copy in frame_copies:
        copy.start()

    values = small[:, pl.ds(0, 256)]
    squares = jnp.sum(small[:, pl.ds(256, 128)]) + jnp.sum(values * values)
    norm = jnp.sqrt(jnp.full((1, 128), squares, F32))
    norm_out[...] = norm
    param_count = 6 * D * D + 2 * D * FF + 2 * D
    clip = jnp.minimum(1.0, 0.02 * math.sqrt(param_count) / norm)[:, :1]

    own = D // n_fsdp
    own_gradient = jnp.zeros((2, own), F32)
    for f in range(n_fsdp):
        part, lane = f * own // 256, f * own % 256
        value = jnp.concatenate(
            [small[pl.ds(4 * row + part, 1), pl.ds(lane, own)] for row in range(2)], axis=0
        )
        own_gradient += jnp.where(fsdp == f, value, 0.0)
    new = adam_update(gains[...], gains_first[...], gains_second[...], clip * own_gradient, 0.3, 0.0)
    gains_out[...], gains_first_out[...], gains_second_out[...] = new

    out_frames = []

    def frames(i):
        starts, counts = plan_send(lengths, packs, i, dp, n_dp)
        for pack in range(n_dp):
            hot[:, pl.ds(pack * slots, slots)] = hot_block(
                (source_rows, slots), 1, starts[pack], counts[pack]
            )
        frame_copies[i].wait()
        for half, target in enumerate((input_out, skip_out)):
            columns = pl.ds(half * D, D)
            back[i, :, columns] = jnp.dot(
                hot[...], came[i, :, columns], preferred_element_type=F32
            ).astype(BF16)
            copy = pltpu.make_async_copy(
                back.at[i, :, columns], target.at[i], frame_sem.at[micro + 2 * i + half]
            )
            copy.start()
            out_frames.append(copy)

    rates = [0.5 / math.sqrt(fan_in) for fan_in in (2 * D, D, D // 16, D, FF)]
    for k, (m, _, _, step) in enumerate(pieces):
        slot = k % DEPTH
        for copy in take(k):
            copy.wait()
        if k >= DEPTH:
            for copy in give(k - DEPTH):
                copy.wait()

        def body(at, m=m, slot=slot):
            new = adam_update(
                taken[slot, 0, at, :], taken[slot, 1, at, :], taken[slot, 2, at, :],
                clip * taken_low[slot, at, :].astype(F32), rates[m], WEIGHT_DECAY,
            )
            for index in range(3):
                given[slot, index, at, :] = new[index]
            given_low[slot, at, :] = new[0].astype(BF16)

        row_loop(step, min(16, step), body)
        for copy in give(k):
            copy.start()
        if k + DEPTH < len(pieces):
            for copy in take(k + DEPTH):
                copy.start()
        if k in (1, 3):
            frames(k // 2)
    for k in range(max(0, len(pieces) - DEPTH), len(pieces)):
        for copy in give(k):
            copy.wait()
    for copy in out_frames:
        copy.wait()


def update_all(lengths, packs, returned, small, gain_arrays, masters, firsts, seconds, gradients, source_rows):
    dims = sizes()
    micro, slab, _ = returned.shape
    shape = jax.ShapeDtypeStruct
    shapes = [master.shape for master in masters]
    anywhere = pl.BlockSpec(memory_space=pl.ANY)
    inside = pl.BlockSpec(memory_space=pltpu.VMEM)
    scalars = pl.BlockSpec(memory_space=pltpu.SMEM)
    out_shape = [shape((micro, source_rows, D), BF16)] * 2 + [shape((1, 128), F32)]
    out_shape += [shape(gain_arrays[0].shape, F32)] * 3
    for s in shapes:
        out_shape += [shape(s, F32)] * 3 + [shape(s, BF16)]
    return pl.pallas_call(
        partial(update_kernel, dims, shapes),
        out_shape=out_shape,
        in_specs=[scalars] * 2 + [anywhere] + [inside] * 4 + [anywhere] * 20,
        out_specs=[anywhere] * 2 + [inside] * 4 + [anywhere] * 20,
        scratch_shapes=[
            pltpu.VMEM((micro, slab, 2 * D), BF16),
            pltpu.VMEM((micro, source_rows, 2 * D), BF16),
            pltpu.VMEM((source_rows, slab), BF16),
            pltpu.VMEM((DEPTH, 3, 128, 1024), F32),
            pltpu.VMEM((DEPTH, 128, 1024), BF16),
            pltpu.VMEM((DEPTH, 3, 128, 1024), F32),
            pltpu.VMEM((DEPTH, 128, 1024), BF16),
            pltpu.SemaphoreType.DMA((DEPTH, 4)),
            pltpu.SemaphoreType.DMA((DEPTH, 4)),
            pltpu.SemaphoreType.DMA((3 * micro,)),
        ],
        compiler_params=pltpu.CompilerParams(vmem_limit_bytes=VMEM_LIMIT),
        name="update",
    )(lengths, packs, returned, small, *gain_arrays, *masters, *firsts, *seconds, *gradients)


def on_device(
    x_source, skip_source, out_cotangent, item_length, item_pack, item_offset, item_count,
    gains, w_skip, w_qkv, w_out, w_up, w_down,
    gains_first, first_skip, first_qkv, first_out, first_up, first_down,
    gains_second, second_skip, second_qkv, second_out, second_up, second_down,
):
    micro, source_rows, width = x_source.shape
    row_count = out_cotangent.shape[1]
    rows = micro * row_count
    items = (item_length, item_pack, item_offset, item_count)
    masters = (w_skip, w_qkv, w_out, w_up, w_down)
    cotangent = out_cotangent.reshape(rows, width)
    results = forward_all(items, masters, x_source, skip_source, gains, cotangent)
    fulls, saved, out_frames, gains_all = results[:5], results[5:19], results[19], results[20]
    fulls = [full.reshape(-1, full.shape[-1]) for full in fulls]
    results = backward_all(items, fulls, saved, cotangent, gains_all, micro, source_rows)
    gradients, returned, small = results[:5], results[5], results[6]
    results = update_all(
        items[0], items[1], returned, small, (gains, gains_first, gains_second), masters,
        (first_skip, first_qkv, first_out, first_up, first_down),
        (second_skip, second_qkv, second_out, second_up, second_down), gradients, source_rows,
    )
    input_gradient, skip_gradient, norm = results[:3]
    return (
        out_frames.reshape(micro, row_count, width), input_gradient, skip_gradient, norm[0, :1],
        *results[3:],
    )


def solution(mesh):
    frames = P(None, ("dp", "fsdp"), None)
    plan = P("fsdp", None, None, None)
    gain, weight = P(None, "fsdp"), P("fsdp", None)
    return jax.shard_map(
        on_device,
        mesh=mesh,
        in_specs=(frames,) * 3 + (plan,) * 4 + ((gain,) + (weight,) * 5) * 3,
        out_specs=(frames,) * 3 + (P(),) + (gain,) * 3 + (weight,) * 20,
        check_vma=False,
    )
```

```python
from functools import partial
import math

import jax
import jax.numpy as jnp
from jax import lax
from jax.experimental import pallas as pl
from jax.experimental.pallas import tpu as pltpu
from jax.sharding import PartitionSpec as P

D = 1024
HEADS = 16
HD = 64
FF = 4096
STEP = 5
CORES = 2
OUTER = 4

BETA_FIRST = 0.5
BETA_SECOND = 0.5
ADAM_EPSILON = 1e-08
WEIGHT_DECAY = 0.01
NORM_EPSILON = 1e-05

BF16 = jnp.bfloat16
F32 = jnp.float32
MESH = pl.DeviceIdType.MESH

GATHER_UNITS = (
    (0, 0, 2, False), (0, 1, 2, False), (1, 0, 2, True), (1, 1, 2, True), (2, 0, 1, False),
    (3, 0, 2, True), (3, 1, 2, True),
    (4, 0, 4, False), (4, 1, 4, False), (4, 2, 4, False), (4, 3, 4, False),
)
WINDOW, OWN_FIRST = 3, 4
VMEM_LIMIT = 63 * 2**20
REDUCE_UNITS = (
    (4, 0, 4, False), (4, 1, 4, False), (4, 2, 4, False), (4, 3, 4, False),
    (3, 0, 2, True), (3, 1, 2, True), (2, 0, 1, False),
    (1, 0, 2, False), (1, 1, 2, False),
    (0, 0, 4, False), (0, 1, 4, False), (0, 2, 4, False), (0, 3, 4, False),
)


def sizes():
    n_dp, n_fsdp = lax.axis_size("dp"), lax.axis_size("fsdp")
    return n_dp // CORES, CORES, OUTER, n_fsdp // OUTER


def turn(value, step, size):
    return lax.rem(value + (step + size) % size, size)


class Remote:
    def __init__(self, src, dst, land, device, **sems):
        def describe(target):
            return pltpu.make_async_remote_copy(
                src_ref=src, dst_ref=target, device_id=device, device_id_type=MESH, **sems
            )

        self.given, self.describe, self.land, self.left = describe(dst), describe, land, False
        self.given.start()

    def wait_recv(self):
        self.describe(self.land).wait_recv()

    def wait_send(self):
        if not self.left:
            self.given.wait_send()
        self.left = True


class Copies:
    def __init__(self, send_sem, recv_sem, local_sem):
        self.send_sem, self.recv_sem, self.local_sem = send_sem, recv_sem, local_sem
        self.locals, self.sent = 0, []

    def remote(self, src, dst, land, device):
        index = len(self.sent)
        sems = dict(send_sem=self.send_sem.at[index], recv_sem=self.recv_sem.at[index])
        self.sent.append(Remote(src, dst, land, device, **sems))
        return self.sent[-1]

    def local(self, src, dst):
        index = self.locals
        self.locals += 1
        copy = pltpu.make_async_copy(src, dst, self.local_sem.at[index])
        copy.start()
        return copy


def greet(dims, dp, fsdp):
    n_y, n_c, n_a, n_b = dims
    n_dp, n_fsdp = n_y * n_c, n_a * n_b
    barrier = pltpu.get_barrier_semaphore()
    partners = [(turn(dp, k, n_dp), fsdp) for k in range(1, n_dp)]
    partners += [(dp, turn(fsdp, k, n_fsdp)) for k in range(1, n_fsdp)]
    for partner in partners:
        pl.semaphore_signal(barrier, inc=1, device_id=partner, device_id_type=MESH)
    pl.semaphore_wait(barrier, len(partners))


def whole(ref, first=0, width=None):
    n_a, n_b, rows, columns = ref.shape
    width = columns if width is None else width
    return ref[:, :, :, pl.ds(first, width)].reshape(n_a * n_b * rows, width)


def row_loop(rows, chunk, body):
    @pl.loop(0, rows // chunk)
    def _(i):
        body(pl.ds(pl.multiple_of(i * chunk, chunk), chunk))


def norm_into(hidden, gain_row, target, hat, scales, first):
    def body(at):
        centre = hidden[at, :]
        centre = centre - jnp.mean(centre, axis=-1, keepdims=True)
        spread = jnp.mean(centre * centre, axis=-1, keepdims=True)
        scale = lax.rsqrt(spread + NORM_EPSILON)
        normal = centre * scale
        target[at, :] = (normal * gain_row).astype(BF16)
        hat[at, :] = normal.astype(BF16)
        scales[at, pl.ds(first, 64)] = jnp.broadcast_to(scale, (scale.shape[0], 64))

    row_loop(hidden.shape[0], 64, body)


GELU_SCALE = math.sqrt(2.0 / math.pi)


def gelu_and_slope(u):
    square = u * u
    bent = jnp.tanh(GELU_SCALE * (u + 0.044715 * (square * u)))
    half = 0.5 * (1.0 + bent)
    slope = half + (0.5 * GELU_SCALE) * u * (1.0 - bent * bent) * (1.0 + 0.134145 * square)
    return u * half, slope


def head_probs(queries, keys_all, distance, same, slope):
    scores = lax.dot_general(
        queries, keys_all, (((1,), (1,)), ((), ())), preferred_element_type=F32
    )
    scores = jnp.where(same, scores * HD ** (-0.5) - slope * distance, -1e30)
    weights = jnp.exp(scores - jnp.max(scores, axis=-1, keepdims=True))
    return weights / jnp.sum(weights, axis=-1, keepdims=True)


def head_slope(head, columns):
    number = jnp.full((1, columns), head + 1, jnp.int32).astype(F32)
    return jnp.exp2(number * (-8.0 / HEADS))


def pair_mask(rows):
    lane = lax.broadcasted_iota(jnp.int32, (rows, 2 * HD), 1)
    return lane < HD


def forward_kernel(dims, *refs):
    n_y, n_c, n_a, n_b = dims
    lengths, packs, offsets, counts = refs[:4]
    masters, x_source, skip_source, gains, cotangent = refs[4:9], *refs[9:13]
    refs = refs[13:]
    fulls_out, refs = refs[:5], refs[5:]
    packed_out, qkv_out, mixed_out, slope_out, act_out, one_out, two_out = refs[:7]
    hat_one_out, hat_two_out, scales_out, low_out, low_far_out, act_far_out = refs[7:13]
    weights_out, frames_out, gains_out = refs[13:16]
    refs = refs[16:]
    fulls, refs = refs[:5], refs[5:]
    stage, arrived, hot, gains_all, packed, base, one, qkv, mixed, after, two, up, out = refs[:13]
    hat_one, hat_two, scales, slope_buf, weights = refs[13:18]
    send_sem, recv_sem, local_sem = refs[18:]
    dp, fsdp = lax.axis_index("dp"), lax.axis_index("fsdp")
    y, c, a, b = dp // n_c, lax.rem(dp, n_c), fsdp // n_b, lax.rem(fsdp, n_b)
    n_dp, n_fsdp = n_y * n_c, n_a * n_b
    copies = Copies(send_sem, recv_sem, local_sem)
    remote, local = copies.remote, copies.local
    sources = [(qkv, 0), (qkv, 1), (qkv, 2), (mixed, 0)]
    source_copies = []
    for index, (ref, part) in enumerate(sources):
        origin = (x_source, skip_source)[index // 2].at[index % 2]
        source_copies.append(local(origin, ref.at[:, pl.ds(part * D, D)]))
    cot_copy = local(cotangent, out)
    greet(dims, dp, fsdp)
    micro, source_rows = x_source.shape[:2]
    slots = source_rows // n_dp

    staged = {}

    def load(m):
        rows, columns = masters[m].shape
        view = stage.at[m % 2, pl.ds(0, rows * columns // 1024)]
        if columns == 1024:
            staged[m] = [local(masters[m], view)]
        else:
            parts = columns // 1024
            staged[m] = [
                local(
                    masters[m].at[:, pl.ds(p * 1024, 1024)],
                    stage.at[m % 2, pl.ds(p * rows, rows)],
                )
                for p in range(parts)
            ]

    load(0)
    load(1)
    frames = []
    own_frames = []

    def slot(group):
        return pl.ds(pl.multiple_of(group * slots, 16), slots)

    outbound = {
        (0, 0): (packed, 0), (0, 1): (packed, D), (1, 0): (hat_one, 0), (1, 1): (hat_two, 0),
    }

    def make_payload():
        for copy in source_copies:
            copy.wait()
        for i in range(micro):
            starts, taken = plan_send(lengths, packs, i, dp, n_dp)
            for pack in range(n_dp):
                hot[pl.ds(pack * slots, slots), :] = hot_block(
                    (slots, source_rows), 0, starts[pack], taken[pack]
                )
            for half in range(2):
                ref, part = sources[2 * half + i]
                target, first = outbound[i, half]
                target[:, pl.ds(first, D)] = jnp.dot(
                    hot[...], ref[:, pl.ds(part * D, D)], preferred_element_type=F32
                ).astype(BF16)
            for k in range(n_dp):
                to, back = turn(dp, k, n_dp), turn(dp, -k, n_dp)
                for half in range(2):
                    ref, first = outbound[i, half]
                    view = ref.at[slot(to), pl.ds(first, D)]
                    cols = pl.ds(half * D, D)
                    if k == 0:
                        own_frames.append(local(view, arrived.at[i, slot(dp), cols]))
                    else:
                        frames.append(
                            remote(
                                view, arrived.at[i, slot(dp), cols], arrived.at[i, slot(back), cols],
                                (to, fsdp),
                            )
                        )

    def make_gain_rows():
        gains_all[fsdp] = jnp.zeros(gains_all.shape[1:], F32)
        own = gains.shape[1]
        gains_all[fsdp, pl.ds(0, 2), pl.ds(0, own)] = gains[...].astype(BF16).astype(F32)
        for k in range(1, n_fsdp):
            to, back = turn(fsdp, k, n_fsdp), turn(fsdp, -k, n_fsdp)
            gain_copies.append(
                remote(gains_all.at[fsdp], gains_all.at[fsdp], gains_all.at[back], (dp, to))
            )

    gain_copies = []

    units = []
    for m, part, parts, shared in GATHER_UNITS:
        width = masters[m].shape[1] // parts
        units.append((m, part * width, width, shared and width // (n_c * n_y) % 128 == 0))
    state = [{"x": [], "y": [], "c": []} for _ in units]

    def columns(u, of_c, of_y):
        m, first, width, shared = units[u]
        if shared:
            step = width // (n_c * n_y)
            return pl.ds(pl.multiple_of(first + (of_c * n_y + of_y) * step, 128), step)
        step = width // n_c
        return pl.ds(pl.multiple_of(first + of_c * step, 128), step)

    def convert(m):
        for copy in staged[m]:
            copy.wait()
        rows, width = masters[m].shape

        def body(at):
            for p in range(width // 1024):
                low = stage[m % 2, pl.ds(at.start + p * rows, at.size), :].astype(BF16)
                fulls[m][a, b, at, pl.ds(p * 1024, 1024)] = low

        row_loop(rows, 32, body)

    def pass_on(u, name, block, mask):
        full, cols = fulls[units[u][0]], columns(u, c, y)
        view, source = full.at[block, b, :, cols], block ^ mask
        landing = full.at[source, b, :, cols]
        copy = remote(view, view, landing, (dp, (a ^ mask) * n_b + b))
        state[u][name] = (copy, source)

    def stage_z(u):
        pass_on(u, "far", a, 2)
        pass_on(u, "near", a, 1)

    def spread(u, block_a, block_b, of_y, to_y):
        m, first, width, shared = units[u]
        full = fulls[m]
        view = full.at[block_a, block_b, :, columns(u, c, of_y)]
        if to_y and shared:
            for k in range(1, n_y):
                source = turn(y, -k, n_y)
                landing = full.at[block_a, block_b, :, columns(u, c, source)]
                copy = remote(view, view, landing, (turn(y, k, n_y) * n_c + c, fsdp))
                state[u]["y"].append((copy, block_a, block_b, source))
        landing = full.at[block_a, block_b, :, columns(u, 1 - c, of_y)]
        state[u]["c"].append(remote(view, view, landing, (y * n_c + 1 - c, fsdp)))

    def send_x(u, block_a):
        m = units[u][0]
        cols = columns(u, c, y)
        view = fulls[m].at[block_a, b, :, cols]
        for k in range(1, n_b):
            landing = fulls[m].at[block_a, turn(b, -k, n_b), :, cols]
            state[u]["x"].append(remote(view, view, landing, (dp, a * n_b + turn(b, k, n_b))))

    def stage_own(u):
        send_x(u, a)

    def relay(u, name):
        copy, source = state[u][name]
        copy.wait_recv()
        if name == "far":
            pass_on(u, "last", source, 1)
        send_x(u, source)
        spread(u, source, b, y, True)

    def relay_own(u):
        relay(u, "far")
        relay(u, "near")

    def stage_x(u):
        relay_own(u)
        relay(u, "last")

    def stage_s(u):
        for copy in state[u]["x"]:
            copy.wait_recv()
        for k in range(1, n_b):
            spread(u, slice(None), turn(b, -k, n_b), y, True)

    def stage_c(u):
        for copy, block_a, block_b, source in state[u]["y"]:
            copy.wait_recv()
            spread(u, block_a, block_b, source, False)

    outgoing = []

    def finish(u):
        m, first, width, shared = units[u]
        for copy in state[u]["c"]:
            copy.wait_recv()
        cols = pl.ds(first, width)
        outgoing.append(local(fulls[m].at[:, :, :, cols], fulls_out[m].at[:, :, :, cols]))

    for m in range(5):
        convert(m)
        if m + 2 < 5:
            load(m + 2)
        for u in range(len(units)):
            if units[u][0] == m and u < WINDOW:
                stage_z(u)
            if units[u][0] == m and u < OWN_FIRST:
                stage_own(u)
        if m == 0:
            make_payload()
            make_gain_rows()

    count = len(units)

    def comm(u):
        if u < count:
            stage_x(u)
        if u + WINDOW < count:
            stage_z(u + WINDOW)
        if OWN_FIRST <= u + WINDOW < count:
            stage_own(u + WINDOW)
        if u == 6 and WINDOW == 3:
            stage_z(10)
            stage_own(10)
        if u >= 1:
            stage_s(u - 1)

    tokens, width = base.shape
    per_pack = tokens // micro

    def make_packed():
        for copy in frames:
            copy.wait_recv()
        for copy in own_frames:
            copy.wait()
        for copy in frames:
            copy.wait_send()
        for i in range(micro):
            offset, length = plan_pack(offsets, packs, i, dp, n_dp), plan_pack(lengths, packs, i, dp, n_dp)
            spots.append((offset, length))
            at = pl.ds(i * per_pack, per_pack)
            for source in range(n_dp):
                hot[at, pl.ds(source * slots, slots)] = hot_block(
                    (per_pack, slots), 1, offset[source], length[source]
                )
            for half in range(2):
                cols = pl.ds(half * 1024, 1024)
                packed[at, cols] = jnp.dot(
                    hot[at, :], arrived[i, :, cols], preferred_element_type=F32
                ).astype(BF16)
        outgoing.append(local(packed, packed_out))

    spots = []
    gain_rows = []

    def make_gains():
        for copy in gain_copies:
            copy.wait_recv()
        outgoing.append(local(gains_all, gains_out))
        own = D // n_fsdp
        for row in range(2):
            gain_rows.append(
                jnp.concatenate([gains_all[f, pl.ds(row, 1), pl.ds(0, own)] for f in range(n_fsdp)], axis=1)
            )

    def make_base():
        for first in (0, 512):
            base[:, pl.ds(first, 512)] = jnp.dot(
                packed[...], whole(fulls[0], first, 512), preferred_element_type=F32
            )
        norm_into(base, gain_rows[0], one, hat_one, scales, 0)
        outgoing.append(local(hat_one, hat_one_out))
        outgoing.append(local(one, one_out))

    def make_qkv():
        for first in range(0, 3 * D, 512):
            qkv[:, pl.ds(first, 512)] = jnp.dot(
                one[...], whole(fulls[1], first, 512), preferred_element_type=F32
            ).astype(BF16)
        outgoing.append(local(qkv, qkv_out))

    def attend(i, first=0, last=HEADS // 2):
        rows = pl.ds(i * per_pack, per_pack)
        position = lax.broadcasted_iota(jnp.int32, (per_pack, per_pack), 0)
        distance = jnp.abs(
            position - lax.broadcasted_iota(jnp.int32, (per_pack, per_pack), 1)
        ).astype(F32)
        first_head = pair_mask(per_pack)
        same = same_item(*spots[i], per_pack)

        @pl.loop(first, last)
        def _(pair):
            def cols(part):
                return pl.ds(pl.multiple_of(part * D + pair * 2 * HD, 128), 2 * HD)

            queries, keys_all, values_all = (qkv[rows, cols(part)] for part in range(3))
            results = []
            for head in range(2):
                mine = first_head if head == 0 else jnp.logical_not(first_head)
                slope = head_slope(2 * pair + head, per_pack)
                probs = head_probs(
                    jnp.where(mine, queries, jnp.zeros_like(queries)), keys_all, distance, same, slope
                )
                results.append(
                    jnp.dot(probs.astype(BF16), values_all, preferred_element_type=F32)
                )
            mixed[rows, cols(0)] = jnp.where(first_head, results[0], results[1]).astype(BF16)

    def make_after():
        outgoing.append(local(mixed, mixed_out))
        for first in (0, 512):
            cols = pl.ds(first, 512)
            after[:, cols] = base[:, cols] + jnp.dot(
                mixed[...], whole(fulls[2], first, 512), preferred_element_type=F32
            )
        norm_into(after, gain_rows[1], two, hat_two, scales, 64)
        outgoing.append(local(hat_two, hat_two_out))
        outgoing.append(local(scales, scales_out))
        outgoing.append(local(two, two_out))

    slope_copies = [None, None]
    half_ff = FF // 2

    def make_up(j):
        slot_now = j % 2
        cols = pl.ds(j * 512, 512)
        up[...] = jnp.dot(two[...], whole(fulls[3], j * 512, 512), preferred_element_type=F32)
        if slope_copies[slot_now] is not None:
            slope_copies[slot_now].wait()
        half, within = j * 512 // half_ff, j * 512 % half_ff

        def body(at):
            value, slope = gelu_and_slope(up[at, :])
            arrived[half, at, pl.ds(within, 512)] = value.astype(BF16)
            slope_buf[slot_now, at, :] = slope.astype(BF16)

        row_loop(tokens, 64, body)
        slope_copies[slot_now] = local(slope_buf.at[slot_now], slope_out.at[:, cols])

    other_core = (y * n_c + 1 - c, fsdp)
    crossing = []

    def send_act(half):
        cols = pl.ds(half * half_ff, half_ff)
        outgoing.append(local(arrived.at[half], act_out.at[:, cols]))
        there = act_far_out.at[:, cols]
        crossing.append(remote(arrived.at[half], there, there, other_core))

    low_copies = []

    def make_low():
        cot_copy.wait()
        for i in range(micro):
            rows = pl.ds(i * per_pack, per_pack)
            offset, length, count = (
                plan_pack(values, packs, i, dp, n_dp) for values in (offsets, lengths, counts)
            )
            over = spans((per_pack, 1), 0, offset, length, count).astype(F32)
            weight = over / spans((per_pack, 1), 0, offset, length, length).astype(F32)
            weights[rows, :] = jnp.broadcast_to(weight, (per_pack, 128))

        def body(at):
            out[at, :] = (weights[at, pl.ds(0, 1)] * out[at, :].astype(F32)).astype(BF16)

        row_loop(tokens, 64, body)
        outgoing.append(local(weights, weights_out))
        low_copies.append(local(out, low_out))
        step = D // n_c
        others = pl.ds(pl.multiple_of((1 - c) * step, 128), step)
        crossing.append(remote(out.at[:, others], low_far_out, low_far_out, other_core))

    def low_left():
        low_copies[0].wait()
        crossing[0].wait_send()

    def make_out(first, step):
        cols = pl.ds(first, step)
        weight = whole(fulls[4], first, step)
        total = after[:, cols] + jnp.dot(
            arrived[0], weight[:half_ff], preferred_element_type=F32
        )
        total += jnp.dot(arrived[1], weight[half_ff:], preferred_element_type=F32)
        out[:, cols] = total.astype(BF16)

    comm(0)
    comm(1)
    comm(2)
    make_gains()
    make_low()
    comm(3)
    make_packed()
    finish(0)
    finish(1)
    make_base()
    comm(4)
    comm(5)
    comm(6)
    stage_c(2)
    relay_own(7)
    stage_c(3)
    finish(2)
    finish(3)
    make_qkv()
    attend(0, 0, 4)
    relay(7, "last")
    relay_own(8)
    stage_s(6)
    attend(0, 4, 8)
    relay(8, "last")
    relay_own(9)
    attend(1, 0, 4)
    relay(9, "last")
    relay_own(10)
    stage_s(7)
    attend(1, 4, 8)
    relay(10, "last")
    finish(4)
    stage_s(8)
    stage_c(5)
    make_after()
    finish(5)
    make_up(0)
    make_up(1)
    make_up(2)
    make_up(3)
    send_act(0)
    stage_c(6)
    stage_s(9)
    low_left()
    finish(6)
    for j in range(4, 8):
        make_up(j)
    send_act(1)
    finish(7)
    make_out(0, 256)
    stage_s(10)
    finish(8)
    make_out(256, 256)
    finish(9)
    make_out(512, 256)
    finish(10)
    make_out(768, 256)
    outgoing.append(local(out, frames_out))
    for copy in crossing:
        copy.wait_recv()
    for copy in outgoing + slope_copies:
        copy.wait()
    for copy in copies.sent:
        copy.wait_send()


def forward_all(items, masters, x_source, skip_source, gains, cotangent):
    dims = sizes()
    n_y, n_c, n_a, n_b = dims
    n_fsdp = n_a * n_b
    micro, source_rows, _ = x_source.shape
    n_dp = n_y * n_c
    slots = source_rows // n_dp
    tokens = cotangent.shape[0]
    per_pack = tokens // micro
    total = 2 * micro * (n_dp - 1) + n_fsdp - 1 + 3
    for _, _, _, shared in GATHER_UNITS:
        groups = n_a - 1 + n_b - 1
        total += (n_a - 1) + n_a * (n_b - 1)
        total += (n_y - 1) * groups + n_y * groups if shared else groups
    shape = jax.ShapeDtypeStruct
    full_shapes = [(n_a, n_b) + master.shape for master in masters]
    out_shape = [shape(s, BF16) for s in full_shapes]
    out_shape += [
        shape((tokens, 2 * D), BF16), shape((tokens, 3 * D), BF16), shape((tokens, D), BF16),
        shape((tokens, FF), BF16), shape((tokens, FF), BF16),
        shape((tokens, D), BF16), shape((tokens, D), BF16),
        shape((tokens, D), BF16), shape((tokens, D), BF16),
        shape((tokens, 128), F32),
        shape((tokens, D), BF16), shape((tokens, D // n_c), BF16), shape((tokens, FF), BF16),
        shape((tokens, 128), F32), shape((tokens, D), BF16), shape((n_fsdp, 8, 128), F32),
    ]
    anywhere = pl.BlockSpec(memory_space=pl.ANY)
    inside = pl.BlockSpec(memory_space=pltpu.VMEM)
    scalars = pl.BlockSpec(memory_space=pltpu.SMEM)
    stage_rows = max(m.shape[0] * m.shape[1] // 1024 for m in masters)
    results = pl.pallas_call(
        partial(forward_kernel, dims),
        out_shape=out_shape,
        in_specs=[scalars] * 4 + [anywhere] * 7 + [inside, anywhere],
        out_specs=[anywhere] * len(out_shape),
        scratch_shapes=[pltpu.VMEM(s, BF16) for s in full_shapes]
        + [
            pltpu.VMEM((2, stage_rows, 1024), F32),
            pltpu.VMEM((micro, n_dp * slots, 2 * D), BF16),
            pltpu.VMEM((source_rows, source_rows), BF16),
            pltpu.VMEM((n_fsdp, 8, 128), F32),
            pltpu.VMEM((tokens, 2 * D), BF16),
            pltpu.VMEM((tokens, D), F32),
            pltpu.VMEM((tokens, D), BF16),
            pltpu.VMEM((tokens, 3 * D), BF16),
            pltpu.VMEM((tokens, D), BF16),
            pltpu.VMEM((tokens, D), F32),
            pltpu.VMEM((tokens, D), BF16),
            pltpu.VMEM((tokens, 512), F32),
            pltpu.VMEM((tokens, D), BF16),
            pltpu.VMEM((tokens, D), BF16),
            pltpu.VMEM((tokens, D), BF16),
            pltpu.VMEM((tokens, 128), F32),
            pltpu.VMEM((2, tokens, 512), BF16),
            pltpu.VMEM((tokens, 128), F32),
            pltpu.SemaphoreType.DMA((total,)),
            pltpu.SemaphoreType.DMA((total,)),
            pltpu.SemaphoreType.DMA((64,)),
        ],
        compiler_params=pltpu.CompilerParams(
            collective_id=0, has_side_effects=True, vmem_limit_bytes=VMEM_LIMIT
        ),
        name="gather_and_forward",
    )(
        *items, *masters, x_source, skip_source, gains, cotangent,
    )
    return results


def norm_back(hat, scale, gain_row, gradient):
    scaled = gradient * gain_row
    back = scale * (
        scaled
        - jnp.mean(scaled, axis=-1, keepdims=True)
        - hat * jnp.mean(scaled * hat, axis=-1, keepdims=True)
    )
    return back, jnp.sum(gradient * hat, axis=0, keepdims=True)


RING = 4


def backward_kernel(dims, shapes, *refs):
    n_y, n_c, n_a, n_b = dims
    fulls, refs = refs[:5], refs[5:]
    (packed, qkv, mixed, slope, act, one, two, hat_one, hat_two, scales, low_in, low_far_in, act_far,
     frame_weight, cotangent, gains_all, lengths, packs, offsets) = refs[:19]
    refs = refs[19:]
    outs, returned, small_out, refs = refs[:5], refs[5], refs[6], refs[7:]
    sums, finals, refs = refs[:5], refs[5:10], refs[10:]
    (pool, low_far, wide, wide_far, left_far, ring, slope_buf, acc, hidden,
     cot, low, hat, gain_buf, gain_land, small, small_total) = refs[:16]
    refs = refs[16:]
    landing, refs = refs[: 3 * len(REDUCE_UNITS)], refs[3 * len(REDUCE_UNITS) :]
    send_sem, recv_sem, local_sem, credit = refs
    dp, fsdp = lax.axis_index("dp"), lax.axis_index("fsdp")
    y, c, a, b = dp // n_c, lax.rem(dp, n_c), fsdp // n_b, lax.rem(fsdp, n_b)
    n_dp, n_fsdp = n_y * n_c, n_a * n_b
    other_core = (y * n_c + 1 - c, fsdp)
    copies = Copies(send_sem, recv_sem, local_sem)
    remote, local = copies.remote, copies.local
    greet(dims, dp, fsdp)
    tokens = cot.shape[0]
    micro, slab = returned.shape[:2]
    per_pack, slots = tokens // micro, slab // n_dp
    spots = [
        [plan_pack(values, packs, i, dp, n_dp) for values in (offsets, lengths)] for i in range(micro)
    ]
    near, far = pl.ds(0, tokens), pl.ds(tokens, tokens)

    order = []
    for block in range(4):
        order += [(4, block * 1024, 0), (4, block * 1024, 512)]
        order += [(3, 0, block * 1024), (3, 0, block * 1024 + 512)]
    order += [(2, 0, 0), (2, 0, 512)]
    order += [(1, 0, first) for first in range(0, 3 * D, 512)]
    order += [(0, first, second) for first in (0, 1024) for second in (0, 512)]
    ring_copies = {}
    ring_state = [0, 0]

    def ring_load():
        index = ring_state[0]
        if index < len(order):
            m, first, second = order[index]
            ring_copies[index] = local(
                fulls[m].at[pl.ds(first, 1024), pl.ds(second, 512)], ring.at[index % RING]
            )
            ring_state[0] += 1

    def ring_next():
        index = ring_state[1]
        ring_state[1] += 1
        ring_copies.pop(index).wait()
        return ring.at[index % RING]

    def far_half(width):
        return pl.ds(pl.multiple_of((1 - c) * width, 128), width)

    half_ff = FF // 2
    low_copies = [local(low_in, low), local(low_far_in, low_far)]
    act_copies = []
    for half in range(2):
        cols = pl.ds(half * half_ff, half_ff)
        act_copies.append(local(act.at[:, cols], pool.at[half, near]))
        act_copies.append(local(act_far.at[:, cols], pool.at[half, far]))
    for _ in range(RING):
        ring_load()
    slope_copies = {}

    def slope_load(j):
        slope_copies[j] = local(slope.at[:, pl.ds(j * 512, 512)], slope_buf.at[j % 2])

    slope_load(0)
    slope_load(1)
    cot_copy = local(cotangent, cot)
    hat_copy = local(hat_two, hat)
    two_away = remote(two, left_far, left_far, other_core)

    units = []
    for m, part, parts, shared in REDUCE_UNITS:
        width = shapes[m][1] // n_c // parts
        units.append((m, part * width, width, shared))
    state = [{} for _ in units]

    def piece(unit, of_y):
        m, first, width, shared = unit
        if shared:
            step = width // n_y
            return pl.ds(pl.multiple_of(first + of_y * step, 128), step), step
        return pl.ds(first, width), width

    def product(u, left_near, left_other, right_near, right_far, count=1):
        m, first, width, shared = units[u]
        width *= count
        rows = sums[m].shape[2]
        group = max(1, 512 // (n_b * rows))
        tile = group * n_b * rows
        half = shapes[m][1] // n_c
        mine = pl.ds(pl.multiple_of(c * half + first, 128), width)

        @pl.loop(0, n_a // group)
        def _(i):
            contract = (((0,), (0,)), ((), ()))
            value = lax.dot_general(
                left_near(i, tile), right_near[:, mine], contract, preferred_element_type=F32
            )
            value += lax.dot_general(
                left_other(i, tile), right_far[:, pl.ds(first, width)], contract,
                preferred_element_type=F32,
            )
            sums[m][pl.ds(i * group, group), :, :, pl.ds(first, width)] = value.astype(BF16).reshape(
                group, n_b, rows, width
            )

    def tiles(ref, rows, first):
        def pick_tile(i, tile):
            return ref[rows, pl.ds(pl.multiple_of(first + i * tile, 128), tile)]

        return pick_tile

    def pool_tiles(rows):
        def pick_tile(i, tile):
            per = half_ff // tile
            return pool[i // per, rows, pl.ds(pl.multiple_of(lax.rem(i, per) * tile, 128), tile)]

        return pick_tile

    def chunks(outer, rows, body):
        chunk = min(64, rows)
        per = rows // chunk

        @pl.loop(0, outer * per)
        def _(i):
            body(i // per, pl.ds(pl.multiple_of(lax.rem(i, per) * chunk, 16), chunk))


    def y_send(u):
        m, first, width, shared = units[u]
        for k in range(1, n_y):
            cols, step = piece(units[u], turn(y, k, n_y))
            there = landing[3 * u].at[k - 1]
            state[u].setdefault("y", []).append(
                remote(sums[m].at[:, :, :, cols], there, there, (turn(y, k, n_y) * n_c + c, fsdp))
            )

    def y_add(u):
        m = units[u][0]
        for copy in state[u]["y"]:
            copy.wait_recv()
        cols, step = piece(units[u], y)

        def body(outer, rows):
            at = (outer // n_b, lax.rem(outer, n_b), rows, cols)
            value = sums[m][at].astype(F32)
            for k in range(1, n_y):
                value += landing[3 * u][k - 1, outer // n_b, lax.rem(outer, n_b), rows, :].astype(F32)
            sums[m][at] = value.astype(BF16)

        chunks(n_a * n_b, sums[m].shape[2], body)

    def x_land(u):
        return landing[3 * u + 1] if units[u][3] else landing[3 * u]

    def z_land(u):
        return landing[3 * u + 2] if units[u][3] else landing[3 * u + 1]

    def x_send(u):
        m = units[u][0]
        cols, step = piece(units[u], y)
        state[u]["x"] = []
        for k in range(1, n_b):
            there = x_land(u).at[k - 1]
            to = turn(b, k, n_b)
            state[u]["x"].append(
                remote(sums[m].at[:, to, :, cols], there, there, (dp, a * n_b + to))
            )

    def x_add(u):
        m = units[u][0]
        for copy in state[u]["x"]:
            copy.wait_recv()
        cols, step = piece(units[u], y)

        def body(outer, rows):
            value = sums[m][outer, b, rows, cols].astype(F32)
            for k in range(1, n_b):
                value += x_land(u)[k - 1, outer, rows, :].astype(F32)
            sums[m][outer, b, rows, cols] = value.astype(BF16)

        chunks(n_a, sums[m].shape[2], body)

    def z_send(u):
        m = units[u][0]
        cols, step = piece(units[u], y)
        device = (dp, (a ^ 1) * n_b + b)
        state[u]["z"] = []
        for slot_at, block in ((0, a ^ 1), (1, a ^ 3)):
            there = z_land(u).at[slot_at]
            state[u]["z"].append(remote(sums[m].at[block, b, :, cols], there, there, device))

    def zz(u):
        m = units[u][0]
        for copy in state[u]["z"]:
            copy.wait_recv()
        cols, step = piece(units[u], y)

        def body(outer, rows):
            block = a ^ (2 * outer)
            value = sums[m][block, b, rows, cols].astype(F32)
            value += z_land(u)[outer, rows, :].astype(F32)
            sums[m][block, b, rows, cols] = value.astype(BF16)

        chunks(2, sums[m].shape[2], body)
        there = z_land(u).at[2]
        device = (dp, (a ^ 2) * n_b + b)
        state[u]["w"] = remote(sums[m].at[a ^ 2, b, :, cols], there, there, device)

    def z_add(u):
        m, first, width, shared = units[u]
        state[u]["w"].wait_recv()
        cols, step = piece(units[u], y)
        half = shapes[m][1] // n_c

        def body(outer, rows):
            value = sums[m][a, b, rows, cols].astype(F32) + z_land(u)[2, rows, :].astype(F32)
            if shared:
                at = pl.ds(pl.multiple_of(c * half + first + y * step, 128), step)
                finals[m][rows, at] = value.astype(BF16)
            elif n_y == 2:
                sums[m][a, b, rows, cols] = value.astype(BF16)
            else:
                landing[3 * u + 2][y, rows, :] = value.astype(BF16)

        chunks(1, sums[m].shape[2], body)

    def last_send(u):
        m, first, width, shared = units[u]
        half = shapes[m][1] // n_c
        state[u]["last"] = []
        for k in range(1, n_y):
            device = (turn(y, k, n_y) * n_c + c, fsdp)
            from_y = turn(y, -k, n_y)
            if shared:
                step = width // n_y
                mine = pl.ds(pl.multiple_of(c * half + first + y * step, 128), step)
                theirs = pl.ds(pl.multiple_of(c * half + first + from_y * step, 128), step)
                view = finals[m].at[:, mine]
                state[u]["last"].append(remote(view, view, finals[m].at[:, theirs], device))
            elif n_y == 2:
                view, there = sums[m].at[a, b, :, piece(units[u], y)[0]], landing[3 * u + 2].at[0]
                state[u]["last"].append(remote(view, there, there, device))
            else:
                view = landing[3 * u + 2].at[y]
                state[u]["last"].append(remote(view, view, landing[3 * u + 2].at[from_y], device))

    def last_add(u):
        m, first, width, shared = units[u]
        half = shapes[m][1] // n_c
        for copy in state[u]["last"]:
            copy.wait_recv()
        at = pl.ds(pl.multiple_of(c * half + first, 128), width)
        if not shared:

            def body(outer, rows):
                value = landing[3 * u + 2][0, rows, :].astype(F32)
                if n_y == 2:
                    value += sums[m][a, b, rows, pl.ds(first, width)].astype(F32)
                for k in range(1, n_y if n_y > 2 else 0):
                    value += landing[3 * u + 2][k, rows, :].astype(F32)
                finals[m][rows, at] = value.astype(BF16)

            chunks(1, sums[m].shape[2], body)
        view = finals[m].at[:, at]
        theirs = pl.ds(pl.multiple_of((1 - c) * half + first, 128), width)
        state[u]["core"] = remote(view, view, finals[m].at[:, theirs], other_core)

    def xz(u):
        x_add(u)
        z_send(u)

    def yx(u):
        y_add(u)
        x_send(u)

    def zl(u):
        z_add(u)
        last_send(u)


    masks = [1 << i for i in range(n_y.bit_length() - 1)]
    dp_partners = [other_core] + [((y ^ mask) * n_c + c, fsdp) for mask in masks]
    gain_copies = {}

    def gain_step(step):
        if step > 0:
            gain_copies[step - 1].wait_recv()
            gain_buf[step] = gain_buf[step - 1] + gain_land[step - 1]
        if step < len(dp_partners):
            there = gain_land.at[step]
            gain_copies[step] = remote(gain_buf.at[step], there, there, dp_partners[step])

    def add_gain(row, value):
        for part in range(4):
            gain_buf[0, pl.ds(4 * row + part, 1), :] += value[:, part * 256 : part * 256 + 256]

    def give_credit(index):
        pl.semaphore_signal(credit.at[index], inc=1, device_id=other_core, device_id_type=MESH)


    own = D // n_fsdp

    def gain_row(row):
        return jnp.concatenate(
            [gains_all[f, pl.ds(row, 1), pl.ds(0, own)] for f in range(n_fsdp)], axis=1
        )

    def dot_right(left, right):
        return lax.dot_general(left, right, (((1,), (1,)), ((), ())), preferred_element_type=F32)

    def add_product(left, weight, first):
        for start in (0, 512):
            cols = pl.ds(start, 512)
            value = dot_right(left, weight[cols, :])
            acc[:, cols] = value if first else acc[:, cols] + value

    def feed_forward(block):
        down = (ring_next(), ring_next())
        for part in range(2):
            j = 2 * block + part
            slope_copies[j].wait()
            rows = pl.ds(part * 512, 512)
            d_act = dot_right(low[:, :512], down[0][rows, :])
            d_act += dot_right(low[:, 512:], down[1][rows, :])
            wide[:, pl.ds(j * 512, 512)] = (d_act * slope_buf[j % 2].astype(F32)).astype(BF16)
            if j + 2 < 8:
                slope_load(j + 2)
        ring_load()
        ring_load()
        for part in range(2):
            j = 2 * block + part
            add_product(wide[:, pl.ds(j * 512, 512)], ring_next(), j == 0)
            ring_load()

    for copy in low_copies + act_copies:
        copy.wait()
    for u in (0, 2):
        product(u, pool_tiles(near), pool_tiles(far), low, low_far, 2)
        x_send(u)
        x_send(u + 1)
    give_credit(0)
    left_here = [
        local(two, pool.at[0, near, pl.ds(0, D)]),
        local(one, pool.at[0, near, pl.ds(D, D)]),
    ]
    qkv_here = [
        local(qkv.at[:, pl.ds(0, D)], pool.at[1, near, pl.ds(0, D)]),
        local(qkv.at[:, pl.ds(D, D)], pool.at[1, near, pl.ds(D, D)]),
        local(qkv.at[:, pl.ds(2 * D, D)], pool.at[1, far, pl.ds(0, D)]),
        local(mixed, pool.at[1, far, pl.ds(D, D)]),
    ]
    for block in range(4):
        feed_forward(block)
        if block == 2:
            xz(0)
    pl.semaphore_wait(credit.at[0], 1)
    there = pool.at[0, far, pl.ds(0, D)]
    mixed_away = remote(mixed, there, there, other_core)
    wide_away = remote(wide.at[:, far_half(half_ff)], wide_far, wide_far, other_core)
    hat_copy.wait()
    cot_copy.wait()
    gain_buf[0] = jnp.zeros_like(gain_buf[0])
    gain_two = gain_row(1)

    def after_body(at):
        back, grad_gain = norm_back(
            hat[at, :].astype(F32), scales[at, pl.ds(64, 1)], gain_two, acc[at, :]
        )
        d_after = frame_weight[at, pl.ds(0, 1)] * cot[at, :].astype(F32) + back
        hidden[at, :] = d_after
        low[at, :] = d_after.astype(BF16)
        add_gain(1, grad_gain)

    row_loop(tokens, 64, after_body)
    after_away = remote(low.at[:, far_half(D // n_c)], low_far, low_far, other_core)
    hat_copy = local(hat_one, hat)
    pair = (ring_next(), ring_next())
    for start in (0, 512):
        cols = pl.ds(start, 512)
        value = dot_right(low[:, :512], pair[0][cols, :]) + dot_right(low[:, 512:], pair[1][cols, :])
        cot[:, cols] = value.astype(BF16)
    ring_load()
    ring_load()
    xz(1)
    zz(0)
    for copy in left_here + qkv_here:
        copy.wait()
    two_away.wait_recv()
    wide_away.wait_recv()
    for u in (4, 5):
        product(u, tiles(pool.at[0], near, 0), tiles(left_far, near, 0), wide, wide_far)
        y_send(u)
    mixed_away.wait_recv()
    after_away.wait_recv()
    product(6, tiles(pool.at[1], far, D), tiles(pool.at[0], far, 0), low, low_far)
    give_credit(1)
    x_send(6)
    wide_away.wait_send()
    pl.semaphore_wait(credit.at[1], 1)
    packed_away = remote(packed, pool.at[0, far], pool.at[0, far], other_core)
    one_away = remote(one, left_far, left_far, other_core)

    def attend_back(i, first_pair=0, last_pair=HEADS // 2):
        rows = pl.ds(i * per_pack, per_pack)
        rows_far = pl.ds(tokens + i * per_pack, per_pack)
        position = lax.broadcasted_iota(jnp.int32, (per_pack, per_pack), 0)
        distance = jnp.abs(
            position - lax.broadcasted_iota(jnp.int32, (per_pack, per_pack), 1)
        ).astype(F32)
        first_head = pair_mask(per_pack)
        same = same_item(*spots[i], per_pack)

        @pl.loop(first_pair, last_pair)
        def _(pair):
            def cols(first):
                return pl.ds(pl.multiple_of(first + pair * 2 * HD, 128), 2 * HD)

            queries, keys_all = pool[1, rows, cols(0)], pool[1, rows, cols(D)]
            values_all = pool[1, rows_far, cols(0)]
            d_mixed = cot[rows, cols(0)]
            zero = jnp.zeros_like(queries)
            total = [None, None, None]
            for head in range(2):
                mine = first_head if head == 0 else jnp.logical_not(first_head)
                query, key, d_head = (
                    jnp.where(mine, value, zero) for value in (queries, keys_all, d_mixed)
                )
                probs = head_probs(
                    query, keys_all, distance, same, head_slope(2 * pair + head, per_pack)
                )
                d_probs = dot_right(d_head, values_all)
                carried = jnp.sum(probs * d_probs, axis=-1, keepdims=True)
                d_scores = (probs * (d_probs - carried)).astype(BF16)
                contract = (((0,), (0,)), ((), ()))
                parts = (
                    jnp.dot(d_scores, key, preferred_element_type=F32),
                    lax.dot_general(d_scores, query, contract, preferred_element_type=F32),
                    lax.dot_general(
                        probs.astype(BF16), d_head, contract, preferred_element_type=F32
                    ),
                )
                total = [p if t is None else t + p for t, p in zip(total, parts)]
            wide[rows, cols(0)] = (total[0] * HD ** (-0.5)).astype(BF16)
            wide[rows, cols(D)] = (total[1] * HD ** (-0.5)).astype(BF16)
            wide[rows, cols(2 * D)] = total[2].astype(BF16)

    zl(0)
    zz(1)
    attend_back(0, 0, 4)
    xz(2)
    attend_back(0, 4, 8)
    zl(1)
    attend_back(1, 0, 4)
    yx(4)
    zz(2)
    attend_back(1, 4, 8)
    xz(3)
    qkv_half = 3 * D // n_c
    qkv_view = wide_far.at[:, pl.ds(0, qkv_half)]
    qkv_away = remote(wide.at[:, far_half(qkv_half)], qkv_view, qkv_view, other_core)
    for part in range(6):
        add_product(wide[:, pl.ds(part * 512, 512)], ring_next(), part == 0)
        ring_load()
    zl(2)
    one_away.wait_recv()
    qkv_away.wait_recv()
    for u in (7, 8):
        product(u, tiles(pool.at[0], near, D), tiles(left_far, near, 0), wide, wide_far)
        x_send(u)
    packed_here = local(packed, pool.at[0, near])
    hat_copy.wait()
    after_away.wait_send()
    gain_one = gain_row(0)

    def base_body(at):
        back, grad_gain = norm_back(
            hat[at, :].astype(F32), scales[at, pl.ds(0, 1)], gain_one, acc[at, :]
        )
        low[at, :] = (hidden[at, :] + back).astype(BF16)
        add_gain(0, grad_gain)

    row_loop(tokens, 64, base_body)
    zz(3)
    xz(6)
    base_away = remote(low.at[:, far_half(D // n_c)], low_far, low_far, other_core)
    gain_step(0)
    qkv_away.wait_send()
    for half in range(2):
        pair = (ring_next(), ring_next())
        for start in (0, 512):
            cols = pl.ds(start, 512)
            value = dot_right(low[:, :512], pair[0][cols, :])
            value += dot_right(low[:, 512:], pair[1][cols, :])
            wide[:, pl.ds(half * 1024 + start, 512)] = value.astype(BF16)
        ring_load()
        ring_load()
    xz(4)
    for i in range(micro):
        offset, length = spots[i]
        for source in range(n_dp):
            at = pl.ds(i * slab + source * slots, slots)
            block = hot_block((slots, per_pack), 0, offset[source], length[source])
            for half in range(2):
                cols = pl.ds(half * 1024, 1024)
                pool[1, at, cols] = jnp.dot(
                    block, wide[pl.ds(i * per_pack, per_pack), cols], preferred_element_type=F32
                ).astype(BF16)
    zl(3)
    gain_step(1)
    frames = []

    def slot(group, base=0):
        return pl.ds(pl.multiple_of(base + group * slots, 16), slots)

    for k in range(1, n_dp):
        to, back = turn(dp, k, n_dp), turn(dp, -k, n_dp)
        for i in range(micro):
            frames.append(
                remote(
                    pool.at[1, slot(to, i * slab)], returned.at[i, slot(dp)],
                    returned.at[i, slot(back)], (to, fsdp),
                )
            )
    own_frames = [local(pool.at[1, slot(dp, i * slab)], returned.at[i, slot(dp)]) for i in range(micro)]
    packed_here.wait()
    packed_away.wait_recv()
    base_away.wait_recv()
    for u in (9, 11):
        product(u, tiles(pool.at[0], near, 0), tiles(pool.at[0], far, 0), low, low_far, 2)
    zz(6)
    yx(5)
    for u in (9, 10, 11, 12):
        x_send(u)
    zz(4)
    zl(6)
    outgoing = []
    small[fsdp, :, pl.ds(256, 128)] = jnp.zeros((8, 128), F32)

    def add_squares(m):
        rows, columns = finals[m].shape
        chunk = min(32, rows)

        @pl.loop(0, rows // chunk)
        def _(i):
            at = pl.ds(pl.multiple_of(i * chunk, chunk), chunk)
            for first in range(0, columns, 1024):
                value = finals[m][at, pl.ds(first, 1024)].astype(F32)
                value = (value * value).reshape(chunk // 8, 8, 8, 128)
                small[fsdp, :, pl.ds(256, 128)] += jnp.sum(value, axis=(0, 2))

    def close(m):
        for u in range(len(units)):
            if units[u][0] == m:
                state[u]["core"].wait_recv()
        outgoing.append(local(finals[m], outs[m]))
        add_squares(m)

    steps = [
        (xz, 7), (zl, 4), (last_add, 0), (last_add, 1), (zz, 7), (last_add, 2), (last_add, 3), (xz, 8),
        (zl, 7), (close, 4), (zz, 8), (xz, 5), (zl, 8), (xz, 9), (zz, 5),
        (xz, 10), (zz, 9), (zl, 5), (xz, 11), (zz, 10), (zl, 9), (xz, 12), (zz, 11), (zl, 10), (last_add, 6),
        (zz, 12), (zl, 11), (last_add, 4), (last_add, 7), (close, 2), (zl, 12), (last_add, 8), (last_add, 5),
        (close, 1), (last_add, 9), (close, 3), (last_add, 10), (last_add, 11), (last_add, 12), (close, 0),
    ]
    for index, (do, u) in enumerate(steps):
        do(u)
        if index > 14 and index % 4 == 0 and index // 4 - 2 <= len(dp_partners):
            gain_step(index // 4 - 2)
    small[fsdp, :, pl.ds(0, 256)] = gain_buf[len(dp_partners)]
    view = small.at[fsdp]
    tail = []
    for k in range(1, n_fsdp):
        to, back = turn(fsdp, k, n_fsdp), turn(fsdp, -k, n_fsdp)
        tail.append(remote(view, view, small.at[back], (dp, to)))
    for copy in tail:
        copy.wait_recv()
    total = small[0]
    for f in range(1, n_fsdp):
        total = total + small[f]
    small_total[...] = total
    outgoing.append(local(small_total, small_out))
    for copy in frames:
        copy.wait_recv()
    for copy in own_frames + outgoing:
        copy.wait()
    for copy in copies.sent:
        copy.wait_send()


def backward_all(items, fulls, saved, cotangent, gains_all, micro, slab):
    dims = sizes()
    n_y, n_c, n_a, n_b = dims
    n_fsdp = n_a * n_b
    tokens = cotangent.shape[0]
    per_pack = tokens // micro
    shapes = [full.shape for full in fulls]
    shape = jax.ShapeDtypeStruct
    anywhere = pl.BlockSpec(memory_space=pl.ANY)
    inside = pl.BlockSpec(memory_space=pltpu.VMEM)
    scalars = pl.BlockSpec(memory_space=pltpu.SMEM)
    steps = (n_y * n_c).bit_length() - 1
    scratch = [pltpu.VMEM((n_a, n_b, r // n_fsdp, w // n_c), BF16) for r, w in shapes]
    scratch += [pltpu.VMEM((r // n_fsdp, w), BF16) for r, w in shapes]
    scratch += [
        pltpu.VMEM((2, 2 * tokens, FF // 2), BF16),
        pltpu.VMEM((tokens, D // n_c), BF16),
        pltpu.VMEM((tokens, FF), BF16),
        pltpu.VMEM((tokens, FF // n_c), BF16),
        pltpu.VMEM((tokens, D), BF16),
        pltpu.VMEM((RING, 1024, 512), BF16),
        pltpu.VMEM((2, tokens, 512), BF16),
        pltpu.VMEM((tokens, D), F32),
        pltpu.VMEM((tokens, D), F32),
        pltpu.VMEM((tokens, D), BF16),
        pltpu.VMEM((tokens, D), BF16),
        pltpu.VMEM((tokens, D), BF16),
        pltpu.VMEM((steps + 1, 8, 256), F32),
        pltpu.VMEM((steps, 8, 256), F32),
        pltpu.VMEM((n_fsdp, 8, 384), F32),
        pltpu.VMEM((8, 384), F32),
    ]
    for m, part, parts, shared in REDUCE_UNITS:
        rows, width = shapes[m][0] // n_fsdp, shapes[m][1] // n_c // parts
        if shared:
            step = width // n_y
            scratch += [
                pltpu.VMEM((n_y - 1, n_a, n_b, rows, step), BF16),
                pltpu.VMEM((n_b - 1, n_a, rows, step), BF16),
                pltpu.VMEM((3, rows, step), BF16),
            ]
        else:
            scratch += [
                pltpu.VMEM((n_b - 1, n_a, rows, width), BF16),
                pltpu.VMEM((3, rows, width), BF16),
                pltpu.VMEM((1 if n_y == 2 else n_y, rows, width), BF16),
            ]
    total = 10 + micro * (n_y * n_c - 1) + steps + n_fsdp - 1
    for _, _, _, shared in REDUCE_UNITS:
        total += (n_b - 1) + (n_a - 1) + (n_y - 1) + 1 + (n_y - 1 if shared else 0)
    scratch += [
        pltpu.SemaphoreType.DMA((total,)),
        pltpu.SemaphoreType.DMA((total,)),
        pltpu.SemaphoreType.DMA((72,)),
        pltpu.SemaphoreType.REGULAR((2,)),
    ]
    out_shape = [shape((r // n_fsdp, w), BF16) for r, w in shapes]
    out_shape += [
        shape((micro, slab, 2 * D), BF16), shape((8, 384), F32),
    ]
    results = pl.pallas_call(
        partial(backward_kernel, dims, shapes),
        out_shape=out_shape,
        in_specs=[anywhere] * 14 + [inside] + [anywhere] * 3 + [inside, anywhere, inside]
        + [scalars] * 3,
        out_specs=[anywhere] * len(out_shape),
        scratch_shapes=scratch,
        compiler_params=pltpu.CompilerParams(
            collective_id=1, has_side_effects=True, vmem_limit_bytes=VMEM_LIMIT
        ),
        name="backward_and_reduce",
    )(
        *fulls, *saved, cotangent, gains_all, *items[:3],
    )
    return results


def adam_update(master, first, second, gradient, rate, decay):
    first_new = BETA_FIRST * first + (1.0 - BETA_FIRST) * gradient
    second_new = BETA_SECOND * second + (1.0 - BETA_SECOND) * gradient * gradient
    first_hat = first_new / (1.0 - BETA_FIRST**STEP)
    second_hat = second_new / (1.0 - BETA_SECOND**STEP)
    master_new = master - rate * (
        first_hat / (jnp.sqrt(second_hat) + ADAM_EPSILON) + decay * master
    )
    return (master_new, first_new, second_new)


def item_at(items, i, source, slot, n_dp):
    return items[0, i, source, slot]


def plan_send(lengths, packs, i, dp, n_dp):
    starts, counts = [], []
    lows = [item_at(lengths, i, dp, j, n_dp) for j in range(n_dp)]
    targets = [item_at(packs, i, dp, j, n_dp) for j in range(n_dp)]
    for pack in range(n_dp):
        start, taken, before = jnp.int32(0), jnp.int32(0), jnp.int32(0)
        for low, target in zip(lows, targets):
            hit = target == pack
            start += jnp.where(hit, before, 0)
            taken += jnp.where(hit, low, 0)
            before += low
        starts.append(start)
        counts.append(taken)
    return starts, counts


def plan_pack(values, packs, i, dp, n_dp):
    result = []
    for source in range(n_dp):
        total = jnp.int32(0)
        for j in range(n_dp):
            hit = item_at(packs, i, source, j, n_dp) == dp
            total += jnp.where(hit, item_at(values, i, source, j, n_dp), 0)
        result.append(total)
    return result


def hot_block(shape, slot_dim, start, count):
    slot = lax.broadcasted_iota(jnp.int32, shape, slot_dim)
    row = lax.broadcasted_iota(jnp.int32, shape, 1 - slot_dim)
    return jnp.where((row == start + slot) & (slot < count), 1.0, 0.0).astype(BF16)


def spans(shape, dim, offsets, lengths, values):
    at = lax.broadcasted_iota(jnp.int32, shape, dim)
    total = jnp.zeros(shape, jnp.int32)
    for offset, length, value in zip(offsets, lengths, values):
        total += jnp.where((at >= offset) & (at < offset + length), value, 0)
    return total


def same_item(offsets, lengths, rows):
    ids = list(range(len(offsets)))
    return spans((rows, 1), 0, offsets, lengths, ids) == spans((1, rows), 1, offsets, lengths, ids)


DEPTH = 5


def update_kernel(dims, shapes, *refs):
    n_y, n_c, n_a, n_b = dims
    n_dp, n_fsdp = n_y * n_c, n_a * n_b
    lengths, packs, returned, small, gains, gains_first, gains_second, layer_out = refs[:8]
    refs = refs[8:]
    masters, firsts, seconds, gradients, refs = refs[:5], refs[5:10], refs[10:15], refs[15:20], refs[20:]
    layer_copy, input_out, skip_out, norm_out, gains_out, gains_first_out, gains_second_out = refs[:7]
    refs = refs[7:]
    outs, refs = [refs[4 * m : 4 * m + 4] for m in range(5)], refs[20:]
    came, back, hot, held, taken, taken_low, given, given_low, in_sem, out_sem, frame_sem = refs
    dp, fsdp = lax.axis_index("dp"), lax.axis_index("fsdp")
    micro, slab, _ = returned.shape
    slots = slab // n_dp
    source_rows = input_out.shape[1]

    pieces = []
    for m, (rows, columns) in enumerate(shapes):
        step = min(128, rows)
        for row in range(0, rows, step):
            for column in range(0, columns, 1024):
                pieces.append((m, pl.ds(row, step), pl.ds(column, 1024), step))

    def take(k):
        m, rows, columns, step = pieces[k]
        slot, at = k % DEPTH, pl.ds(0, step)
        result = [
            pltpu.make_async_copy(
                ref.at[rows, columns], taken.at[slot, index, at], in_sem.at[slot, index]
            )
            for index, ref in enumerate((masters[m], firsts[m], seconds[m]))
        ]
        result.append(
            pltpu.make_async_copy(
                gradients[m].at[rows, columns], taken_low.at[slot, at], in_sem.at[slot, 3]
            )
        )
        return result

    def give(k):
        m, rows, columns, step = pieces[k]
        slot, at = k % DEPTH, pl.ds(0, step)
        result = [
            pltpu.make_async_copy(
                given.at[slot, index, at], outs[m][index].at[rows, columns], out_sem.at[slot, index]
            )
            for index in range(3)
        ]
        result.append(
            pltpu.make_async_copy(
                given_low.at[slot, at], outs[m][3].at[rows, columns], out_sem.at[slot, 3]
            )
        )
        return result

    for k in range(DEPTH):
        for copy in take(k):
            copy.start()
    frame_copies = [
        pltpu.make_async_copy(returned.at[i], came.at[i], frame_sem.at[i]) for i in range(micro)
    ]
    for copy in frame_copies:
        copy.start()
    layer_in = pltpu.make_async_copy(layer_out, held, frame_sem.at[3 * micro])
    layer_in.start()

    values = small[:, pl.ds(0, 256)]
    squares = jnp.sum(small[:, pl.ds(256, 128)]) + jnp.sum(values * values)
    norm = jnp.sqrt(jnp.full((1, 128), squares, F32))
    norm_out[...] = norm
    param_count = 6 * D * D + 2 * D * FF + 2 * D
    clip = jnp.minimum(1.0, 0.02 * math.sqrt(param_count) / norm)[:, :1]

    own = D // n_fsdp
    own_gradient = jnp.zeros((2, own), F32)
    for f in range(n_fsdp):
        part, lane = f * own // 256, f * own % 256
        value = jnp.concatenate(
            [small[pl.ds(4 * row + part, 1), pl.ds(lane, own)] for row in range(2)], axis=0
        )
        own_gradient += jnp.where(fsdp == f, value, 0.0)
    new = adam_update(gains[...], gains_first[...], gains_second[...], clip * own_gradient, 0.3, 0.0)
    gains_out[...], gains_first_out[...], gains_second_out[...] = new

    out_frames = []

    def frames(i):
        starts, counts = plan_send(lengths, packs, i, dp, n_dp)
        for pack in range(n_dp):
            hot[:, pl.ds(pack * slots, slots)] = hot_block(
                (source_rows, slots), 1, starts[pack], counts[pack]
            )
        frame_copies[i].wait()
        for half, target in enumerate((input_out, skip_out)):
            columns = pl.ds(half * D, D)
            back[i, :, columns] = jnp.dot(
                hot[...], came[i, :, columns], preferred_element_type=F32
            ).astype(BF16)
            copy = pltpu.make_async_copy(
                back.at[i, :, columns], target.at[i], frame_sem.at[micro + 2 * i + half]
            )
            copy.start()
            out_frames.append(copy)

    rates = [0.5 / math.sqrt(fan_in) for fan_in in (2 * D, D, D // 16, D, FF)]
    for k, (m, _, _, step) in enumerate(pieces):
        slot = k % DEPTH
        for copy in take(k):
            copy.wait()
        if k >= DEPTH:
            for copy in give(k - DEPTH):
                copy.wait()

        def body(at, m=m, slot=slot):
            new = adam_update(
                taken[slot, 0, at, :], taken[slot, 1, at, :], taken[slot, 2, at, :],
                clip * taken_low[slot, at, :].astype(F32), rates[m], WEIGHT_DECAY,
            )
            for index in range(3):
                given[slot, index, at, :] = new[index]
            given_low[slot, at, :] = new[0].astype(BF16)

        row_loop(step, min(16, step), body)
        for copy in give(k):
            copy.start()
        if k + DEPTH < len(pieces):
            for copy in take(k + DEPTH):
                copy.start()
        if k in (1, 3):
            frames(k // 2)
        if k == 2:
            layer_in.wait()
            copy = pltpu.make_async_copy(held, layer_copy, frame_sem.at[3 * micro + 1])
            copy.start()
            out_frames.append(copy)
    for k in range(max(0, len(pieces) - DEPTH), len(pieces)):
        for copy in give(k):
            copy.wait()
    for copy in out_frames:
        copy.wait()


def update_all(lengths, packs, returned, small, gain_arrays, layer_out, masters, firsts, seconds, gradients, source_rows):
    dims = sizes()
    micro, slab, _ = returned.shape
    shape = jax.ShapeDtypeStruct
    shapes = [master.shape for master in masters]
    anywhere = pl.BlockSpec(memory_space=pl.ANY)
    inside = pl.BlockSpec(memory_space=pltpu.VMEM)
    scalars = pl.BlockSpec(memory_space=pltpu.SMEM)
    out_shape = [shape(layer_out.shape, BF16)] + [shape((micro, source_rows, D), BF16)] * 2
    out_shape.append(shape((1, 128), F32))
    out_shape += [shape(gain_arrays[0].shape, F32)] * 3
    for s in shapes:
        out_shape += [shape(s, F32)] * 3 + [shape(s, BF16)]
    return pl.pallas_call(
        partial(update_kernel, dims, shapes),
        out_shape=out_shape,
        in_specs=[scalars] * 2 + [anywhere] + [inside] * 4 + [anywhere] * 21,
        out_specs=[anywhere] * 3 + [inside] * 4 + [anywhere] * 20,
        scratch_shapes=[
            pltpu.VMEM((micro, slab, 2 * D), BF16),
            pltpu.VMEM((micro, source_rows, 2 * D), BF16),
            pltpu.VMEM((source_rows, slab), BF16),
            pltpu.VMEM(layer_out.shape, BF16),
            pltpu.VMEM((DEPTH, 3, 128, 1024), F32),
            pltpu.VMEM((DEPTH, 128, 1024), BF16),
            pltpu.VMEM((DEPTH, 3, 128, 1024), F32),
            pltpu.VMEM((DEPTH, 128, 1024), BF16),
            pltpu.SemaphoreType.DMA((DEPTH, 4)),
            pltpu.SemaphoreType.DMA((DEPTH, 4)),
            pltpu.SemaphoreType.DMA((3 * micro + 2,)),
        ],
        compiler_params=pltpu.CompilerParams(vmem_limit_bytes=VMEM_LIMIT),
        name="update",
    )(lengths, packs, returned, small, *gain_arrays, layer_out, *masters, *firsts, *seconds, *gradients)


def on_device(
    x_source, skip_source, out_cotangent, item_length, item_pack, item_offset, item_count,
    gains, w_skip, w_qkv, w_out, w_up, w_down,
    gains_first, first_skip, first_qkv, first_out, first_up, first_down,
    gains_second, second_skip, second_qkv, second_out, second_up, second_down,
):
    micro, source_rows, width = x_source.shape
    row_count = out_cotangent.shape[1]
    rows = micro * row_count
    items = (item_length, item_pack, item_offset, item_count)
    masters = (w_skip, w_qkv, w_out, w_up, w_down)
    cotangent = out_cotangent.reshape(rows, width)
    results = forward_all(items, masters, x_source, skip_source, gains, cotangent)
    fulls, saved, out_frames, gains_all = results[:5], results[5:19], results[19], results[20]
    fulls = [full.reshape(-1, full.shape[-1]) for full in fulls]
    results = backward_all(items, fulls, saved, cotangent, gains_all, micro, source_rows)
    gradients, returned, small = results[:5], results[5], results[6]
    results = update_all(
        items[0], items[1], returned, small, (gains, gains_first, gains_second),
        out_frames, masters,
        (first_skip, first_qkv, first_out, first_up, first_down),
        (second_skip, second_qkv, second_out, second_up, second_down), gradients, source_rows,
    )
    out_frames, input_gradient, skip_gradient, norm = results[:4]
    return (
        out_frames.reshape(micro, row_count, width), input_gradient, skip_gradient, norm[0, :1],
        *results[4:],
    )


def solution(mesh):
    frames = P(None, ("dp", "fsdp"), None)
    plan = P("fsdp", None, None, None)
    gain, weight = P(None, "fsdp"), P("fsdp", None)
    return jax.shard_map(
        on_device,
        mesh=mesh,
        in_specs=(frames,) * 3 + (plan,) * 4 + ((gain,) + (weight,) * 5) * 3,
        out_specs=(frames,) * 3 + (P(),) + (gain,) * 3 + (weight,) * 20,
        check_vma=False,
    )
```

```python
from functools import partial
import math

import jax
import jax.numpy as jnp
from jax import lax
from jax.experimental import pallas as pl
from jax.experimental.pallas import tpu as pltpu
from jax.sharding import PartitionSpec as P

D = 1024
HEADS = 16
HD = 64
FF = 4096
STEP = 5
CORES = 2
OUTER = 4

BETA_FIRST = 0.5
BETA_SECOND = 0.5
ADAM_EPSILON = 1e-08
WEIGHT_DECAY = 0.01
NORM_EPSILON = 1e-05

BF16 = jnp.bfloat16
F32 = jnp.float32
MESH = pl.DeviceIdType.MESH

GATHER_UNITS = (
    (0, 0, 2, False), (0, 1, 2, False), (1, 0, 2, True), (1, 1, 2, True), (2, 0, 1, False),
    (3, 0, 2, True), (3, 1, 2, True),
    (4, 0, 4, False), (4, 1, 4, False), (4, 2, 4, False), (4, 3, 4, False),
)
WINDOW, OWN_FIRST = 3, 4
VMEM_LIMIT = 63 * 2**20
REDUCE_UNITS = (
    (4, 0, 4, False), (4, 1, 4, False), (4, 2, 4, False), (4, 3, 4, False),
    (3, 0, 2, True), (3, 1, 2, True), (2, 0, 1, False),
    (1, 0, 2, False), (1, 1, 2, False),
    (0, 0, 4, False), (0, 1, 4, False), (0, 2, 4, False), (0, 3, 4, False),
)


def sizes():
    n_dp, n_fsdp = lax.axis_size("dp"), lax.axis_size("fsdp")
    return n_dp // CORES, CORES, OUTER, n_fsdp // OUTER


def turn(value, step, size):
    return lax.rem(value + (step + size) % size, size)


class Remote:
    def __init__(self, src, dst, land, device, **sems):
        def describe(target):
            return pltpu.make_async_remote_copy(
                src_ref=src, dst_ref=target, device_id=device, device_id_type=MESH, **sems
            )

        self.given, self.describe, self.land, self.left = describe(dst), describe, land, False
        self.given.start()

    def wait_recv(self):
        self.describe(self.land).wait_recv()

    def wait_send(self):
        if not self.left:
            self.given.wait_send()
        self.left = True


class Copies:
    def __init__(self, send_sem, recv_sem, local_sem):
        self.send_sem, self.recv_sem, self.local_sem = send_sem, recv_sem, local_sem
        self.locals, self.sent = 0, []

    def remote(self, src, dst, land, device):
        index = len(self.sent)
        sems = dict(send_sem=self.send_sem.at[index], recv_sem=self.recv_sem.at[index])
        self.sent.append(Remote(src, dst, land, device, **sems))
        return self.sent[-1]

    def local(self, src, dst):
        index = self.locals
        self.locals += 1
        copy = pltpu.make_async_copy(src, dst, self.local_sem.at[index])
        copy.start()
        return copy


def greet(dims, dp, fsdp):
    n_y, n_c, n_a, n_b = dims
    n_dp, n_fsdp = n_y * n_c, n_a * n_b
    barrier = pltpu.get_barrier_semaphore()
    partners = [(turn(dp, k, n_dp), fsdp) for k in range(1, n_dp)]
    partners += [(dp, turn(fsdp, k, n_fsdp)) for k in range(1, n_fsdp)]
    for partner in partners:
        pl.semaphore_signal(barrier, inc=1, device_id=partner, device_id_type=MESH)
    pl.semaphore_wait(barrier, len(partners))


def whole(ref, first=0, width=None):
    n_a, n_b, rows, columns = ref.shape
    width = columns if width is None else width
    return ref[:, :, :, pl.ds(first, width)].reshape(n_a * n_b * rows, width)


def row_loop(rows, chunk, body):
    @pl.loop(0, rows // chunk)
    def _(i):
        body(pl.ds(pl.multiple_of(i * chunk, chunk), chunk))


def norm_into(hidden, gain_row, target, hat, scales, first):
    def body(at):
        centre = hidden[at, :]
        centre = centre - jnp.mean(centre, axis=-1, keepdims=True)
        spread = jnp.mean(centre * centre, axis=-1, keepdims=True)
        scale = lax.rsqrt(spread + NORM_EPSILON)
        normal = centre * scale
        target[at, :] = (normal * gain_row).astype(BF16)
        hat[at, :] = normal.astype(BF16)
        scales[at, pl.ds(first, 64)] = jnp.broadcast_to(scale, (scale.shape[0], 64))

    row_loop(hidden.shape[0], 64, body)


GELU_SCALE = math.sqrt(2.0 / math.pi)


def gelu_and_slope(u):
    square = u * u
    bent = jnp.tanh(GELU_SCALE * (u + 0.044715 * (square * u)))
    half = 0.5 * (1.0 + bent)
    slope = half + (0.5 * GELU_SCALE) * u * (1.0 - bent * bent) * (1.0 + 0.134145 * square)
    return u * half, slope


def head_probs(queries, keys_all, distance, same, slope):
    scores = lax.dot_general(
        queries, keys_all, (((1,), (1,)), ((), ())), preferred_element_type=F32
    )
    scores = jnp.where(same, scores * HD ** (-0.5) - slope * distance, -1e30)
    weights = jnp.exp(scores - jnp.max(scores, axis=-1, keepdims=True))
    return weights / jnp.sum(weights, axis=-1, keepdims=True)


def head_slope(head, columns):
    number = jnp.full((1, columns), head + 1, jnp.int32).astype(F32)
    return jnp.exp2(number * (-8.0 / HEADS))


def pair_mask(rows):
    lane = lax.broadcasted_iota(jnp.int32, (rows, 2 * HD), 1)
    return lane < HD


def forward_kernel(dims, *refs):
    n_y, n_c, n_a, n_b = dims
    lengths, packs, offsets, counts = refs[:4]
    masters, x_source, skip_source, gains, cotangent = refs[4:9], *refs[9:13]
    refs = refs[13:]
    fulls_out, refs = refs[:5], refs[5:]
    packed_out, qkv_out, mixed_out, slope_out, act_out, one_out, two_out = refs[:7]
    hat_one_out, hat_two_out, scales_out, low_out, low_far_out, act_far_out = refs[7:13]
    weights_out, frames_out, gains_out = refs[13:16]
    refs = refs[16:]
    fulls, refs = refs[:5], refs[5:]
    stage, arrived, hot, gains_all, packed, base, one, qkv, mixed, after, two, up, out = refs[:13]
    hat_one, hat_two, scales, slope_buf, weights = refs[13:18]
    send_sem, recv_sem, local_sem = refs[18:]
    dp, fsdp = lax.axis_index("dp"), lax.axis_index("fsdp")
    y, c, a, b = dp // n_c, lax.rem(dp, n_c), fsdp // n_b, lax.rem(fsdp, n_b)
    n_dp, n_fsdp = n_y * n_c, n_a * n_b
    copies = Copies(send_sem, recv_sem, local_sem)
    remote, local = copies.remote, copies.local
    sources = [(qkv, 0), (qkv, 1), (qkv, 2), (mixed, 0)]
    source_copies = []
    for index, (ref, part) in enumerate(sources):
        origin = (x_source, skip_source)[index // 2].at[index % 2]
        source_copies.append(local(origin, ref.at[:, pl.ds(part * D, D)]))
    cot_copy = local(cotangent, out)
    greet(dims, dp, fsdp)
    micro, source_rows = x_source.shape[:2]
    slots = source_rows // n_dp

    staged = {}

    def load(m):
        rows, columns = masters[m].shape
        view = stage.at[m % 2, pl.ds(0, rows * columns // 1024)]
        if columns == 1024:
            staged[m] = [local(masters[m], view)]
        else:
            parts = columns // 1024
            staged[m] = [
                local(
                    masters[m].at[:, pl.ds(p * 1024, 1024)],
                    stage.at[m % 2, pl.ds(p * rows, rows)],
                )
                for p in range(parts)
            ]

    load(0)
    load(1)
    frames = []
    own_frames = []

    def slot(group):
        return pl.ds(pl.multiple_of(group * slots, 16), slots)

    outbound = {
        (0, 0): (packed, 0), (0, 1): (packed, D), (1, 0): (hat_one, 0), (1, 1): (hat_two, 0),
    }

    def make_payload():
        for copy in source_copies:
            copy.wait()
        for i in range(micro):
            starts, taken = plan_send(lengths, packs, i, dp, n_dp)
            for pack in range(n_dp):
                hot[pl.ds(pack * slots, slots), :] = hot_block(
                    (slots, source_rows), 0, starts[pack], taken[pack]
                )
            for half in range(2):
                ref, part = sources[2 * half + i]
                target, first = outbound[i, half]
                target[:, pl.ds(first, D)] = jnp.dot(
                    hot[...], ref[:, pl.ds(part * D, D)], preferred_element_type=F32
                ).astype(BF16)
            for k in range(n_dp):
                to, back = turn(dp, k, n_dp), turn(dp, -k, n_dp)
                for half in range(2):
                    ref, first = outbound[i, half]
                    view = ref.at[slot(to), pl.ds(first, D)]
                    cols = pl.ds(half * D, D)
                    if k == 0:
                        own_frames.append(local(view, arrived.at[i, slot(dp), cols]))
                    else:
                        frames.append(
                            remote(
                                view, arrived.at[i, slot(dp), cols], arrived.at[i, slot(back), cols],
                                (to, fsdp),
                            )
                        )

    def make_gain_rows():
        gains_all[fsdp] = jnp.zeros(gains_all.shape[1:], F32)
        own = gains.shape[1]
        gains_all[fsdp, pl.ds(0, 2), pl.ds(0, own)] = gains[...].astype(BF16).astype(F32)
        for k in range(1, n_fsdp):
            to, back = turn(fsdp, k, n_fsdp), turn(fsdp, -k, n_fsdp)
            gain_copies.append(
                remote(gains_all.at[fsdp], gains_all.at[fsdp], gains_all.at[back], (dp, to))
            )

    gain_copies = []

    units = []
    for m, part, parts, shared in GATHER_UNITS:
        width = masters[m].shape[1] // parts
        units.append((m, part * width, width, shared and width // (n_c * n_y) % 128 == 0))
    state = [{"x": [], "y": [], "c": []} for _ in units]

    def columns(u, of_c, of_y):
        m, first, width, shared = units[u]
        if shared:
            step = width // (n_c * n_y)
            return pl.ds(pl.multiple_of(first + (of_c * n_y + of_y) * step, 128), step)
        step = width // n_c
        return pl.ds(pl.multiple_of(first + of_c * step, 128), step)

    def convert(m):
        for copy in staged[m]:
            copy.wait()
        rows, width = masters[m].shape

        def body(at):
            for p in range(width // 1024):
                low = stage[m % 2, pl.ds(at.start + p * rows, at.size), :].astype(BF16)
                fulls[m][a, b, at, pl.ds(p * 1024, 1024)] = low

        row_loop(rows, 32, body)

    def pass_on(u, name, block, mask):
        full, cols = fulls[units[u][0]], columns(u, c, y)
        view, source = full.at[block, b, :, cols], block ^ mask
        landing = full.at[source, b, :, cols]
        copy = remote(view, view, landing, (dp, (a ^ mask) * n_b + b))
        state[u][name] = (copy, source)

    def stage_z(u):
        pass_on(u, "far", a, 2)
        pass_on(u, "near", a, 1)

    def spread(u, block_a, block_b, of_y, to_y):
        m, first, width, shared = units[u]
        full = fulls[m]
        view = full.at[block_a, block_b, :, columns(u, c, of_y)]
        if to_y and shared:
            for k in range(1, n_y):
                source = turn(y, -k, n_y)
                landing = full.at[block_a, block_b, :, columns(u, c, source)]
                copy = remote(view, view, landing, (turn(y, k, n_y) * n_c + c, fsdp))
                state[u]["y"].append((copy, block_a, block_b, source))
        landing = full.at[block_a, block_b, :, columns(u, 1 - c, of_y)]
        state[u]["c"].append(remote(view, view, landing, (y * n_c + 1 - c, fsdp)))

    def send_x(u, block_a):
        m = units[u][0]
        cols = columns(u, c, y)
        view = fulls[m].at[block_a, b, :, cols]
        for k in range(1, n_b):
            landing = fulls[m].at[block_a, turn(b, -k, n_b), :, cols]
            state[u]["x"].append(remote(view, view, landing, (dp, a * n_b + turn(b, k, n_b))))

    def stage_own(u):
        send_x(u, a)

    def relay(u, name):
        copy, source = state[u][name]
        copy.wait_recv()
        if name == "far":
            pass_on(u, "last", source, 1)
        send_x(u, source)
        spread(u, source, b, y, True)

    def relay_own(u):
        relay(u, "far")
        relay(u, "near")

    def stage_x(u):
        relay_own(u)
        relay(u, "last")

    def stage_s(u):
        for copy in state[u]["x"]:
            copy.wait_recv()
        for k in range(1, n_b):
            spread(u, slice(None), turn(b, -k, n_b), y, True)

    def stage_c(u):
        for copy, block_a, block_b, source in state[u]["y"]:
            copy.wait_recv()
            spread(u, block_a, block_b, source, False)

    outgoing = []

    def finish(u):
        m, first, width, shared = units[u]
        for copy in state[u]["c"]:
            copy.wait_recv()
        cols = pl.ds(first, width)
        outgoing.append(local(fulls[m].at[:, :, :, cols], fulls_out[m].at[:, :, :, cols]))

    for m in range(5):
        convert(m)
        if m + 2 < 5:
            load(m + 2)
        for u in range(len(units)):
            if units[u][0] == m and u < WINDOW:
                stage_z(u)
            if units[u][0] == m and u < OWN_FIRST:
                stage_own(u)
        if m == 0:
            make_payload()
            make_gain_rows()

    count = len(units)

    def comm(u):
        if u < count:
            stage_x(u)
        if u + WINDOW < count:
            stage_z(u + WINDOW)
        if OWN_FIRST <= u + WINDOW < count:
            stage_own(u + WINDOW)
        if u == 6 and WINDOW == 3:
            stage_z(10)
            stage_own(10)
        if u >= 1:
            stage_s(u - 1)

    tokens, width = base.shape
    per_pack = tokens // micro

    def make_packed():
        for copy in frames:
            copy.wait_recv()
        for copy in own_frames:
            copy.wait()
        for copy in frames:
            copy.wait_send()
        for i in range(micro):
            offset, length = plan_pack(offsets, packs, i, dp, n_dp), plan_pack(lengths, packs, i, dp, n_dp)
            spots.append((offset, length))
            at = pl.ds(i * per_pack, per_pack)
            for source in range(n_dp):
                hot[at, pl.ds(source * slots, slots)] = hot_block(
                    (per_pack, slots), 1, offset[source], length[source]
                )
            for half in range(2):
                cols = pl.ds(half * 1024, 1024)
                packed[at, cols] = jnp.dot(
                    hot[at, :], arrived[i, :, cols], preferred_element_type=F32
                ).astype(BF16)
        outgoing.append(local(packed, packed_out))

    spots = []
    gain_rows = []

    def make_gains():
        for copy in gain_copies:
            copy.wait_recv()
        outgoing.append(local(gains_all, gains_out))
        own = D // n_fsdp
        for row in range(2):
            gain_rows.append(
                jnp.concatenate([gains_all[f, pl.ds(row, 1), pl.ds(0, own)] for f in range(n_fsdp)], axis=1)
            )

    def make_base():
        for first in (0, 512):
            base[:, pl.ds(first, 512)] = jnp.dot(
                packed[...], whole(fulls[0], first, 512), preferred_element_type=F32
            )
        norm_into(base, gain_rows[0], one, hat_one, scales, 0)
        outgoing.append(local(hat_one, hat_one_out))
        outgoing.append(local(one, one_out))

    def make_qkv():
        for first in range(0, 3 * D, 512):
            qkv[:, pl.ds(first, 512)] = jnp.dot(
                one[...], whole(fulls[1], first, 512), preferred_element_type=F32
            ).astype(BF16)
        outgoing.append(local(qkv, qkv_out))

    def attend(i, first=0, last=HEADS // 2):
        rows = pl.ds(i * per_pack, per_pack)
        position = lax.broadcasted_iota(jnp.int32, (per_pack, per_pack), 0)
        distance = jnp.abs(
            position - lax.broadcasted_iota(jnp.int32, (per_pack, per_pack), 1)
        ).astype(F32)
        first_head = pair_mask(per_pack)
        same = same_item(*spots[i], per_pack)

        @pl.loop(first, last)
        def _(pair):
            def cols(part):
                return pl.ds(pl.multiple_of(part * D + pair * 2 * HD, 128), 2 * HD)

            queries, keys_all, values_all = (qkv[rows, cols(part)] for part in range(3))
            results = []
            for head in range(2):
                mine = first_head if head == 0 else jnp.logical_not(first_head)
                slope = head_slope(2 * pair + head, per_pack)
                probs = head_probs(
                    jnp.where(mine, queries, jnp.zeros_like(queries)), keys_all, distance, same, slope
                )
                results.append(
                    jnp.dot(probs.astype(BF16), values_all, preferred_element_type=F32)
                )
            mixed[rows, cols(0)] = jnp.where(first_head, results[0], results[1]).astype(BF16)

    def make_after():
        outgoing.append(local(mixed, mixed_out))
        for first in (0, 512):
            cols = pl.ds(first, 512)
            after[:, cols] = base[:, cols] + jnp.dot(
                mixed[...], whole(fulls[2], first, 512), preferred_element_type=F32
            )
        norm_into(after, gain_rows[1], two, hat_two, scales, 64)
        outgoing.append(local(hat_two, hat_two_out))
        outgoing.append(local(scales, scales_out))
        outgoing.append(local(two, two_out))

    slope_copies = [None, None]
    half_ff = FF // 2

    def make_up(j):
        slot_now = j % 2
        cols = pl.ds(j * 512, 512)
        up[...] = jnp.dot(two[...], whole(fulls[3], j * 512, 512), preferred_element_type=F32)
        if slope_copies[slot_now] is not None:
            slope_copies[slot_now].wait()
        half, within = j * 512 // half_ff, j * 512 % half_ff

        def body(at):
            value, slope = gelu_and_slope(up[at, :])
            arrived[half, at, pl.ds(within, 512)] = value.astype(BF16)
            slope_buf[slot_now, at, :] = slope.astype(BF16)

        row_loop(tokens, 64, body)
        slope_copies[slot_now] = local(slope_buf.at[slot_now], slope_out.at[:, cols])

    other_core = (y * n_c + 1 - c, fsdp)
    crossing = []

    def send_act(half):
        cols = pl.ds(half * half_ff, half_ff)
        outgoing.append(local(arrived.at[half], act_out.at[:, cols]))
        there = act_far_out.at[:, cols]
        crossing.append(remote(arrived.at[half], there, there, other_core))

    low_copies = []

    def make_low():
        cot_copy.wait()
        for i in range(micro):
            rows = pl.ds(i * per_pack, per_pack)
            offset, length, count = (
                plan_pack(values, packs, i, dp, n_dp) for values in (offsets, lengths, counts)
            )
            over = spans((per_pack, 1), 0, offset, length, count).astype(F32)
            weight = over / spans((per_pack, 1), 0, offset, length, length).astype(F32)
            weights[rows, :] = jnp.broadcast_to(weight, (per_pack, 128))

        def body(at):
            out[at, :] = (weights[at, pl.ds(0, 1)] * out[at, :].astype(F32)).astype(BF16)

        row_loop(tokens, 64, body)
        outgoing.append(local(weights, weights_out))
        low_copies.append(local(out, low_out))
        step = D // n_c
        others = pl.ds(pl.multiple_of((1 - c) * step, 128), step)
        crossing.append(remote(out.at[:, others], low_far_out, low_far_out, other_core))

    def low_left():
        low_copies[0].wait()
        crossing[0].wait_send()

    begun = set()

    def begin_out(first, step):
        cols = pl.ds(first, step)
        weight = whole(fulls[4], first, step)[:half_ff]
        after[:, cols] += jnp.dot(arrived[0], weight, preferred_element_type=F32)
        begun.add(first)

    def make_out(first, step):
        if first not in begun:
            begin_out(first, step)
        cols = pl.ds(first, step)
        weight = whole(fulls[4], first, step)[half_ff:]
        total = after[:, cols] + jnp.dot(arrived[1], weight, preferred_element_type=F32)
        out[:, cols] = total.astype(BF16)

    comm(0)
    comm(1)
    comm(2)
    make_gains()
    make_low()
    comm(3)
    make_packed()
    finish(0)
    finish(1)
    make_base()
    comm(4)
    comm(5)
    comm(6)
    stage_c(2)
    relay_own(7)
    stage_c(3)
    finish(2)
    finish(3)
    make_qkv()
    attend(0, 0, 4)
    relay(7, "last")
    relay_own(8)
    stage_s(6)
    attend(0, 4, 8)
    relay(8, "last")
    relay_own(9)
    attend(1, 0, 4)
    relay(9, "last")
    relay_own(10)
    stage_s(7)
    attend(1, 4, 8)
    relay(10, "last")
    finish(4)
    stage_s(8)
    stage_c(5)
    make_after()
    finish(5)
    make_up(0)
    make_up(1)
    make_up(2)
    make_up(3)
    send_act(0)
    stage_c(6)
    stage_s(9)
    low_left()
    finish(7)
    begin_out(0, 256)
    finish(8)
    begin_out(256, 256)
    finish(6)
    for j in range(4, 8):
        make_up(j)
    send_act(1)
    make_out(0, 256)
    stage_s(10)
    make_out(256, 256)
    finish(9)
    make_out(512, 256)
    finish(10)
    make_out(768, 256)
    outgoing.append(local(out, frames_out))
    for copy in crossing:
        copy.wait_recv()
    for copy in outgoing + slope_copies:
        copy.wait()
    for copy in copies.sent:
        copy.wait_send()


def forward_all(items, masters, x_source, skip_source, gains, cotangent):
    dims = sizes()
    n_y, n_c, n_a, n_b = dims
    n_fsdp = n_a * n_b
    micro, source_rows, _ = x_source.shape
    n_dp = n_y * n_c
    slots = source_rows // n_dp
    tokens = cotangent.shape[0]
    per_pack = tokens // micro
    total = 2 * micro * (n_dp - 1) + n_fsdp - 1 + 3
    for _, _, _, shared in GATHER_UNITS:
        groups = n_a - 1 + n_b - 1
        total += (n_a - 1) + n_a * (n_b - 1)
        total += (n_y - 1) * groups + n_y * groups if shared else groups
    shape = jax.ShapeDtypeStruct
    full_shapes = [(n_a, n_b) + master.shape for master in masters]
    out_shape = [shape(s, BF16) for s in full_shapes]
    out_shape += [
        shape((tokens, 2 * D), BF16), shape((tokens, 3 * D), BF16), shape((tokens, D), BF16),
        shape((tokens, FF), BF16), shape((tokens, FF), BF16),
        shape((tokens, D), BF16), shape((tokens, D), BF16),
        shape((tokens, D), BF16), shape((tokens, D), BF16),
        shape((tokens, 128), F32),
        shape((tokens, D), BF16), shape((tokens, D // n_c), BF16), shape((tokens, FF), BF16),
        shape((tokens, 128), F32), shape((tokens, D), BF16), shape((n_fsdp, 8, 128), F32),
    ]
    anywhere = pl.BlockSpec(memory_space=pl.ANY)
    inside = pl.BlockSpec(memory_space=pltpu.VMEM)
    scalars = pl.BlockSpec(memory_space=pltpu.SMEM)
    stage_rows = max(m.shape[0] * m.shape[1] // 1024 for m in masters)
    results = pl.pallas_call(
        partial(forward_kernel, dims),
        out_shape=out_shape,
        in_specs=[scalars] * 4 + [anywhere] * 7 + [inside, anywhere],
        out_specs=[anywhere] * len(out_shape),
        scratch_shapes=[pltpu.VMEM(s, BF16) for s in full_shapes]
        + [
            pltpu.VMEM((2, stage_rows, 1024), F32),
            pltpu.VMEM((micro, n_dp * slots, 2 * D), BF16),
            pltpu.VMEM((source_rows, source_rows), BF16),
            pltpu.VMEM((n_fsdp, 8, 128), F32),
            pltpu.VMEM((tokens, 2 * D), BF16),
            pltpu.VMEM((tokens, D), F32),
            pltpu.VMEM((tokens, D), BF16),
            pltpu.VMEM((tokens, 3 * D), BF16),
            pltpu.VMEM((tokens, D), BF16),
            pltpu.VMEM((tokens, D), F32),
            pltpu.VMEM((tokens, D), BF16),
            pltpu.VMEM((tokens, 512), F32),
            pltpu.VMEM((tokens, D), BF16),
            pltpu.VMEM((tokens, D), BF16),
            pltpu.VMEM((tokens, D), BF16),
            pltpu.VMEM((tokens, 128), F32),
            pltpu.VMEM((2, tokens, 512), BF16),
            pltpu.VMEM((tokens, 128), F32),
            pltpu.SemaphoreType.DMA((total,)),
            pltpu.SemaphoreType.DMA((total,)),
            pltpu.SemaphoreType.DMA((64,)),
        ],
        compiler_params=pltpu.CompilerParams(
            collective_id=0, has_side_effects=True, vmem_limit_bytes=VMEM_LIMIT
        ),
        name="gather_and_forward",
    )(
        *items, *masters, x_source, skip_source, gains, cotangent,
    )
    return results


def norm_back(hat, scale, gain_row, gradient):
    scaled = gradient * gain_row
    back = scale * (
        scaled
        - jnp.mean(scaled, axis=-1, keepdims=True)
        - hat * jnp.mean(scaled * hat, axis=-1, keepdims=True)
    )
    return back, jnp.sum(gradient * hat, axis=0, keepdims=True)


RING = 4


def backward_kernel(dims, shapes, *refs):
    n_y, n_c, n_a, n_b = dims
    fulls, refs = refs[:5], refs[5:]
    (packed, qkv, mixed, slope, act, one, two, hat_one, hat_two, scales, low_in, low_far_in, act_far,
     frame_weight, cotangent, gains_all, lengths, packs, offsets) = refs[:19]
    refs = refs[19:]
    outs, returned, small_out, refs = refs[:5], refs[5], refs[6], refs[7:]
    sums, finals, refs = refs[:5], refs[5:10], refs[10:]
    (pool, low_far, wide, wide_far, left_far, ring, slope_buf, acc, hidden,
     cot, low, hat, gain_buf, gain_land, small, small_total) = refs[:16]
    refs = refs[16:]
    landing, refs = refs[: 3 * len(REDUCE_UNITS)], refs[3 * len(REDUCE_UNITS) :]
    send_sem, recv_sem, local_sem, credit = refs
    dp, fsdp = lax.axis_index("dp"), lax.axis_index("fsdp")
    y, c, a, b = dp // n_c, lax.rem(dp, n_c), fsdp // n_b, lax.rem(fsdp, n_b)
    n_dp, n_fsdp = n_y * n_c, n_a * n_b
    other_core = (y * n_c + 1 - c, fsdp)
    copies = Copies(send_sem, recv_sem, local_sem)
    remote, local = copies.remote, copies.local
    greet(dims, dp, fsdp)
    tokens = cot.shape[0]
    micro, slab = returned.shape[:2]
    per_pack, slots = tokens // micro, slab // n_dp
    spots = [
        [plan_pack(values, packs, i, dp, n_dp) for values in (offsets, lengths)] for i in range(micro)
    ]
    near, far = pl.ds(0, tokens), pl.ds(tokens, tokens)

    order = []
    for block in range(4):
        order += [(4, block * 1024, 0), (4, block * 1024, 512)]
        order += [(3, 0, block * 1024), (3, 0, block * 1024 + 512)]
    order += [(2, 0, 0), (2, 0, 512)]
    order += [(1, 0, first) for first in range(0, 3 * D, 512)]
    order += [(0, first, second) for first in (0, 1024) for second in (0, 512)]
    ring_copies = {}
    ring_state = [0, 0]

    def ring_load():
        index = ring_state[0]
        if index < len(order):
            m, first, second = order[index]
            ring_copies[index] = local(
                fulls[m].at[pl.ds(first, 1024), pl.ds(second, 512)], ring.at[index % RING]
            )
            ring_state[0] += 1

    def ring_next():
        index = ring_state[1]
        ring_state[1] += 1
        ring_copies.pop(index).wait()
        return ring.at[index % RING]

    def far_half(width):
        return pl.ds(pl.multiple_of((1 - c) * width, 128), width)

    half_ff = FF // 2
    low_copies = [local(low_in, low), local(low_far_in, low_far)]
    act_copies = []
    for half in range(2):
        cols = pl.ds(half * half_ff, half_ff)
        act_copies.append(local(act.at[:, cols], pool.at[half, near]))
        act_copies.append(local(act_far.at[:, cols], pool.at[half, far]))
    for _ in range(RING):
        ring_load()
    slope_copies = {}

    def slope_load(j):
        slope_copies[j] = local(slope.at[:, pl.ds(j * 512, 512)], slope_buf.at[j % 2])

    slope_load(0)
    slope_load(1)
    cot_copy = local(cotangent, cot)
    hat_copy = local(hat_two, hat)
    two_away = remote(two, left_far, left_far, other_core)

    units = []
    for m, part, parts, shared in REDUCE_UNITS:
        width = shapes[m][1] // n_c // parts
        units.append((m, part * width, width, shared))
    state = [{} for _ in units]

    def piece(unit, of_y):
        m, first, width, shared = unit
        if shared:
            step = width // n_y
            return pl.ds(pl.multiple_of(first + of_y * step, 128), step), step
        return pl.ds(first, width), width

    def product(u, left_near, left_other, right_near, right_far, count=1):
        m, first, width, shared = units[u]
        width *= count
        rows = sums[m].shape[2]
        group = max(1, 512 // (n_b * rows))
        tile = group * n_b * rows
        half = shapes[m][1] // n_c
        mine = pl.ds(pl.multiple_of(c * half + first, 128), width)

        @pl.loop(0, n_a // group)
        def _(i):
            contract = (((0,), (0,)), ((), ()))
            value = lax.dot_general(
                left_near(i, tile), right_near[:, mine], contract, preferred_element_type=F32
            )
            value += lax.dot_general(
                left_other(i, tile), right_far[:, pl.ds(first, width)], contract,
                preferred_element_type=F32,
            )
            sums[m][pl.ds(i * group, group), :, :, pl.ds(first, width)] = value.astype(BF16).reshape(
                group, n_b, rows, width
            )

    def tiles(ref, rows, first):
        def pick_tile(i, tile):
            return ref[rows, pl.ds(pl.multiple_of(first + i * tile, 128), tile)]

        return pick_tile

    def pool_tiles(rows):
        def pick_tile(i, tile):
            per = half_ff // tile
            return pool[i // per, rows, pl.ds(pl.multiple_of(lax.rem(i, per) * tile, 128), tile)]

        return pick_tile

    def chunks(outer, rows, body):
        chunk = min(64, rows)
        per = rows // chunk

        @pl.loop(0, outer * per)
        def _(i):
            body(i // per, pl.ds(pl.multiple_of(lax.rem(i, per) * chunk, 16), chunk))


    def y_send(u):
        m, first, width, shared = units[u]
        for k in range(1, n_y):
            cols, step = piece(units[u], turn(y, k, n_y))
            there = landing[3 * u].at[k - 1]
            state[u].setdefault("y", []).append(
                remote(sums[m].at[:, :, :, cols], there, there, (turn(y, k, n_y) * n_c + c, fsdp))
            )

    def y_add(u):
        m = units[u][0]
        for copy in state[u]["y"]:
            copy.wait_recv()
        cols, step = piece(units[u], y)

        def body(outer, rows):
            at = (outer // n_b, lax.rem(outer, n_b), rows, cols)
            value = sums[m][at].astype(F32)
            for k in range(1, n_y):
                value += landing[3 * u][k - 1, outer // n_b, lax.rem(outer, n_b), rows, :].astype(F32)
            sums[m][at] = value.astype(BF16)

        chunks(n_a * n_b, sums[m].shape[2], body)

    def x_land(u):
        return landing[3 * u + 1] if units[u][3] else landing[3 * u]

    def z_land(u):
        return landing[3 * u + 2] if units[u][3] else landing[3 * u + 1]

    def x_send(u):
        m = units[u][0]
        cols, step = piece(units[u], y)
        state[u]["x"] = []
        for k in range(1, n_b):
            there = x_land(u).at[k - 1]
            to = turn(b, k, n_b)
            state[u]["x"].append(
                remote(sums[m].at[:, to, :, cols], there, there, (dp, a * n_b + to))
            )

    def x_add(u):
        m = units[u][0]
        for copy in state[u]["x"]:
            copy.wait_recv()
        cols, step = piece(units[u], y)

        def body(outer, rows):
            value = sums[m][outer, b, rows, cols].astype(F32)
            for k in range(1, n_b):
                value += x_land(u)[k - 1, outer, rows, :].astype(F32)
            sums[m][outer, b, rows, cols] = value.astype(BF16)

        chunks(n_a, sums[m].shape[2], body)

    def z_send(u):
        m = units[u][0]
        cols, step = piece(units[u], y)
        device = (dp, (a ^ 1) * n_b + b)
        state[u]["z"] = []
        for slot_at, block in ((0, a ^ 1), (1, a ^ 3)):
            there = z_land(u).at[slot_at]
            state[u]["z"].append(remote(sums[m].at[block, b, :, cols], there, there, device))

    def zz(u):
        m = units[u][0]
        for copy in state[u]["z"]:
            copy.wait_recv()
        cols, step = piece(units[u], y)

        def body(outer, rows):
            block = a ^ (2 * outer)
            value = sums[m][block, b, rows, cols].astype(F32)
            value += z_land(u)[outer, rows, :].astype(F32)
            sums[m][block, b, rows, cols] = value.astype(BF16)

        chunks(2, sums[m].shape[2], body)
        there = z_land(u).at[2]
        device = (dp, (a ^ 2) * n_b + b)
        state[u]["w"] = remote(sums[m].at[a ^ 2, b, :, cols], there, there, device)

    def z_add(u):
        m, first, width, shared = units[u]
        state[u]["w"].wait_recv()
        cols, step = piece(units[u], y)
        half = shapes[m][1] // n_c

        def body(outer, rows):
            value = sums[m][a, b, rows, cols].astype(F32) + z_land(u)[2, rows, :].astype(F32)
            if shared:
                at = pl.ds(pl.multiple_of(c * half + first + y * step, 128), step)
                finals[m][rows, at] = value.astype(BF16)
            elif n_y == 2:
                sums[m][a, b, rows, cols] = value.astype(BF16)
            else:
                landing[3 * u + 2][y, rows, :] = value.astype(BF16)

        chunks(1, sums[m].shape[2], body)

    def last_send(u):
        m, first, width, shared = units[u]
        half = shapes[m][1] // n_c
        state[u]["last"] = []
        for k in range(1, n_y):
            device = (turn(y, k, n_y) * n_c + c, fsdp)
            from_y = turn(y, -k, n_y)
            if shared:
                step = width // n_y
                mine = pl.ds(pl.multiple_of(c * half + first + y * step, 128), step)
                theirs = pl.ds(pl.multiple_of(c * half + first + from_y * step, 128), step)
                view = finals[m].at[:, mine]
                state[u]["last"].append(remote(view, view, finals[m].at[:, theirs], device))
            elif n_y == 2:
                view, there = sums[m].at[a, b, :, piece(units[u], y)[0]], landing[3 * u + 2].at[0]
                state[u]["last"].append(remote(view, there, there, device))
            else:
                view = landing[3 * u + 2].at[y]
                state[u]["last"].append(remote(view, view, landing[3 * u + 2].at[from_y], device))

    def last_add(u):
        m, first, width, shared = units[u]
        half = shapes[m][1] // n_c
        for copy in state[u]["last"]:
            copy.wait_recv()
        at = pl.ds(pl.multiple_of(c * half + first, 128), width)
        if not shared:

            def body(outer, rows):
                value = landing[3 * u + 2][0, rows, :].astype(F32)
                if n_y == 2:
                    value += sums[m][a, b, rows, pl.ds(first, width)].astype(F32)
                for k in range(1, n_y if n_y > 2 else 0):
                    value += landing[3 * u + 2][k, rows, :].astype(F32)
                finals[m][rows, at] = value.astype(BF16)

            chunks(1, sums[m].shape[2], body)
        view = finals[m].at[:, at]
        theirs = pl.ds(pl.multiple_of((1 - c) * half + first, 128), width)
        state[u]["core"] = remote(view, view, finals[m].at[:, theirs], other_core)

    def xz(u):
        x_add(u)
        z_send(u)

    def yx(u):
        y_add(u)
        x_send(u)

    def zl(u):
        z_add(u)
        last_send(u)


    masks = [1 << i for i in range(n_y.bit_length() - 1)]
    dp_partners = [other_core] + [((y ^ mask) * n_c + c, fsdp) for mask in masks]
    gain_copies = {}

    def gain_step(step):
        if step > 0:
            gain_copies[step - 1].wait_recv()
            gain_buf[step] = gain_buf[step - 1] + gain_land[step - 1]
        if step < len(dp_partners):
            there = gain_land.at[step]
            gain_copies[step] = remote(gain_buf.at[step], there, there, dp_partners[step])

    def add_gain(row, value):
        for part in range(4):
            gain_buf[0, pl.ds(4 * row + part, 1), :] += value[:, part * 256 : part * 256 + 256]

    def give_credit(index):
        pl.semaphore_signal(credit.at[index], inc=1, device_id=other_core, device_id_type=MESH)


    own = D // n_fsdp

    def gain_row(row):
        return jnp.concatenate(
            [gains_all[f, pl.ds(row, 1), pl.ds(0, own)] for f in range(n_fsdp)], axis=1
        )

    def dot_right(left, right):
        return lax.dot_general(left, right, (((1,), (1,)), ((), ())), preferred_element_type=F32)

    def add_product(left, weight, first):
        for start in (0, 512):
            cols = pl.ds(start, 512)
            value = dot_right(left, weight[cols, :])
            acc[:, cols] = value if first else acc[:, cols] + value

    def feed_forward(block):
        down = (ring_next(), ring_next())
        for part in range(2):
            j = 2 * block + part
            slope_copies[j].wait()
            rows = pl.ds(part * 512, 512)
            d_act = dot_right(low[:, :512], down[0][rows, :])
            d_act += dot_right(low[:, 512:], down[1][rows, :])
            wide[:, pl.ds(j * 512, 512)] = (d_act * slope_buf[j % 2].astype(F32)).astype(BF16)
            if j + 2 < 8:
                slope_load(j + 2)
        ring_load()
        ring_load()
        for part in range(2):
            j = 2 * block + part
            add_product(wide[:, pl.ds(j * 512, 512)], ring_next(), j == 0)
            ring_load()

    for copy in low_copies + act_copies:
        copy.wait()
    for u in (0, 2):
        product(u, pool_tiles(near), pool_tiles(far), low, low_far, 2)
        x_send(u)
        x_send(u + 1)
    give_credit(0)
    left_here = [
        local(two, pool.at[0, near, pl.ds(0, D)]),
        local(one, pool.at[0, near, pl.ds(D, D)]),
    ]
    qkv_here = [
        local(qkv.at[:, pl.ds(0, D)], pool.at[1, near, pl.ds(0, D)]),
        local(qkv.at[:, pl.ds(D, D)], pool.at[1, near, pl.ds(D, D)]),
        local(qkv.at[:, pl.ds(2 * D, D)], pool.at[1, far, pl.ds(0, D)]),
        local(mixed, pool.at[1, far, pl.ds(D, D)]),
    ]
    for block in range(4):
        feed_forward(block)
        if block == 2:
            xz(0)
    pl.semaphore_wait(credit.at[0], 1)
    there = pool.at[0, far, pl.ds(0, D)]
    mixed_away = remote(mixed, there, there, other_core)
    wide_away = remote(wide.at[:, far_half(half_ff)], wide_far, wide_far, other_core)
    hat_copy.wait()
    cot_copy.wait()
    gain_buf[0] = jnp.zeros_like(gain_buf[0])
    gain_two = gain_row(1)

    def after_body(at):
        back, grad_gain = norm_back(
            hat[at, :].astype(F32), scales[at, pl.ds(64, 1)], gain_two, acc[at, :]
        )
        d_after = frame_weight[at, pl.ds(0, 1)] * cot[at, :].astype(F32) + back
        hidden[at, :] = d_after
        low[at, :] = d_after.astype(BF16)
        add_gain(1, grad_gain)

    row_loop(tokens, 64, after_body)
    after_away = remote(low.at[:, far_half(D // n_c)], low_far, low_far, other_core)
    hat_copy = local(hat_one, hat)
    pair = (ring_next(), ring_next())
    for start in (0, 512):
        cols = pl.ds(start, 512)
        value = dot_right(low[:, :512], pair[0][cols, :]) + dot_right(low[:, 512:], pair[1][cols, :])
        cot[:, cols] = value.astype(BF16)
    ring_load()
    ring_load()
    xz(1)
    zz(0)
    for copy in left_here + qkv_here:
        copy.wait()
    two_away.wait_recv()
    wide_away.wait_recv()
    for u in (4, 5):
        product(u, tiles(pool.at[0], near, 0), tiles(left_far, near, 0), wide, wide_far)
        y_send(u)
    mixed_away.wait_recv()
    after_away.wait_recv()
    product(6, tiles(pool.at[1], far, D), tiles(pool.at[0], far, 0), low, low_far)
    give_credit(1)
    x_send(6)
    wide_away.wait_send()
    pl.semaphore_wait(credit.at[1], 1)
    packed_away = remote(packed, pool.at[0, far], pool.at[0, far], other_core)
    one_away = remote(one, left_far, left_far, other_core)

    def attend_back(i, first_pair=0, last_pair=HEADS // 2):
        rows = pl.ds(i * per_pack, per_pack)
        rows_far = pl.ds(tokens + i * per_pack, per_pack)
        position = lax.broadcasted_iota(jnp.int32, (per_pack, per_pack), 0)
        distance = jnp.abs(
            position - lax.broadcasted_iota(jnp.int32, (per_pack, per_pack), 1)
        ).astype(F32)
        first_head = pair_mask(per_pack)
        same = same_item(*spots[i], per_pack)

        @pl.loop(first_pair, last_pair)
        def _(pair):
            def cols(first):
                return pl.ds(pl.multiple_of(first + pair * 2 * HD, 128), 2 * HD)

            queries, keys_all = pool[1, rows, cols(0)], pool[1, rows, cols(D)]
            values_all = pool[1, rows_far, cols(0)]
            d_mixed = cot[rows, cols(0)]
            zero = jnp.zeros_like(queries)
            total = [None, None, None]
            for head in range(2):
                mine = first_head if head == 0 else jnp.logical_not(first_head)
                query, key, d_head = (
                    jnp.where(mine, value, zero) for value in (queries, keys_all, d_mixed)
                )
                probs = head_probs(
                    query, keys_all, distance, same, head_slope(2 * pair + head, per_pack)
                )
                d_probs = dot_right(d_head, values_all)
                carried = jnp.sum(probs * d_probs, axis=-1, keepdims=True)
                d_scores = (probs * (d_probs - carried)).astype(BF16)
                contract = (((0,), (0,)), ((), ()))
                parts = (
                    jnp.dot(d_scores, key, preferred_element_type=F32),
                    lax.dot_general(d_scores, query, contract, preferred_element_type=F32),
                    lax.dot_general(
                        probs.astype(BF16), d_head, contract, preferred_element_type=F32
                    ),
                )
                total = [p if t is None else t + p for t, p in zip(total, parts)]
            wide[rows, cols(0)] = (total[0] * HD ** (-0.5)).astype(BF16)
            wide[rows, cols(D)] = (total[1] * HD ** (-0.5)).astype(BF16)
            wide[rows, cols(2 * D)] = total[2].astype(BF16)

    zl(0)
    zz(1)
    attend_back(0, 0, 4)
    xz(2)
    attend_back(0, 4, 8)
    zl(1)
    attend_back(1, 0, 4)
    yx(4)
    zz(2)
    attend_back(1, 4, 8)
    xz(3)
    qkv_half = 3 * D // n_c
    qkv_view = wide_far.at[:, pl.ds(0, qkv_half)]
    qkv_away = remote(wide.at[:, far_half(qkv_half)], qkv_view, qkv_view, other_core)
    for part in range(6):
        add_product(wide[:, pl.ds(part * 512, 512)], ring_next(), part == 0)
        ring_load()
    zl(2)
    one_away.wait_recv()
    qkv_away.wait_recv()
    for u in (7, 8):
        product(u, tiles(pool.at[0], near, D), tiles(left_far, near, 0), wide, wide_far)
        x_send(u)
    packed_here = local(packed, pool.at[0, near])
    hat_copy.wait()
    after_away.wait_send()
    gain_one = gain_row(0)

    def base_body(at):
        back, grad_gain = norm_back(
            hat[at, :].astype(F32), scales[at, pl.ds(0, 1)], gain_one, acc[at, :]
        )
        low[at, :] = (hidden[at, :] + back).astype(BF16)
        add_gain(0, grad_gain)

    row_loop(tokens, 64, base_body)
    zz(3)
    xz(6)
    base_away = remote(low.at[:, far_half(D // n_c)], low_far, low_far, other_core)
    gain_step(0)
    qkv_away.wait_send()
    for half in range(2):
        pair = (ring_next(), ring_next())
        for start in (0, 512):
            cols = pl.ds(start, 512)
            value = dot_right(low[:, :512], pair[0][cols, :])
            value += dot_right(low[:, 512:], pair[1][cols, :])
            wide[:, pl.ds(half * 1024 + start, 512)] = value.astype(BF16)
        ring_load()
        ring_load()
    xz(4)
    for i in range(micro):
        offset, length = spots[i]
        for source in range(n_dp):
            at = pl.ds(i * slab + source * slots, slots)
            block = hot_block((slots, per_pack), 0, offset[source], length[source])
            for half in range(2):
                cols = pl.ds(half * 1024, 1024)
                pool[1, at, cols] = jnp.dot(
                    block, wide[pl.ds(i * per_pack, per_pack), cols], preferred_element_type=F32
                ).astype(BF16)
    zl(3)
    gain_step(1)
    frames = []

    def slot(group, base=0):
        return pl.ds(pl.multiple_of(base + group * slots, 16), slots)

    for k in range(1, n_dp):
        to, back = turn(dp, k, n_dp), turn(dp, -k, n_dp)
        for i in range(micro):
            frames.append(
                remote(
                    pool.at[1, slot(to, i * slab)], returned.at[i, slot(dp)],
                    returned.at[i, slot(back)], (to, fsdp),
                )
            )
    own_frames = [local(pool.at[1, slot(dp, i * slab)], returned.at[i, slot(dp)]) for i in range(micro)]
    packed_here.wait()
    packed_away.wait_recv()
    base_away.wait_recv()
    for u in (9, 11):
        product(u, tiles(pool.at[0], near, 0), tiles(pool.at[0], far, 0), low, low_far, 2)
    zz(6)
    yx(5)
    for u in (9, 10, 11, 12):
        x_send(u)
    zz(4)
    zl(6)
    outgoing = []
    small[fsdp, :, pl.ds(256, 128)] = jnp.zeros((8, 128), F32)

    def add_squares(m):
        rows, columns = finals[m].shape
        chunk = min(32, rows)

        @pl.loop(0, rows // chunk)
        def _(i):
            at = pl.ds(pl.multiple_of(i * chunk, chunk), chunk)
            for first in range(0, columns, 1024):
                value = finals[m][at, pl.ds(first, 1024)].astype(F32)
                value = (value * value).reshape(chunk // 8, 8, 8, 128)
                small[fsdp, :, pl.ds(256, 128)] += jnp.sum(value, axis=(0, 2))

    def close(m):
        for u in range(len(units)):
            if units[u][0] == m:
                state[u]["core"].wait_recv()
        outgoing.append(local(finals[m], outs[m]))
        add_squares(m)

    steps = [
        (xz, 7), (zl, 4), (last_add, 0), (last_add, 1), (zz, 7), (last_add, 2), (last_add, 3), (xz, 8),
        (zl, 7), (close, 4), (zz, 8), (xz, 5), (zl, 8), (xz, 9), (zz, 5),
        (xz, 10), (zz, 9), (zl, 5), (xz, 11), (zz, 10), (zl, 9), (xz, 12), (zz, 11), (zl, 10), (last_add, 6),
        (zz, 12), (zl, 11), (last_add, 4), (last_add, 7), (close, 2), (zl, 12), (last_add, 8), (last_add, 5),
        (close, 1), (last_add, 9), (close, 3), (last_add, 10), (last_add, 11), (last_add, 12), (close, 0),
    ]
    for index, (do, u) in enumerate(steps):
        do(u)
        if index > 14 and index % 4 == 0 and index // 4 - 2 <= len(dp_partners):
            gain_step(index // 4 - 2)
    small[fsdp, :, pl.ds(0, 256)] = gain_buf[len(dp_partners)]
    view = small.at[fsdp]
    tail = []
    for k in range(1, n_fsdp):
        to, back = turn(fsdp, k, n_fsdp), turn(fsdp, -k, n_fsdp)
        tail.append(remote(view, view, small.at[back], (dp, to)))
    for copy in tail:
        copy.wait_recv()
    total = small[0]
    for f in range(1, n_fsdp):
        total = total + small[f]
    small_total[...] = total
    outgoing.append(local(small_total, small_out))
    for copy in frames:
        copy.wait_recv()
    for copy in own_frames + outgoing:
        copy.wait()
    for copy in copies.sent:
        copy.wait_send()


def backward_all(items, fulls, saved, cotangent, gains_all, micro, slab):
    dims = sizes()
    n_y, n_c, n_a, n_b = dims
    n_fsdp = n_a * n_b
    tokens = cotangent.shape[0]
    per_pack = tokens // micro
    shapes = [full.shape for full in fulls]
    shape = jax.ShapeDtypeStruct
    anywhere = pl.BlockSpec(memory_space=pl.ANY)
    inside = pl.BlockSpec(memory_space=pltpu.VMEM)
    scalars = pl.BlockSpec(memory_space=pltpu.SMEM)
    steps = (n_y * n_c).bit_length() - 1
    scratch = [pltpu.VMEM((n_a, n_b, r // n_fsdp, w // n_c), BF16) for r, w in shapes]
    scratch += [pltpu.VMEM((r // n_fsdp, w), BF16) for r, w in shapes]
    scratch += [
        pltpu.VMEM((2, 2 * tokens, FF // 2), BF16),
        pltpu.VMEM((tokens, D // n_c), BF16),
        pltpu.VMEM((tokens, FF), BF16),
        pltpu.VMEM((tokens, FF // n_c), BF16),
        pltpu.VMEM((tokens, D), BF16),
        pltpu.VMEM((RING, 1024, 512), BF16),
        pltpu.VMEM((2, tokens, 512), BF16),
        pltpu.VMEM((tokens, D), F32),
        pltpu.VMEM((tokens, D), F32),
        pltpu.VMEM((tokens, D), BF16),
        pltpu.VMEM((tokens, D), BF16),
        pltpu.VMEM((tokens, D), BF16),
        pltpu.VMEM((steps + 1, 8, 256), F32),
        pltpu.VMEM((steps, 8, 256), F32),
        pltpu.VMEM((n_fsdp, 8, 384), F32),
        pltpu.VMEM((8, 384), F32),
    ]
    for m, part, parts, shared in REDUCE_UNITS:
        rows, width = shapes[m][0] // n_fsdp, shapes[m][1] // n_c // parts
        if shared:
            step = width // n_y
            scratch += [
                pltpu.VMEM((n_y - 1, n_a, n_b, rows, step), BF16),
                pltpu.VMEM((n_b - 1, n_a, rows, step), BF16),
                pltpu.VMEM((3, rows, step), BF16),
            ]
        else:
            scratch += [
                pltpu.VMEM((n_b - 1, n_a, rows, width), BF16),
                pltpu.VMEM((3, rows, width), BF16),
                pltpu.VMEM((1 if n_y == 2 else n_y, rows, width), BF16),
            ]
    total = 10 + micro * (n_y * n_c - 1) + steps + n_fsdp - 1
    for _, _, _, shared in REDUCE_UNITS:
        total += (n_b - 1) + (n_a - 1) + (n_y - 1) + 1 + (n_y - 1 if shared else 0)
    scratch += [
        pltpu.SemaphoreType.DMA((total,)),
        pltpu.SemaphoreType.DMA((total,)),
        pltpu.SemaphoreType.DMA((72,)),
        pltpu.SemaphoreType.REGULAR((2,)),
    ]
    out_shape = [shape((r // n_fsdp, w), BF16) for r, w in shapes]
    out_shape += [
        shape((micro, slab, 2 * D), BF16), shape((8, 384), F32),
    ]
    results = pl.pallas_call(
        partial(backward_kernel, dims, shapes),
        out_shape=out_shape,
        in_specs=[anywhere] * 14 + [inside] + [anywhere] * 3 + [inside, anywhere, inside]
        + [scalars] * 3,
        out_specs=[anywhere] * len(out_shape),
        scratch_shapes=scratch,
        compiler_params=pltpu.CompilerParams(
            collective_id=1, has_side_effects=True, vmem_limit_bytes=VMEM_LIMIT
        ),
        name="backward_and_reduce",
    )(
        *fulls, *saved, cotangent, gains_all, *items[:3],
    )
    return results


def adam_update(master, first, second, gradient, rate, decay):
    first_new = BETA_FIRST * first + (1.0 - BETA_FIRST) * gradient
    second_new = BETA_SECOND * second + (1.0 - BETA_SECOND) * gradient * gradient
    first_hat = first_new / (1.0 - BETA_FIRST**STEP)
    second_hat = second_new / (1.0 - BETA_SECOND**STEP)
    master_new = master - rate * (
        first_hat / (jnp.sqrt(second_hat) + ADAM_EPSILON) + decay * master
    )
    return (master_new, first_new, second_new)


def item_at(items, i, source, slot, n_dp):
    return items[0, i, source, slot]


def plan_send(lengths, packs, i, dp, n_dp):
    starts, counts = [], []
    lows = [item_at(lengths, i, dp, j, n_dp) for j in range(n_dp)]
    targets = [item_at(packs, i, dp, j, n_dp) for j in range(n_dp)]
    for pack in range(n_dp):
        start, taken, before = jnp.int32(0), jnp.int32(0), jnp.int32(0)
        for low, target in zip(lows, targets):
            hit = target == pack
            start += jnp.where(hit, before, 0)
            taken += jnp.where(hit, low, 0)
            before += low
        starts.append(start)
        counts.append(taken)
    return starts, counts


def plan_pack(values, packs, i, dp, n_dp):
    result = []
    for source in range(n_dp):
        total = jnp.int32(0)
        for j in range(n_dp):
            hit = item_at(packs, i, source, j, n_dp) == dp
            total += jnp.where(hit, item_at(values, i, source, j, n_dp), 0)
        result.append(total)
    return result


def hot_block(shape, slot_dim, start, count):
    slot = lax.broadcasted_iota(jnp.int32, shape, slot_dim)
    row = lax.broadcasted_iota(jnp.int32, shape, 1 - slot_dim)
    return jnp.where((row == start + slot) & (slot < count), 1.0, 0.0).astype(BF16)


def spans(shape, dim, offsets, lengths, values):
    at = lax.broadcasted_iota(jnp.int32, shape, dim)
    total = jnp.zeros(shape, jnp.int32)
    for offset, length, value in zip(offsets, lengths, values):
        total += jnp.where((at >= offset) & (at < offset + length), value, 0)
    return total


def same_item(offsets, lengths, rows):
    ids = list(range(len(offsets)))
    return spans((rows, 1), 0, offsets, lengths, ids) == spans((1, rows), 1, offsets, lengths, ids)


DEPTH = 5


def update_kernel(dims, shapes, *refs):
    n_y, n_c, n_a, n_b = dims
    n_dp, n_fsdp = n_y * n_c, n_a * n_b
    lengths, packs, returned, small, gains, gains_first, gains_second, layer_out = refs[:8]
    refs = refs[8:]
    masters, firsts, seconds, gradients, refs = refs[:5], refs[5:10], refs[10:15], refs[15:20], refs[20:]
    layer_copy, input_out, skip_out, norm_out, gains_out, gains_first_out, gains_second_out = refs[:7]
    refs = refs[7:]
    outs, refs = [refs[4 * m : 4 * m + 4] for m in range(5)], refs[20:]
    came, back, hot, held, taken, taken_low, given, given_low, in_sem, out_sem, frame_sem = refs
    dp, fsdp = lax.axis_index("dp"), lax.axis_index("fsdp")
    micro, slab, _ = returned.shape
    slots = slab // n_dp
    source_rows = input_out.shape[1]

    pieces = []
    for m, (rows, columns) in enumerate(shapes):
        step = min(128, rows)
        for row in range(0, rows, step):
            for column in range(0, columns, 1024):
                pieces.append((m, pl.ds(row, step), pl.ds(column, 1024), step))

    def take(k):
        m, rows, columns, step = pieces[k]
        slot, at = k % DEPTH, pl.ds(0, step)
        result = [
            pltpu.make_async_copy(
                ref.at[rows, columns], taken.at[slot, index, at], in_sem.at[slot, index]
            )
            for index, ref in enumerate((masters[m], firsts[m], seconds[m]))
        ]
        result.append(
            pltpu.make_async_copy(
                gradients[m].at[rows, columns], taken_low.at[slot, at], in_sem.at[slot, 3]
            )
        )
        return result

    def give(k):
        m, rows, columns, step = pieces[k]
        slot, at = k % DEPTH, pl.ds(0, step)
        result = [
            pltpu.make_async_copy(
                given.at[slot, index, at], outs[m][index].at[rows, columns], out_sem.at[slot, index]
            )
            for index in range(3)
        ]
        result.append(
            pltpu.make_async_copy(
                given_low.at[slot, at], outs[m][3].at[rows, columns], out_sem.at[slot, 3]
            )
        )
        return result

    for k in range(DEPTH):
        for copy in take(k):
            copy.start()
    frame_copies = [
        pltpu.make_async_copy(returned.at[i], came.at[i], frame_sem.at[i]) for i in range(micro)
    ]
    for copy in frame_copies:
        copy.start()
    layer_in = pltpu.make_async_copy(layer_out, held, frame_sem.at[3 * micro])
    layer_in.start()

    values = small[:, pl.ds(0, 256)]
    squares = jnp.sum(small[:, pl.ds(256, 128)]) + jnp.sum(values * values)
    norm = jnp.sqrt(jnp.full((1, 128), squares, F32))
    norm_out[...] = norm
    param_count = 6 * D * D + 2 * D * FF + 2 * D
    clip = jnp.minimum(1.0, 0.02 * math.sqrt(param_count) / norm)[:, :1]

    own = D // n_fsdp
    own_gradient = jnp.zeros((2, own), F32)
    for f in range(n_fsdp):
        part, lane = f * own // 256, f * own % 256
        value = jnp.concatenate(
            [small[pl.ds(4 * row + part, 1), pl.ds(lane, own)] for row in range(2)], axis=0
        )
        own_gradient += jnp.where(fsdp == f, value, 0.0)
    new = adam_update(gains[...], gains_first[...], gains_second[...], clip * own_gradient, 0.3, 0.0)
    gains_out[...], gains_first_out[...], gains_second_out[...] = new

    out_frames = []

    def frames(i):
        starts, counts = plan_send(lengths, packs, i, dp, n_dp)
        for pack in range(n_dp):
            hot[:, pl.ds(pack * slots, slots)] = hot_block(
                (source_rows, slots), 1, starts[pack], counts[pack]
            )
        frame_copies[i].wait()
        for half, target in enumerate((input_out, skip_out)):
            columns = pl.ds(half * D, D)
            back[i, :, columns] = jnp.dot(
                hot[...], came[i, :, columns], preferred_element_type=F32
            ).astype(BF16)
            copy = pltpu.make_async_copy(
                back.at[i, :, columns], target.at[i], frame_sem.at[micro + 2 * i + half]
            )
            copy.start()
            out_frames.append(copy)

    rates = [0.5 / math.sqrt(fan_in) for fan_in in (2 * D, D, D // 16, D, FF)]
    for k, (m, _, _, step) in enumerate(pieces):
        slot = k % DEPTH
        for copy in take(k):
            copy.wait()
        if k >= DEPTH:
            for copy in give(k - DEPTH):
                copy.wait()

        def body(at, m=m, slot=slot):
            new = adam_update(
                taken[slot, 0, at, :], taken[slot, 1, at, :], taken[slot, 2, at, :],
                clip * taken_low[slot, at, :].astype(F32), rates[m], WEIGHT_DECAY,
            )
            for index in range(3):
                given[slot, index, at, :] = new[index]
            given_low[slot, at, :] = new[0].astype(BF16)

        row_loop(step, min(16, step), body)
        for copy in give(k):
            copy.start()
        if k + DEPTH < len(pieces):
            for copy in take(k + DEPTH):
                copy.start()
        if k in (1, 3):
            frames(k // 2)
        if k == 2:
            layer_in.wait()
            copy = pltpu.make_async_copy(held, layer_copy, frame_sem.at[3 * micro + 1])
            copy.start()
            out_frames.append(copy)
    for k in range(max(0, len(pieces) - DEPTH), len(pieces)):
        for copy in give(k):
            copy.wait()
    for copy in out_frames:
        copy.wait()


def update_all(lengths, packs, returned, small, gain_arrays, layer_out, masters, firsts, seconds, gradients, source_rows):
    dims = sizes()
    micro, slab, _ = returned.shape
    shape = jax.ShapeDtypeStruct
    shapes = [master.shape for master in masters]
    anywhere = pl.BlockSpec(memory_space=pl.ANY)
    inside = pl.BlockSpec(memory_space=pltpu.VMEM)
    scalars = pl.BlockSpec(memory_space=pltpu.SMEM)
    out_shape = [shape(layer_out.shape, BF16)] + [shape((micro, source_rows, D), BF16)] * 2
    out_shape.append(shape((1, 128), F32))
    out_shape += [shape(gain_arrays[0].shape, F32)] * 3
    for s in shapes:
        out_shape += [shape(s, F32)] * 3 + [shape(s, BF16)]
    return pl.pallas_call(
        partial(update_kernel, dims, shapes),
        out_shape=out_shape,
        in_specs=[scalars] * 2 + [anywhere] + [inside] * 4 + [anywhere] * 21,
        out_specs=[anywhere] * 3 + [inside] * 4 + [anywhere] * 20,
        scratch_shapes=[
            pltpu.VMEM((micro, slab, 2 * D), BF16),
            pltpu.VMEM((micro, source_rows, 2 * D), BF16),
            pltpu.VMEM((source_rows, slab), BF16),
            pltpu.VMEM(layer_out.shape, BF16),
            pltpu.VMEM((DEPTH, 3, 128, 1024), F32),
            pltpu.VMEM((DEPTH, 128, 1024), BF16),
            pltpu.VMEM((DEPTH, 3, 128, 1024), F32),
            pltpu.VMEM((DEPTH, 128, 1024), BF16),
            pltpu.SemaphoreType.DMA((DEPTH, 4)),
            pltpu.SemaphoreType.DMA((DEPTH, 4)),
            pltpu.SemaphoreType.DMA((3 * micro + 2,)),
        ],
        compiler_params=pltpu.CompilerParams(vmem_limit_bytes=VMEM_LIMIT),
        name="update",
    )(lengths, packs, returned, small, *gain_arrays, layer_out, *masters, *firsts, *seconds, *gradients)


def on_device(
    x_source, skip_source, out_cotangent, item_length, item_pack, item_offset, item_count,
    gains, w_skip, w_qkv, w_out, w_up, w_down,
    gains_first, first_skip, first_qkv, first_out, first_up, first_down,
    gains_second, second_skip, second_qkv, second_out, second_up, second_down,
):
    micro, source_rows, width = x_source.shape
    row_count = out_cotangent.shape[1]
    rows = micro * row_count
    items = (item_length, item_pack, item_offset, item_count)
    masters = (w_skip, w_qkv, w_out, w_up, w_down)
    cotangent = out_cotangent.reshape(rows, width)
    results = forward_all(items, masters, x_source, skip_source, gains, cotangent)
    fulls, saved, out_frames, gains_all = results[:5], results[5:19], results[19], results[20]
    fulls = [full.reshape(-1, full.shape[-1]) for full in fulls]
    results = backward_all(items, fulls, saved, cotangent, gains_all, micro, source_rows)
    gradients, returned, small = results[:5], results[5], results[6]
    results = update_all(
        items[0], items[1], returned, small, (gains, gains_first, gains_second),
        out_frames, masters,
        (first_skip, first_qkv, first_out, first_up, first_down),
        (second_skip, second_qkv, second_out, second_up, second_down), gradients, source_rows,
    )
    out_frames, input_gradient, skip_gradient, norm = results[:4]
    return (
        out_frames.reshape(micro, row_count, width), input_gradient, skip_gradient, norm[0, :1],
        *results[4:],
    )


def solution(mesh):
    frames = P(None, ("dp", "fsdp"), None)
    plan = P("fsdp", None, None, None)
    gain, weight = P(None, "fsdp"), P("fsdp", None)
    return jax.shard_map(
        on_device,
        mesh=mesh,
        in_specs=(frames,) * 3 + (plan,) * 4 + ((gain,) + (weight,) * 5) * 3,
        out_specs=(frames,) * 3 + (P(),) + (gain,) * 3 + (weight,) * 20,
        check_vma=False,
    )
```
